256 devices in a mesh: seq: 16 (over z_lo, x, core), head: 16 (over z_hi, y).
Axes of the slice: x: 4, y: 4, z: 8 (z_hi: 4, z_lo: 2; z = z_hi * 2 + z_lo), core: 2. Of those that a mesh axis runs over, the one named last changes fastest.
Arguments:
- queries: bfloat16 [32768, 4096], P(('seq', 'head')), may hold values from -6 to 6
- outputs: bfloat16 [32768, 4096], P(('seq', 'head')), may hold values from -6 to 6
- out_grads: bfloat16 [32768, 4096], P(('seq', 'head')), may hold values from -0.5 to 0.5
- log_norms: bfloat16 [32768, 32], P(('seq', 'head')), may hold values from 2 to 5
- keys: bfloat16 [32768, 512], P(('seq', 'head')), may hold values from -6 to 6
- values: bfloat16 [32768, 512], P(('seq', 'head')), may hold values from -6 to 6
- doc_start: int32 [256], P('seq'), may hold values from 0 to 255, as said below
Outputs:
- query_grads: bfloat16 [32768, 4096], P(('seq', 'head'))
- key_grads: bfloat16 [32768, 512], P(('seq', 'head'))
- value_grads: bfloat16 [32768, 512], P(('seq', 'head'))
The draws below stay inside these ranges and needn't reach their ends.
Inputs may be any that keep to these rules, and one draw needn't show every extreme that they name: doc_start never falls, doc_start[b] <= b, and equals b exactly where a document begins; every document covers 1 to 8 blocks, one document of exactly 8 blocks has 7 of its blocks before block 16 and one at it, and the last block begins a document.
All inputs are finite; a program needn't handle non-finite values.
Results may differ from the reference program's by a relative error of at most 0.0053.
Values may be sent and summed in bfloat16 or wider, within the bound.
No kernel may reach another device: no remote copies, remote signals or barrier semaphores. Data moves between devices by JAX's collectives and lax.ppermute only.
A program may use at most 128 MiB of HBM per device.

```python
import math
import jax
import jax.numpy as jnp
from jax import lax

H = 32
KVH = 4
DH = 128
BLOCK = 128
MAXB = 8
TOKENS = 32768
GROUP_BLOCKS = 16
BLOCKS = 256
GQ = 8
TAIL = 896


def draw_doc_start(key, part):
    lengths = jax.random.randint(key, (BLOCKS,), 1, MAXB + 1)
    starts = jnp.cumsum(lengths) - lengths
    marks = jnp.zeros((BLOCKS,), jnp.int32).at[starts].set(1, mode='drop')
    places = jnp.arange(BLOCKS, dtype=jnp.int32)
    first = GROUP_BLOCKS - MAXB + 1
    marks = jnp.where((places > first) & (places <= GROUP_BLOCKS), 0, marks)
    marks = jnp.where((places == first) | (places == GROUP_BLOCKS + 1) | (places == 0) | (places == BLOCKS - 1), 1, marks)
    return lax.cummax(jnp.where(marks == 1, places, 0), axis=0)


def level_of(rng, shape, cuts, smallest, high):
    loudness, own = 1.0, jax.random.fold_in(rng, 6)
    for position, parts in cuts:
        heights = jnp.exp(jax.random.uniform(jax.random.fold_in(own, position), (parts,), jnp.float32, smallest / len(cuts), high / len(cuts)))
        loudness = loudness * jnp.repeat(heights, shape[position] // parts).reshape([-1 if axis == position else 1 for axis in range(len(shape))])
    return loudness


def centred(key, dims, deviation, reach, cuts=(), held_as=jnp.bfloat16):
    result = jax.random.normal(key, dims, jnp.float32) * deviation
    if len(cuts) > 0:
        result = level_of(key, dims, cuts, -0.22, 0.18) * result
    return jnp.clip(result, min=-reach, max=reach).astype(held_as)


def setup_inputs(seed: int = 0) -> dict:
    key_of = jax.random.split(jax.random.key(seed), 8)
    return {
        "queries": centred(key_of[0], (TOKENS, H * DH), 1.0, 6.0, ((0, 256),)),
        "outputs": centred(key_of[1], (TOKENS, H * DH), 1.0, 6.0, ((0, 256),)),
        "out_grads": centred(key_of[2], (TOKENS, H * DH), 0.09, 0.5, ((0, 256),)),
        "log_norms": jnp.clip(2.0 + 3.0 * jax.random.uniform(key_of[3], (TOKENS, H), jnp.float32) ** level_of(key_of[3], (TOKENS, H), ((0, 256),), -0.2, 0.2), 2.0, 5.0).astype(jnp.bfloat16),
        "keys": centred(key_of[4], (TOKENS, KVH * DH), 1.0, 6.0, ((0, 256),)),
        "values": centred(key_of[5], (TOKENS, KVH * DH), 1.0, 6.0, ((0, 256),)),
        "doc_start": draw_doc_start(jax.random.fold_in(key_of[7], 71), 0),
    }


def core_grads(query_part, grad_part, dot_part, norm_part, key_part, value_part, visible):
    scale = DH ** -0.5
    query_full = query_part.astype(jnp.float32)
    grad_full = grad_part.astype(jnp.float32)
    key_full = key_part.astype(jnp.float32)
    value_full = value_part.astype(jnp.float32)
    scores = jnp.einsum("rhgd,khd->hgrk", query_full, key_full) * scale
    norm_moved = jnp.transpose(norm_part, (1, 2, 0))[..., None]
    weights = jnp.where(visible[None, None], jnp.exp(scores - norm_moved), 0.0)
    weight_bf = lax.optimization_barrier(weights.astype(jnp.bfloat16)).astype(jnp.float32)
    grad_weights = jnp.einsum("rhgd,khd->hgrk", grad_full, value_full)
    dot_moved = jnp.transpose(dot_part, (1, 2, 0))[..., None]
    grad_scores = lax.optimization_barrier((weights * (grad_weights - dot_moved)).astype(jnp.bfloat16)).astype(jnp.float32)
    value_grad = jnp.einsum("hgrk,rhgd->khd", weight_bf, grad_full)
    key_grad = jnp.einsum("hgrk,rhgd->khd", grad_scores, query_full) * scale
    query_grad = jnp.einsum("hgrk,khd->rhgd", grad_scores, key_full) * scale
    return query_grad, key_grad, value_grad


def sweep(query4, grad4, dot3, norm3, key_ext, value_ext, query_doc, first_pos, block_rows):
    row_count = query4.shape[0]
    tail_rows = key_ext.shape[0] - row_count
    span = block_rows + tail_rows
    zeros = jnp.zeros(key_ext.shape, jnp.float32)

    def turn(carry, number):
        key_acc, value_acc = carry
        start = number * block_rows

        def window(array, length):
            return lax.dynamic_slice_in_dim(array, start, length, 0)

        query_pos = first_pos + start + jnp.arange(block_rows, dtype=jnp.int32)
        key_pos = first_pos - tail_rows + start + jnp.arange(span, dtype=jnp.int32)
        visible = (key_pos[None, :] <= query_pos[:, None]) & ((key_pos // BLOCK)[None, :] >= window(query_doc, block_rows)[:, None])
        query_grad, key_grad, value_grad = core_grads(window(query4, block_rows), window(grad4, block_rows), window(dot3, block_rows), window(norm3, block_rows), window(key_ext, span), window(value_ext, span), visible)
        key_acc = lax.dynamic_update_slice_in_dim(key_acc, window(key_acc, span) + key_grad, start, 0)
        value_acc = lax.dynamic_update_slice_in_dim(value_acc, window(value_acc, span) + value_grad, start, 0)
        return (key_acc, value_acc), query_grad

    (key_acc, value_acc), query_grads = lax.scan(turn, (zeros, zeros), jnp.arange(row_count // block_rows, dtype=jnp.int32))
    return query_grads.reshape(query4.shape), key_acc, value_acc


def reference(queries, outputs, out_grads, log_norms, keys, values, doc_start):
    query4 = queries.reshape(TOKENS, KVH, GQ, DH)
    grad4 = out_grads.reshape(TOKENS, KVH, GQ, DH)
    output4 = outputs.reshape(TOKENS, KVH, GQ, DH)
    dot3 = jnp.sum(grad4.astype(jnp.float32) * output4.astype(jnp.float32), axis=-1)
    norm3 = log_norms.reshape(TOKENS, KVH, GQ).astype(jnp.float32)
    padding = jnp.zeros((TAIL, KVH, DH), keys.dtype)
    key_ext = jnp.concatenate([padding, keys.reshape(TOKENS, KVH, DH)], axis=0)
    value_ext = jnp.concatenate([padding, values.reshape(TOKENS, KVH, DH)], axis=0)
    query_doc = jnp.repeat(doc_start, BLOCK, total_repeat_length=TOKENS)
    query_grad, key_grad, value_grad = sweep(query4, grad4, dot3, norm3, key_ext, value_ext, query_doc, jnp.int32(0), math.gcd(TOKENS, 512))
    return (query_grad.astype(jnp.bfloat16).reshape(TOKENS, H * DH),
            key_grad[TAIL:].astype(jnp.bfloat16).reshape(TOKENS, KVH * DH),
            value_grad[TAIL:].astype(jnp.bfloat16).reshape(TOKENS, KVH * DH))
```

```python
import jax
import jax.numpy as jnp
from jax import lax
from jax.experimental import pallas as pl
from jax.experimental.pallas import tpu as pltpu
from jax.sharding import PartitionSpec as P

H = 32
KVH = 4
DH = 128
BLOCK = 128
GQ = 8
ROW = 4
WIDE = GQ * DH
SCALE = DH ** (-0.5)
AXES = ("seq", "head")
STAT = 2 * BLOCK
PIECE = STAT + 16
F32 = jnp.float32
BF16 = jnp.bfloat16

VMEM = pl.BlockSpec(memory_space=pltpu.VMEM)
SMEM = pl.BlockSpec(memory_space=pltpu.SMEM)
PARAMS = pltpu.CompilerParams(vmem_limit_bytes=48 << 20)


def nt(left, right):
    return lax.dot_general(left, right, (((1,), (1,)), ((), ())), preferred_element_type=F32)


def nn(left, right):
    return jnp.dot(left, right, preferred_element_type=F32)


def pack_kv(keys, values, *pieces):
    place = lax.rem(lax.axis_index("head"), ROW)
    for shift in range(ROW):
        head = lax.rem(place + shift, ROW)
        columns = pl.ds(pl.multiple_of(head * DH, DH), DH)
        pieces[shift][:, :DH] = keys[:, columns]
        pieces[shift][:, DH:] = values[:, columns]


def pack_queries(queries, outputs, grads, norms, *pieces):
    place = lax.rem(lax.axis_index("head"), ROW)
    rows = lax.broadcasted_iota(jnp.int32, (H, H), 0)
    columns = lax.broadcasted_iota(jnp.int32, (H, H), 1)
    unit = (rows == columns).astype(BF16)
    turned = nt(unit, norms[...])
    ones = jnp.ones((16, DH), BF16)
    row_id = lax.broadcasted_iota(jnp.int32, (16, BLOCK), 0)
    head_id = lax.broadcasted_iota(jnp.int32, (H, BLOCK), 0)
    for shift in range(ROW):
        group = lax.rem(place + shift, ROW)
        span = pl.ds(pl.multiple_of(group * WIDE, WIDE), WIDE)
        pieces[shift][:BLOCK, :] = queries[:, span]
        pieces[shift][BLOCK:STAT, :] = grads[:, span]
        for head in range(GQ):
            cut = pl.ds(pl.multiple_of(group * WIDE + head * DH, DH), DH)
            product = grads[:, cut].astype(F32) * outputs[:, cut].astype(F32)
            high = product.astype(BF16)
            low = (product - high.astype(F32)).astype(BF16)
            dots = nt(ones, high) + nt(ones, low)
            first = dots.astype(BF16).astype(F32)
            second = (dots - first).astype(BF16).astype(F32)
            third = dots - first - second
            norm = jnp.sum(
                jnp.where(head_id == group * GQ + head, turned, 0.0), axis=0, keepdims=True
            )
            stats = jnp.where(
                row_id == 0,
                norm,
                jnp.where(row_id == 1, first, jnp.where(row_id == 2, second, third)),
            )
            pieces[shift][STAT:, head * DH : (head + 1) * DH] = stats.astype(BF16)


def stacked(piece, start):
    return jnp.concatenate(
        [piece[start : start + BLOCK, head * DH : (head + 1) * DH] for head in range(GQ)], axis=0
    )


def sweep(back, doc_start, pieces, kv, dq, dkv):
    head = lax.axis_index("head")
    place = lax.rem(head, ROW)
    own_row = head // ROW
    first_key = lax.axis_index("seq") * (ROW * ROW) + (own_row - back) * ROW
    dkv[...] = jnp.zeros_like(dkv)
    for slot in range(ROW):
        query_place = lax.rem(place + ROW - slot, ROW)
        start = doc_start[own_row * ROW + query_place]

        def turn(key_slot, carry):
            key_place = lax.rem(place + ROW - key_slot, ROW)
            seen = first_key + key_place >= start
            if back == 0:
                seen = seen & (key_place <= query_place)

            @pl.when(seen)
            def _():
                piece = pieces[slot]
                key = kv[key_slot, :, :DH]
                value = kv[key_slot, :, DH:]
                query = stacked(piece, 0)
                grad = stacked(piece, BLOCK)
                stats = piece[STAT:, :].astype(F32)
                norm = stats[0:1]
                dots = stats[1:2] + stats[2:3] + stats[3:4]
                weights = jnp.exp(nt(key, query) * SCALE - norm)
                if back == 0:
                    key_pos = lax.broadcasted_iota(jnp.int32, (BLOCK, WIDE), 0)
                    query_pos = lax.broadcasted_iota(jnp.int32, (BLOCK, WIDE), 1) % BLOCK
                    ahead = (query_place - key_place) * BLOCK
                    weights = jnp.where(key_pos <= query_pos + ahead, weights, 0.0)
                grad_scores = (weights * (nt(value, grad) - dots)).astype(BF16)
                dkv[key_slot, :, DH:] += nn(weights.astype(BF16), grad)
                dkv[key_slot, :, :DH] += nn(grad_scores, query)
                dq[slot] += nn(key.T, grad_scores)

            return carry

        lax.fori_loop(0, ROW, turn, 0)


def row_two(doc_start, piece0, piece1, piece2, piece3, kv, dkv_out, dq, dkv):
    dq[...] = jnp.zeros_like(dq)
    sweep(2, doc_start, (piece0, piece1, piece2, piece3), kv, dq, dkv)
    dkv_out[:, :, :DH] = (dkv[:, :, :DH] * SCALE).astype(BF16)
    dkv_out[:, :, DH:] = dkv[:, :, DH:].astype(BF16)


def row_one(doc_start, piece0, piece1, piece2, piece3, kv, dq_in, dkv_out, dq, dkv):
    dq[...] = dq_in[...]
    sweep(1, doc_start, (piece0, piece1, piece2, piece3), kv, dq, dkv)
    dkv_out[:, :, :DH] = (dkv[:, :, :DH] * SCALE).astype(BF16)
    dkv_out[:, :, DH:] = dkv[:, :, DH:].astype(BF16)


def row_own(doc_start, piece0, piece1, piece2, piece3, kv, dq_in, dkv, *rest):
    outs, dq = rest[:ROW], rest[ROW]
    dq[...] = dq_in[...]
    sweep(0, doc_start, (piece0, piece1, piece2, piece3), kv, dq, dkv)
    dkv[:, :, :DH] = dkv[:, :, :DH] * SCALE
    for slot in range(ROW):
        for head in range(GQ):
            cut = slice(head * DH, (head + 1) * DH)
            outs[slot][:, cut] = (dq[slot, :, cut].T * SCALE).astype(BF16)


def add_up(own, one, two, *pieces):
    for slot in range(ROW):
        pieces[slot][...] = (
            own[slot] + one[slot].astype(F32) + two[slot].astype(F32)
        ).astype(BF16)


def join_queries(piece0, piece1, piece2, piece3, out):
    place = lax.rem(lax.axis_index("head"), ROW)
    for shift, piece in enumerate((piece0, piece1, piece2, piece3)):
        group = lax.rem(place + shift, ROW)
        out[:, pl.ds(pl.multiple_of(group * WIDE, WIDE), WIDE)] = piece[...]


def join_kv(piece0, piece1, piece2, piece3, key_out, value_out):
    place = lax.rem(lax.axis_index("head"), ROW)
    for shift, piece in enumerate((piece0, piece1, piece2, piece3)):
        columns = pl.ds(pl.multiple_of(lax.rem(place + shift, ROW) * DH, DH), DH)
        key_out[:, columns] = piece[:, :DH]
        value_out[:, columns] = piece[:, DH:]


def kernel(body, name, in_specs, shapes, scratch=(), flops=0, size=0):
    return pl.pallas_call(
        body,
        in_specs=in_specs,
        out_specs=[VMEM] * len(shapes),
        out_shape=[jax.ShapeDtypeStruct(*shape) for shape in shapes],
        scratch_shapes=scratch,
        compiler_params=PARAMS,
        cost_estimate=pl.CostEstimate(flops=flops, bytes_accessed=size, transcendentals=0),
        name=name,
    )


def per_device(queries, outputs, out_grads, log_norms, keys, values, doc_start):
    seqs = lax.axis_size("seq")
    heads = lax.axis_size("head")
    total = seqs * heads

    def along_row(value, shift):
        if shift % ROW == 0:
            return value
        pairs = [(b, b - b % ROW + (b + shift) % ROW) for b in range(total)]
        return lax.ppermute(value, AXES, pairs)

    def along_rows(value, rows):
        by = rows * ROW
        return lax.ppermute(
            value, AXES, [(b, b + by) for b in range(total) if 0 <= b + by < total]
        )

    kv_sent = kernel(
        pack_kv, "pack_kv", [VMEM] * 2, [((BLOCK, 2 * DH), BF16)] * ROW, size=1 << 19
    )(keys, values)
    kv_own = jnp.stack([along_row(kv_sent[shift], shift) for shift in range(ROW)])
    kv_two = along_rows(kv_own, 2)
    kv_one = along_rows(kv_own, 1)
    sent = kernel(
        pack_queries, "pack_queries", [VMEM] * 4, [((PIECE, WIDE), BF16)] * ROW, size=5 << 20
    )(queries, outputs, out_grads, log_norms)
    pieces = [along_row(sent[shift], shift) for shift in range(ROW)]

    dq_shape = ((ROW, DH, WIDE), F32)
    kv_shape = (ROW, BLOCK, 2 * DH)
    scratch = [pltpu.VMEM(kv_shape, F32)]
    dkv_two, dq = kernel(
        row_two,
        "row_two",
        [SMEM] + [VMEM] * 5,
        [(kv_shape, BF16), dq_shape],
        scratch,
        flops=6 * 1 << 30,
    )(doc_start, *pieces, kv_two)
    back_two = along_rows(dkv_two, -2)
    dkv_one, dq = kernel(
        row_one,
        "row_one",
        [SMEM] + [VMEM] * 6,
        [(kv_shape, BF16), dq_shape],
        scratch,
        flops=16 * 1 << 30,
    )(doc_start, *pieces, kv_one, dq)
    back_one = along_rows(dkv_one, -1)
    dkv_own, *dq_sent = kernel(
        row_own,
        "row_own",
        [SMEM] + [VMEM] * 6,
        [(kv_shape, F32)] + [((BLOCK, WIDE), BF16)] * ROW,
        [pltpu.VMEM(*dq_shape)],
        flops=10 * 1 << 30,
    )(doc_start, *pieces, kv_own, dq)
    dq_pieces = [along_row(dq_sent[slot], -slot) for slot in range(ROW)]
    dkv_sent = kernel(
        add_up, "add_up", [VMEM] * 3, [((BLOCK, 2 * DH), BF16)] * ROW, size=1 << 20
    )(dkv_own, back_one, back_two)
    dkv_pieces = [along_row(dkv_sent[slot], -slot) for slot in range(ROW)]
    (query_out,) = kernel(
        join_queries, "join_queries", [VMEM] * ROW, [((BLOCK, H * DH), BF16)], size=2 << 20
    )(*dq_pieces)
    key_out, value_out = kernel(
        join_kv, "join_kv", [VMEM] * ROW, [((BLOCK, KVH * DH), BF16)] * 2, size=1 << 19
    )(*dkv_pieces)
    return (query_out, key_out, value_out)


def solution(mesh):
    placed = P(("seq", "head"), None)
    return jax.shard_map(
        per_device,
        mesh=mesh,
        in_specs=(placed,) * 6 + (P("seq"),),
        out_specs=(placed,) * 3,
        check_vma=False,
    )
```

```python
import jax
import jax.numpy as jnp
from jax import lax
from jax.experimental import pallas as pl
from jax.experimental.pallas import tpu as pltpu
from jax.sharding import PartitionSpec as P

H = 32
KVH = 4
DH = 128
BLOCK = 128
GQ = 8
ROW = 4
WIDE = GQ * DH
SCALE = DH ** (-0.5)
AXES = ("seq", "head")
STAT = 2 * BLOCK
PIECE = STAT + 16
F32 = jnp.float32
BF16 = jnp.bfloat16

VMEM = pl.BlockSpec(memory_space=pltpu.VMEM)
SMEM = pl.BlockSpec(memory_space=pltpu.SMEM)
PARAMS = pltpu.CompilerParams(vmem_limit_bytes=24 << 20)


def nt(left, right):
    return lax.dot_general(left, right, (((1,), (1,)), ((), ())), preferred_element_type=F32)


def nn(left, right):
    return jnp.dot(left, right, preferred_element_type=F32)


def pack_kv(keys, values, *pieces):
    place = lax.rem(lax.axis_index("head"), ROW)
    for shift in range(ROW):
        head = lax.rem(place + shift, ROW)
        columns = pl.ds(pl.multiple_of(head * DH, DH), DH)
        pieces[shift][:, :DH] = keys[:, columns]
        pieces[shift][:, DH:] = values[:, columns]


def pack_queries(queries, outputs, grads, norms, *pieces):
    place = lax.rem(lax.axis_index("head"), ROW)
    rows = lax.broadcasted_iota(jnp.int32, (H, H), 0)
    columns = lax.broadcasted_iota(jnp.int32, (H, H), 1)
    unit = (rows == columns).astype(BF16)
    turned = nt(unit, norms[...])
    ones = jnp.ones((16, DH), BF16)
    row_id = lax.broadcasted_iota(jnp.int32, (16, BLOCK), 0)
    head_id = lax.broadcasted_iota(jnp.int32, (H, BLOCK), 0)
    for shift in range(ROW):
        group = lax.rem(place + shift, ROW)
        span = pl.ds(pl.multiple_of(group * WIDE, WIDE), WIDE)
        pieces[shift][:BLOCK, :] = queries[:, span]
        pieces[shift][BLOCK:STAT, :] = grads[:, span]
        for head in range(GQ):
            cut = pl.ds(pl.multiple_of(group * WIDE + head * DH, DH), DH)
            product = grads[:, cut].astype(F32) * outputs[:, cut].astype(F32)
            high = product.astype(BF16)
            low = (product - high.astype(F32)).astype(BF16)
            dots = nt(ones, high) + nt(ones, low)
            first = dots.astype(BF16).astype(F32)
            second = (dots - first).astype(BF16).astype(F32)
            third = dots - first - second
            norm = jnp.sum(
                jnp.where(head_id == group * GQ + head, turned, 0.0), axis=0, keepdims=True
            )
            stats = jnp.where(
                row_id == 0,
                norm,
                jnp.where(row_id == 1, first, jnp.where(row_id == 2, second, third)),
            )
            pieces[shift][STAT:, head * DH : (head + 1) * DH] = stats.astype(BF16)


def stacked(piece, start):
    return jnp.concatenate(
        [piece[start : start + BLOCK, head * DH : (head + 1) * DH] for head in range(GQ)], axis=0
    )


def sweep(back, doc_start, pieces, kv, dq, dkv):
    head = lax.axis_index("head")
    place = lax.rem(head, ROW)
    own_row = head // ROW
    first_key = lax.axis_index("seq") * (ROW * ROW) + (own_row - back) * ROW
    for slot in range(ROW):
        query_place = lax.rem(place + ROW - slot, ROW)
        start = doc_start[own_row * ROW + query_place]

        def turn(key_slot, carry):
            key_place = lax.rem(place + ROW - key_slot, ROW)
            seen = first_key + key_place >= start
            if back == 0:
                seen = seen & (key_place <= query_place)

            @pl.when(seen)
            def _():
                piece = pieces[slot]
                key = kv[key_slot, :, :DH]
                value = kv[key_slot, :, DH:]
                query = stacked(piece, 0)
                grad = stacked(piece, BLOCK)
                stats = piece[STAT:, :].astype(F32)
                norm = stats[0:1]
                dots = stats[1:2] + stats[2:3] + stats[3:4]
                weights = jnp.exp(nt(key, query) * SCALE - norm)
                if back == 0:
                    key_pos = lax.broadcasted_iota(jnp.int32, (BLOCK, WIDE), 0)
                    query_pos = lax.broadcasted_iota(jnp.int32, (BLOCK, WIDE), 1) % BLOCK
                    ahead = (query_place - key_place) * BLOCK
                    weights = jnp.where(key_pos <= query_pos + ahead, weights, 0.0)
                grad_scores = (weights * (nt(value, grad) - dots)).astype(BF16)
                dkv[key_slot, :, DH:] += nn(weights.astype(BF16), grad)
                dkv[key_slot, :, :DH] += nn(grad_scores, query)
                dq[slot] += nn(key.T, grad_scores)

            return carry

        lax.fori_loop(0, ROW, turn, 0)


def row_two(doc_start, piece0, piece1, piece2, piece3, kv, dkv_out, dq, dkv):
    dq[...] = jnp.zeros_like(dq)
    dkv[...] = jnp.zeros_like(dkv)
    sweep(2, doc_start, (piece0, piece1, piece2, piece3), kv, dq, dkv)
    dkv_out[:, :, :DH] = (dkv[:, :, :DH] * SCALE).astype(BF16)
    dkv_out[:, :, DH:] = dkv[:, :, DH:].astype(BF16)


def row_one(doc_start, piece0, piece1, piece2, piece3, kv, dq_in, dkv_out, dq, dkv):
    dq[...] = dq_in[...]
    dkv[...] = jnp.zeros_like(dkv)
    sweep(1, doc_start, (piece0, piece1, piece2, piece3), kv, dq, dkv)
    dkv_out[:, :, :DH] = (dkv[:, :, :DH] * SCALE).astype(BF16)
    dkv_out[:, :, DH:] = dkv[:, :, DH:].astype(BF16)


def row_own(doc_start, piece0, piece1, piece2, piece3, kv, dq_in, back_two, dkv, *rest):
    outs, dq = rest[:ROW], rest[ROW]
    dq[...] = dq_in[...]
    dkv[...] = jnp.zeros_like(dkv)
    sweep(0, doc_start, (piece0, piece1, piece2, piece3), kv, dq, dkv)
    dkv[:, :, :DH] = dkv[:, :, :DH] * SCALE + back_two[:, :, :DH].astype(F32)
    dkv[:, :, DH:] = dkv[:, :, DH:] + back_two[:, :, DH:].astype(F32)
    for slot in range(ROW):
        for head in range(GQ):
            cut = slice(head * DH, (head + 1) * DH)
            outs[slot][:, cut] = (dq[slot, :, cut].T * SCALE).astype(BF16)


def add_up(own, one, *pieces):
    for slot in range(ROW):
        pieces[slot][...] = (own[slot] + one[slot].astype(F32)).astype(BF16)


def join_queries(piece0, piece1, piece2, piece3, out):
    place = lax.rem(lax.axis_index("head"), ROW)
    for shift, piece in enumerate((piece0, piece1, piece2, piece3)):
        group = lax.rem(place + shift, ROW)
        out[:, pl.ds(pl.multiple_of(group * WIDE, WIDE), WIDE)] = piece[...]


def join_kv(piece0, piece1, piece2, piece3, key_out, value_out):
    place = lax.rem(lax.axis_index("head"), ROW)
    for shift, piece in enumerate((piece0, piece1, piece2, piece3)):
        columns = pl.ds(pl.multiple_of(lax.rem(place + shift, ROW) * DH, DH), DH)
        key_out[:, columns] = piece[:, :DH]
        value_out[:, columns] = piece[:, DH:]


def kernel(body, name, in_specs, shapes, scratch=(), flops=0, size=0):
    return pl.pallas_call(
        body,
        in_specs=in_specs,
        out_specs=[VMEM] * len(shapes),
        out_shape=[jax.ShapeDtypeStruct(*shape) for shape in shapes],
        scratch_shapes=scratch,
        compiler_params=PARAMS,
        cost_estimate=pl.CostEstimate(flops=flops, bytes_accessed=size, transcendentals=0),
        name=name,
    )


def per_device(queries, outputs, out_grads, log_norms, keys, values, doc_start):
    seqs = lax.axis_size("seq")
    heads = lax.axis_size("head")
    total = seqs * heads

    def along_row(value, shift):
        if shift % ROW == 0:
            return value
        pairs = [(b, b - b % ROW + (b + shift) % ROW) for b in range(total)]
        return lax.ppermute(value, AXES, pairs)

    def along_rows(value, rows):
        by = rows * ROW
        return lax.ppermute(
            value, AXES, [(b, b + by) for b in range(total) if 0 <= b + by < total]
        )

    kv_sent = kernel(
        pack_kv, "pack_kv", [VMEM] * 2, [((BLOCK, 2 * DH), BF16)] * ROW
    )(keys, values)
    kv_own = jnp.stack([along_row(kv_sent[shift], shift) for shift in range(ROW)])
    sent = kernel(
        pack_queries, "pack_queries", [VMEM] * 4, [((PIECE, WIDE), BF16)] * ROW
    )(queries, outputs, out_grads, log_norms)
    kv_own, *sent = lax.optimization_barrier((kv_own, *sent))
    kv_two = along_rows(kv_own, 2)
    kv_one = along_rows(kv_own, 1)
    pieces = [along_row(sent[shift], shift) for shift in range(ROW)]

    dq_shape = ((ROW, DH, WIDE), F32)
    kv_shape = (ROW, BLOCK, 2 * DH)
    scratch = [pltpu.VMEM(kv_shape, F32)]
    dkv_two, dq = kernel(
        row_two,
        "row_two",
        [SMEM] + [VMEM] * 5,
        [(kv_shape, BF16), dq_shape],
        scratch,
    )(doc_start, *pieces, kv_two)
    back_two = along_rows(dkv_two, -2)
    dkv_one, dq = kernel(
        row_one,
        "row_one",
        [SMEM] + [VMEM] * 6,
        [(kv_shape, BF16), dq_shape],
        scratch,
    )(doc_start, *pieces, kv_one, dq)
    back_one = along_rows(dkv_one, -1)
    dkv_own, *dq_sent = kernel(
        row_own,
        "row_own",
        [SMEM] + [VMEM] * 7,
        [(kv_shape, F32)] + [((BLOCK, WIDE), BF16)] * ROW,
        [pltpu.VMEM(*dq_shape)],
    )(doc_start, *pieces, kv_own, dq, back_two)
    dq_pieces = [along_row(dq_sent[slot], -slot) for slot in range(ROW)]
    dkv_sent = kernel(
        add_up, "add_up", [VMEM] * 2, [((BLOCK, 2 * DH), BF16)] * ROW
    )(dkv_own, back_one)
    dkv_pieces = [along_row(dkv_sent[slot], -slot) for slot in range(ROW)]
    (query_out,) = kernel(
        join_queries, "join_queries", [VMEM] * ROW, [((BLOCK, H * DH), BF16)]
    )(*dq_pieces)
    key_out, value_out = kernel(
        join_kv, "join_kv", [VMEM] * ROW, [((BLOCK, KVH * DH), BF16)] * 2
    )(*dkv_pieces)
    return (query_out, key_out, value_out)


def solution(mesh):
    placed = P(("seq", "head"), None)
    return jax.shard_map(
        per_device,
        mesh=mesh,
        in_specs=(placed,) * 6 + (P("seq"),),
        out_specs=(placed,) * 3,
        check_vma=False,
    )
```

```python
import jax
import jax.numpy as jnp
from jax import lax
from jax.experimental import pallas as pl
from jax.experimental.pallas import tpu as pltpu
from jax.sharding import PartitionSpec as P

H = 32
KVH = 4
DH = 128
BLOCK = 128
GQ = 8
ROW = 4
WIDE = GQ * DH
SCALE = DH ** (-0.5)
AXES = ("seq", "head")
STAT = 2 * BLOCK
PIECE = STAT + 16
F32 = jnp.float32
BF16 = jnp.bfloat16

VMEM = pl.BlockSpec(memory_space=pltpu.VMEM)
HBM = pl.BlockSpec(memory_space=pltpu.HBM)
SMEM = pl.BlockSpec(memory_space=pltpu.SMEM)


def nt(left, right):
    return lax.dot_general(left, right, (((1,), (1,)), ((), ())), preferred_element_type=F32)


def nn(left, right):
    return jnp.dot(left, right, preferred_element_type=F32)


def pack_kv(keys, values, piece0, piece1, piece2, piece3, sems):
    place = lax.rem(lax.axis_index("head"), ROW)
    copies = []
    for shift, piece in enumerate((piece0, piece1, piece2, piece3)):
        columns = pl.ds(pl.multiple_of(lax.rem(place + shift, ROW) * DH, DH), DH)
        for part, source in enumerate((keys, values)):
            copies.append(
                pltpu.make_async_copy(
                    source.at[:, columns],
                    piece.at[:, pl.ds(part * DH, DH)],
                    sems.at[shift, part],
                )
            )
    for copy in copies:
        copy.start()
    for copy in copies:
        copy.wait()


def pack_queries(
    queries, outputs, grads, norms, piece0, piece1, piece2, piece3, held, sems
):
    place = lax.rem(lax.axis_index("head"), ROW)
    pieces = (piece0, piece1, piece2, piece3)
    copies = []
    for shift, piece in enumerate(pieces):
        group = lax.rem(place + shift, ROW)
        span = pl.ds(pl.multiple_of(group * WIDE, WIDE), WIDE)
        copies.append(
            [
                pltpu.make_async_copy(source.at[:, span], target, sems.at[shift, part])
                for part, (source, target) in enumerate(
                    (
                        (grads, piece.at[pl.ds(BLOCK, BLOCK), :]),
                        (outputs, held.at[shift]),
                        (queries, piece.at[pl.ds(0, BLOCK), :]),
                    )
                )
            ]
        )
    for copy in copies:
        for part in copy:
            part.start()
    turned = norms[...].astype(F32)
    ones = jnp.ones((16, DH), BF16)
    row_id = lax.broadcasted_iota(jnp.int32, (16, BLOCK), 0)
    head_id = lax.broadcasted_iota(jnp.int32, (H, BLOCK), 0)
    for shift, piece in enumerate(pieces):
        group = lax.rem(place + shift, ROW)
        copies[shift][0].wait()
        copies[shift][1].wait()
        for head in range(GQ):
            cut = slice(head * DH, (head + 1) * DH)
            product = piece[BLOCK:STAT, cut].astype(F32) * held[shift, :, cut].astype(F32)
            high = product.astype(BF16)
            low = (product - high.astype(F32)).astype(BF16)
            dots = nt(ones, high) + nt(ones, low)
            first = dots.astype(BF16).astype(F32)
            second = (dots - first).astype(BF16).astype(F32)
            third = dots - first - second
            norm = jnp.sum(
                jnp.where(head_id == group * GQ + head, turned, 0.0), axis=0, keepdims=True
            )
            stats = jnp.where(
                row_id == 0,
                norm,
                jnp.where(row_id == 1, first, jnp.where(row_id == 2, second, third)),
            )
            piece[STAT:, cut] = stats.astype(BF16)
    for copy in copies:
        copy[2].wait()


def stacked(piece, start):
    return jnp.concatenate(
        [piece[start : start + BLOCK, head * DH : (head + 1) * DH] for head in range(GQ)], axis=0
    )


def sweep(back, doc_start, pieces, kv, dq, dkv):
    head = lax.axis_index("head")
    place = lax.rem(head, ROW)
    own_row = head // ROW
    first_key = lax.axis_index("seq") * (ROW * ROW) + (own_row - back) * ROW
    for slot, piece in pieces.items():
        query_place = lax.rem(place + ROW - slot, ROW)
        start = doc_start[own_row * ROW + query_place]

        def turn(key_slot, carry, slot=slot, piece=piece, start=start, query_place=query_place):
            key_place = lax.rem(place + ROW - key_slot, ROW)
            seen = first_key + key_place >= start
            if back == 0:
                seen = seen & (key_place <= query_place)

            @pl.when(seen)
            def _():
                key = kv[key_slot, :, :DH]
                value = kv[key_slot, :, DH:]
                query = stacked(piece, 0)
                grad = stacked(piece, BLOCK)
                stats = piece[STAT:, :].astype(F32)
                norm = stats[0:1]
                dots = stats[1:2] + stats[2:3] + stats[3:4]
                weights = jnp.exp(nt(key, query) * SCALE - norm)
                if back == 0:
                    key_pos = lax.broadcasted_iota(jnp.int32, (BLOCK, WIDE), 0)
                    query_pos = lax.broadcasted_iota(jnp.int32, (BLOCK, WIDE), 1) % BLOCK
                    ahead = (query_place - key_place) * BLOCK
                    weights = jnp.where(key_pos <= query_pos + ahead, weights, 0.0)
                grad_scores = (weights * (nt(value, grad) - dots)).astype(BF16)
                dkv[key_slot, :, DH:] += nn(weights.astype(BF16), grad)
                dkv[key_slot, :, :DH] += nn(grad_scores, query)
                dq[slot] += nn(key.T, grad_scores)

            return carry

        lax.fori_loop(0, ROW, turn, 0)


def begin_own(doc_start, piece0, piece1, piece3, kv, dkv, dq):
    dkv[...] = jnp.zeros_like(dkv)
    for slot in (0, 1, 3):
        dq[slot] = jnp.zeros((DH, WIDE), F32)
    sweep(0, doc_start, {0: piece0, 1: piece1, 3: piece3}, kv, dq, dkv)


def begin_one(doc_start, piece0, piece1, piece3, kv, dq_in, dkv, dq):
    dkv[...] = jnp.zeros_like(dkv)
    for slot in (0, 1, 3):
        dq[slot] = dq_in[slot]
    sweep(1, doc_start, {0: piece0, 1: piece1, 3: piece3}, kv, dq, dkv)


def round_kv(dkv, out):
    out[:, :, :DH] = (dkv[:, :, :DH] * SCALE).astype(BF16)
    out[:, :, DH:] = dkv[:, :, DH:].astype(BF16)


def finish_earlier(
    doc_start, piece0, piece1, piece2, piece3, kv_two, kv_one, dkv_in, dq_in,
    two_out, one_out, dq, dkv,
):
    for slot in (0, 1, 3):
        dq[slot] = dq_in[slot]
    dq[2] = jnp.zeros((DH, WIDE), F32)
    dkv[...] = jnp.zeros_like(dkv)
    sweep(2, doc_start, {0: piece0, 1: piece1, 2: piece2, 3: piece3}, kv_two, dq, dkv)
    round_kv(dkv, two_out)
    dkv[...] = dkv_in[...]
    sweep(1, doc_start, {2: piece2}, kv_one, dq, dkv)
    round_kv(dkv, one_out)


def finish_own(doc_start, piece2, kv, dkv_in, dq_in, dkv, out0, out1, out2, out3, late):
    dkv[...] = dkv_in[...]
    late[0] = dq_in[2]
    sweep(0, doc_start, {2: piece2}, kv, Shifted(late), dkv)
    dkv[:, :, :DH] = dkv[:, :, :DH] * SCALE
    for slot, out in enumerate((out0, out1, out2, out3)):
        for head in range(GQ):
            cut = slice(head * DH, (head + 1) * DH)
            total = late[0, :, cut] if slot == 2 else dq_in[slot, :, cut]
            out[:, cut] = (total.T * SCALE).astype(BF16)


class Shifted:
    def __init__(self, ref):
        self.ref = ref

    def __getitem__(self, slot):
        return self.ref[slot - 2]

    def __setitem__(self, slot, value):
        self.ref[slot - 2] = value


def add_up(own, one, two, *pieces):
    for slot in range(ROW):
        pieces[slot][...] = (
            own[slot] + one[slot].astype(F32) + two[slot].astype(F32)
        ).astype(BF16)


def join_queries(piece0, piece1, piece2, piece3, out, sems):
    place = lax.rem(lax.axis_index("head"), ROW)
    copies = []
    for shift, piece in enumerate((piece0, piece1, piece2, piece3)):
        span = pl.ds(pl.multiple_of(lax.rem(place + shift, ROW) * WIDE, WIDE), WIDE)
        copies.append(pltpu.make_async_copy(piece, out.at[:, span], sems.at[shift]))
    for copy in copies:
        copy.start()
    for copy in copies:
        copy.wait()


def join_kv(piece0, piece1, piece2, piece3, key_out, value_out, sems):
    place = lax.rem(lax.axis_index("head"), ROW)
    copies = []
    for shift, piece in enumerate((piece0, piece1, piece2, piece3)):
        columns = pl.ds(pl.multiple_of(lax.rem(place + shift, ROW) * DH, DH), DH)
        for part, out in enumerate((key_out, value_out)):
            copies.append(
                pltpu.make_async_copy(
                    piece.at[:, pl.ds(part * DH, DH)], out.at[:, columns], sems.at[shift, part]
                )
            )
    for copy in copies:
        copy.start()
    for copy in copies:
        copy.wait()


def kernel(body, name, in_specs, shapes, scratch=(), out_spec=VMEM, grant=24):
    return pl.pallas_call(
        body,
        in_specs=in_specs,
        out_specs=[out_spec] * len(shapes),
        out_shape=[jax.ShapeDtypeStruct(*shape) for shape in shapes],
        scratch_shapes=scratch,
        compiler_params=pltpu.CompilerParams(vmem_limit_bytes=grant << 20),
        name=name,
    )


def per_device(queries, outputs, out_grads, log_norms, keys, values, doc_start):
    seqs = lax.axis_size("seq")
    heads = lax.axis_size("head")
    total = seqs * heads
    sems = pltpu.SemaphoreType.DMA

    def along_row(value, shift):
        if shift % ROW == 0:
            return value
        pairs = [(b, b - b % ROW + (b + shift) % ROW) for b in range(total)]
        return lax.ppermute(value, AXES, pairs)

    def along_rows(value, rows):
        by = rows * ROW
        return lax.ppermute(
            value, AXES, [(b, b + by) for b in range(total) if 0 <= b + by < total]
        )

    kv_sent = kernel(
        pack_kv,
        "pack_kv",
        [HBM] * 2,
        [((BLOCK, 2 * DH), BF16)] * ROW,
        [sems((ROW, 2))],
        grant=56,
    )(keys, values)
    kv_pieces = [along_row(kv_sent[shift], shift) for shift in range(ROW)]
    sent = kernel(
        pack_queries,
        "pack_queries",
        [HBM] * 3 + [VMEM],
        [((PIECE, WIDE), BF16)] * ROW,
        [pltpu.VMEM((ROW, BLOCK, WIDE), BF16), sems((ROW, 3))],
        grant=56,
    )(queries, outputs, out_grads, log_norms.T)
    kv_pieces, sent = lax.optimization_barrier((kv_pieces, sent))
    piece0 = sent[0]
    piece1 = along_row(sent[1], 1)
    piece3 = along_row(sent[3], 3)
    kv_own = jnp.stack(kv_pieces)
    kv_two = along_rows(kv_own, 2)
    kv_one = along_rows(kv_own, 1)
    piece2 = along_row(sent[2], 2)

    dq_shape = ((ROW, DH, WIDE), F32)
    kv_shape = (ROW, BLOCK, 2 * DH)
    dkv_own, dq = kernel(
        begin_own, "begin_own", [SMEM] + [VMEM] * 4, [(kv_shape, F32), dq_shape]
    )(doc_start, piece0, piece1, piece3, kv_own)
    dkv_one, dq = kernel(
        begin_one, "begin_one", [SMEM] + [VMEM] * 5, [(kv_shape, F32), dq_shape]
    )(doc_start, piece0, piece1, piece3, kv_one, dq)
    dkv_two, dkv_one, dq = kernel(
        finish_earlier,
        "finish_earlier",
        [SMEM] + [VMEM] * 8,
        [(kv_shape, BF16), (kv_shape, BF16), dq_shape],
        [pltpu.VMEM(kv_shape, F32)],
    )(doc_start, piece0, piece1, piece2, piece3, kv_two, kv_one, dkv_one, dq)
    back_two = along_rows(dkv_two, -2)
    back_one = along_rows(dkv_one, -1)
    dkv_own, *dq_sent = kernel(
        finish_own,
        "finish_own",
        [SMEM] + [VMEM] * 4,
        [(kv_shape, F32)] + [((BLOCK, WIDE), BF16)] * ROW,
        [pltpu.VMEM((1, DH, WIDE), F32)],
    )(doc_start, piece2, kv_own, dkv_own, dq)
    dq_pieces = [along_row(dq_sent[slot], -slot) for slot in range(ROW)]
    dkv_sent = kernel(add_up, "add_up", [VMEM] * 3, [((BLOCK, 2 * DH), BF16)] * ROW)(
        dkv_own, back_one, back_two
    )
    dkv_pieces = [along_row(dkv_sent[slot], -slot) for slot in range(ROW)]
    (query_out,) = kernel(
        join_queries,
        "join_queries",
        [VMEM] * ROW,
        [((BLOCK, H * DH), BF16)],
        [sems((ROW,))],
        HBM,
    )(*dq_pieces)
    key_out, value_out = kernel(
        join_kv,
        "join_kv",
        [VMEM] * ROW,
        [((BLOCK, KVH * DH), BF16)] * 2,
        [sems((ROW, 2))],
        HBM,
    )(*dkv_pieces)
    return (query_out, key_out, value_out)


def solution(mesh):
    placed = P(("seq", "head"), None)
    return jax.shard_map(
        per_device,
        mesh=mesh,
        in_specs=(placed,) * 6 + (P("seq"),),
        out_specs=(placed,) * 3,
        check_vma=False,
    )
```

```python
import jax
import jax.numpy as jnp
from jax import lax
from jax.experimental import pallas as pl
from jax.experimental.pallas import tpu as pltpu
from jax.sharding import PartitionSpec as P

H = 32
KVH = 4
DH = 128
BLOCK = 128
GQ = 8
ROW = 4
WIDE = GQ * DH
SCALE = DH ** (-0.5)
AXES = ("seq", "head")
STAT = 2 * BLOCK
PIECE = STAT + 16
F32 = jnp.float32
BF16 = jnp.bfloat16

VMEM = pl.BlockSpec(memory_space=pltpu.VMEM)
HBM = pl.BlockSpec(memory_space=pltpu.HBM)
SMEM = pl.BlockSpec(memory_space=pltpu.SMEM)


def nt(left, right):
    return lax.dot_general(left, right, (((1,), (1,)), ((), ())), preferred_element_type=F32)


def nn(left, right):
    return jnp.dot(left, right, preferred_element_type=F32)


def pack(
    queries, outputs, grads, norms, keys, values,
    kv0, kv1, kv2, kv3, piece0, piece1, piece2, piece3, held, sems,
):
    place = lax.rem(lax.axis_index("head"), ROW)
    pieces = (piece0, piece1, piece2, piece3)
    early = []
    copies = []
    for shift, (piece, kv) in enumerate(zip(pieces, (kv0, kv1, kv2, kv3))):
        group = lax.rem(place + shift, ROW)
        span = pl.ds(pl.multiple_of(group * WIDE, WIDE), WIDE)
        columns = pl.ds(pl.multiple_of(group * DH, DH), DH)
        for part, (source, target) in enumerate(
            ((keys, kv.at[:, pl.ds(0, DH)]), (values, kv.at[:, pl.ds(DH, DH)]))
        ):
            early.append(
                pltpu.make_async_copy(source.at[:, columns], target, sems.at[shift, 3 + part])
            )
        copies.append(
            [
                pltpu.make_async_copy(source.at[:, span], target, sems.at[shift, part])
                for part, (source, target) in enumerate(
                    (
                        (grads, piece.at[pl.ds(BLOCK, BLOCK), :]),
                        (outputs, held.at[shift]),
                        (queries, piece.at[pl.ds(0, BLOCK), :]),
                    )
                )
            ]
        )
    for part in range(3):
        for copy in copies:
            copy[part].start()
    for copy in early:
        copy.start()
    turned = norms[...].astype(F32)
    ones = jnp.ones((16, DH), BF16)
    row_id = lax.broadcasted_iota(jnp.int32, (16, BLOCK), 0)
    head_id = lax.broadcasted_iota(jnp.int32, (H, BLOCK), 0)
    for shift, piece in enumerate(pieces):
        group = lax.rem(place + shift, ROW)
        copies[shift][0].wait()
        copies[shift][1].wait()
        for head in range(GQ):
            cut = slice(head * DH, (head + 1) * DH)
            product = piece[BLOCK:STAT, cut].astype(F32) * held[shift, :, cut].astype(F32)
            high = product.astype(BF16)
            low = (product - high.astype(F32)).astype(BF16)
            dots = nt(ones, high) + nt(ones, low)
            first = dots.astype(BF16).astype(F32)
            second = (dots - first).astype(BF16).astype(F32)
            third = dots - first - second
            norm = jnp.sum(
                jnp.where(head_id == group * GQ + head, turned, 0.0), axis=0, keepdims=True
            )
            stats = jnp.where(
                row_id == 0,
                norm,
                jnp.where(row_id == 1, first, jnp.where(row_id == 2, second, third)),
            )
            piece[STAT:, cut] = stats.astype(BF16)
    for copy in copies:
        copy[2].wait()
    for copy in early:
        copy.wait()


def in_order(piece0, piece1, piece2, piece3, all_out, late_out):
    place = lax.rem(lax.axis_index("head"), ROW)
    for block in range(ROW):
        shift = lax.rem(place + ROW - block, ROW)
        value = piece0[...]
        for number, piece in enumerate((piece1, piece2, piece3)):
            value = jnp.where(shift == number + 1, piece[...], value)
        all_out[block] = value
        if block > 0:
            late_out[block - 1] = value


def stacked(piece, start):
    return jnp.concatenate(
        [piece[start : start + BLOCK, head * DH : (head + 1) * DH] for head in range(GQ)], axis=0
    )


def sweep(back, doc_start, pieces, kv, dq, dkv):
    head = lax.axis_index("head")
    place = lax.rem(head, ROW)
    own_row = head // ROW
    first_key = lax.axis_index("seq") * (ROW * ROW) + (own_row - back) * ROW
    for slot, piece in pieces.items():
        query_place = lax.rem(place + ROW - slot, ROW)
        start = doc_start[own_row * ROW + query_place]

        def turn(key_slot, carry, slot=slot, piece=piece, start=start, query_place=query_place):
            key_place = key_slot + (1 if back == 2 else 0)
            seen = first_key + key_place >= start
            if back == 0:
                seen = seen & (key_place <= query_place)

            @pl.when(seen)
            def _():
                key = kv[key_slot, :, :DH]
                value = kv[key_slot, :, DH:]
                query = stacked(piece, 0)
                grad = stacked(piece, BLOCK)
                stats = piece[STAT:, :].astype(F32)
                norm = stats[0:1]
                dots = stats[1:2] + stats[2:3] + stats[3:4]
                weights = jnp.exp(nt(key, query) * SCALE - norm)
                if back == 0:
                    key_pos = lax.broadcasted_iota(jnp.int32, (BLOCK, WIDE), 0)
                    query_pos = lax.broadcasted_iota(jnp.int32, (BLOCK, WIDE), 1) % BLOCK
                    ahead = (query_place - key_place) * BLOCK
                    weights = jnp.where(key_pos <= query_pos + ahead, weights, 0.0)
                grad_scores = (weights * (nt(value, grad) - dots)).astype(BF16)
                dkv[key_slot, :, DH:] += nn(weights.astype(BF16), grad)
                dkv[key_slot, :, :DH] += nn(grad_scores, query)
                dq[slot] += nn(key.T, grad_scores)

            return carry

        lax.fori_loop(0, ROW - 1 if back == 2 else ROW, turn, 0)


def begin_own(doc_start, piece0, piece1, piece3, kv, dkv, dq):
    dkv[...] = jnp.zeros_like(dkv)
    for slot in (0, 1, 3):
        dq[slot] = jnp.zeros((DH, WIDE), F32)
    sweep(0, doc_start, {0: piece0, 1: piece1, 3: piece3}, kv, dq, dkv)


def begin_one(doc_start, piece0, piece1, piece3, kv, dq_in, dkv, dq):
    dkv[...] = jnp.zeros_like(dkv)
    for slot in (0, 1, 3):
        dq[slot] = dq_in[slot]
    sweep(1, doc_start, {0: piece0, 1: piece1, 3: piece3}, kv, dq, dkv)


def round_kv(dkv, out):
    out[:, :, :DH] = (dkv[:, :, :DH] * SCALE).astype(BF16)
    out[:, :, DH:] = dkv[:, :, DH:].astype(BF16)


def finish_earlier(
    doc_start, piece0, piece1, piece2, piece3, kv_two, kv_one, dkv_in, dq_in,
    two_out, one_out, dq, dkv_two, dkv,
):
    for slot in (0, 1, 3):
        dq[slot] = dq_in[slot]
    dq[2] = jnp.zeros((DH, WIDE), F32)
    dkv_two[...] = jnp.zeros_like(dkv_two)
    sweep(2, doc_start, {0: piece0, 1: piece1, 2: piece2, 3: piece3}, kv_two, dq, dkv_two)
    round_kv(dkv_two, two_out)
    dkv[...] = dkv_in[...]
    sweep(1, doc_start, {2: piece2}, kv_one, dq, dkv)
    round_kv(dkv, one_out)


def finish_own(doc_start, piece2, kv, dkv_in, dq_in, dkv, out0, out1, out2, out3, late):
    dkv[...] = dkv_in[...]
    late[0] = dq_in[2]
    sweep(0, doc_start, {2: piece2}, kv, Shifted(late), dkv)
    dkv[:, :, :DH] = dkv[:, :, :DH] * SCALE
    for slot, out in enumerate((out0, out1, out2, out3)):
        for head in range(GQ):
            cut = slice(head * DH, (head + 1) * DH)
            total = late[0, :, cut] if slot == 2 else dq_in[slot, :, cut]
            out[:, cut] = (total.T * SCALE).astype(BF16)


class Shifted:
    def __init__(self, ref):
        self.ref = ref

    def __getitem__(self, slot):
        return self.ref[slot - 2]

    def __setitem__(self, slot, value):
        self.ref[slot - 2] = value


def add_up(own, one, two, *pieces):
    place = lax.rem(lax.axis_index("head"), ROW)
    for slot in range(ROW):
        block = lax.rem(place + ROW - slot, ROW)
        earlier = jnp.where(block > 0, two[jnp.maximum(block - 1, 0)].astype(F32), 0.0)
        pieces[slot][...] = (own[block] + one[block].astype(F32) + earlier).astype(BF16)


def join_queries(piece0, piece1, piece2, piece3, out, sems):
    place = lax.rem(lax.axis_index("head"), ROW)
    copies = []
    for shift, piece in enumerate((piece0, piece1, piece2, piece3)):
        span = pl.ds(pl.multiple_of(lax.rem(place + shift, ROW) * WIDE, WIDE), WIDE)
        copies.append(pltpu.make_async_copy(piece, out.at[:, span], sems.at[shift]))
    for copy in copies:
        copy.start()
    for copy in copies:
        copy.wait()


def join_kv(piece0, piece1, piece2, piece3, key_out, value_out, sems):
    place = lax.rem(lax.axis_index("head"), ROW)
    copies = []
    for shift, piece in enumerate((piece0, piece1, piece2, piece3)):
        columns = pl.ds(pl.multiple_of(lax.rem(place + shift, ROW) * DH, DH), DH)
        for part, out in enumerate((key_out, value_out)):
            copies.append(
                pltpu.make_async_copy(
                    piece.at[:, pl.ds(part * DH, DH)], out.at[:, columns], sems.at[shift, part]
                )
            )
    for copy in copies:
        copy.start()
    for copy in copies:
        copy.wait()


def kernel(body, name, in_specs, shapes, scratch=(), out_spec=VMEM, grant=24, cost=200_000_000_000):
    return pl.pallas_call(
        body,
        in_specs=in_specs,
        out_specs=[out_spec] * len(shapes),
        out_shape=[jax.ShapeDtypeStruct(*shape) for shape in shapes],
        scratch_shapes=scratch,
        compiler_params=pltpu.CompilerParams(vmem_limit_bytes=grant << 20),
        cost_estimate=pl.CostEstimate(flops=cost, bytes_accessed=cost, transcendentals=0),
        name=name,
    )


def per_device(queries, outputs, out_grads, log_norms, keys, values, doc_start):
    seqs = lax.axis_size("seq")
    heads = lax.axis_size("head")
    total = seqs * heads
    sems = pltpu.SemaphoreType.DMA

    def along_row(value, shift):
        if shift % ROW == 0:
            return value
        pairs = [(b, b - b % ROW + (b + shift) % ROW) for b in range(total)]
        return lax.ppermute(value, AXES, pairs)

    def along_rows(value, rows):
        by = rows * ROW
        return lax.ppermute(
            value, AXES, [(b, b + by) for b in range(total) if 0 <= b + by < total]
        )

    kv_shape = (ROW, BLOCK, 2 * DH)
    late_shape = (ROW - 1, BLOCK, 2 * DH)
    packed = kernel(
        pack,
        "pack",
        [HBM] * 3 + [VMEM] + [HBM] * 2,
        [((BLOCK, 2 * DH), BF16)] * ROW + [((PIECE, WIDE), BF16)] * ROW,
        [pltpu.VMEM((ROW, BLOCK, WIDE), BF16), sems((ROW, 5))],
        grant=52,
    )(queries, outputs, out_grads, log_norms.T, keys, values)
    kv_pieces = [along_row(packed[shift], shift) for shift in range(ROW)]
    kv_pieces, sent = lax.optimization_barrier((kv_pieces, packed[ROW:]))
    piece0 = sent[0]
    piece1 = along_row(sent[1], 1)
    piece3 = along_row(sent[3], 3)
    kv_own, kv_late = kernel(
        in_order, "in_order", [VMEM] * ROW, [(kv_shape, BF16), (late_shape, BF16)]
    )(*kv_pieces)
    kv_one = along_rows(kv_own, 1)
    kv_two = along_rows(kv_late, 2)
    piece1, piece3, far = lax.optimization_barrier((piece1, piece3, sent[2]))
    piece2 = along_row(far, 2)

    dq_shape = ((ROW, DH, WIDE), F32)
    dkv_own, dq = kernel(
        begin_own, "begin_own", [SMEM] + [VMEM] * 4, [(kv_shape, F32), dq_shape]
    )(doc_start, piece0, piece1, piece3, kv_own)
    dkv_one, dq = kernel(
        begin_one, "begin_one", [SMEM] + [VMEM] * 5, [(kv_shape, F32), dq_shape]
    )(doc_start, piece0, piece1, piece3, kv_one, dq)
    dkv_two, dkv_one, dq = kernel(
        finish_earlier,
        "finish_earlier",
        [SMEM] + [VMEM] * 8,
        [(late_shape, BF16), (kv_shape, BF16), dq_shape],
        [pltpu.VMEM(late_shape, F32), pltpu.VMEM(kv_shape, F32)],
    )(doc_start, piece0, piece1, piece2, piece3, kv_two, kv_one, dkv_one, dq)
    back_two = along_rows(dkv_two, -2)
    back_one = along_rows(dkv_one, -1)
    dkv_own, *dq_sent = kernel(
        finish_own,
        "finish_own",
        [SMEM] + [VMEM] * 4,
        [(kv_shape, F32)] + [((BLOCK, WIDE), BF16)] * ROW,
        [pltpu.VMEM((1, DH, WIDE), F32)],
    )(doc_start, piece2, kv_own, dkv_own, dq)
    dq_pieces = [along_row(dq_sent[slot], -slot) for slot in range(ROW)]
    (query_out,) = kernel(
        join_queries,
        "join_queries",
        [VMEM] * ROW,
        [((BLOCK, H * DH), BF16)],
        [sems((ROW,))],
        HBM,
    )(*dq_pieces)
    dkv_sent = kernel(add_up, "add_up", [VMEM] * 3, [((BLOCK, 2 * DH), BF16)] * ROW)(
        dkv_own, back_one, back_two
    )
    dkv_pieces = [along_row(dkv_sent[slot], -slot) for slot in range(ROW)]
    key_out, value_out = kernel(
        join_kv,
        "join_kv",
        [VMEM] * ROW,
        [((BLOCK, KVH * DH), BF16)] * 2,
        [sems((ROW, 2))],
        HBM,
    )(*dkv_pieces)
    return (query_out, key_out, value_out)


def solution(mesh):
    placed = P(("seq", "head"), None)
    return jax.shard_map(
        per_device,
        mesh=mesh,
        in_specs=(placed,) * 6 + (P("seq"),),
        out_specs=(placed,) * 3,
        check_vma=False,
    )
```

```python
import functools

import jax
import jax.numpy as jnp
from jax import lax
from jax.experimental import pallas as pl
from jax.experimental.pallas import tpu as pltpu
from jax.sharding import PartitionSpec as P

H = 32
KVH = 4
DH = 128
BLOCK = 128
GQ = 8
ROW = 4
WIDE = GQ * DH
SCALE = DH ** (-0.5)
AXES = ("seq", "head")
STAT = 2 * BLOCK
PIECE = STAT + 16
HEAVY = 20_000_000_000
F32 = jnp.float32
BF16 = jnp.bfloat16

VMEM = pl.BlockSpec(memory_space=pltpu.VMEM)
HBM = pl.BlockSpec(memory_space=pltpu.HBM)
SMEM = pl.BlockSpec(memory_space=pltpu.SMEM)


def nt(left, right):
    return lax.dot_general(left, right, (((1,), (1,)), ((), ())), preferred_element_type=F32)


def nn(left, right):
    return jnp.dot(left, right, preferred_element_type=F32)


def pack(shifts, queries, outputs, grads, norms, *rest):
    place = lax.rem(lax.axis_index("head"), ROW)
    count = len(shifts)
    rest = list(rest)
    copies = []
    held_outputs, held_grads, stats, held_norms, sems = rest[-5:]
    if count < len(rest) - 5:
        keys, values = rest[:2]
        kv_pieces = rest[2 : 2 + ROW]
        pieces = rest[2 + ROW : 2 + ROW + count]
    else:
        kv_pieces = []
        pieces = rest[:count]
    norm_copy = pltpu.make_async_copy(norms, held_norms, sems.at[0, 5])
    norm_copy.start()
    loads = []
    for slot, shift in enumerate(shifts):
        group = lax.rem(place + shift, ROW)
        span = pl.ds(pl.multiple_of(group * WIDE, WIDE), WIDE)
        load = [
            pltpu.make_async_copy(source.at[:, span], target.at[slot], sems.at[slot, part])
            for part, (source, target) in enumerate(
                ((grads, held_grads), (outputs, held_outputs))
            )
        ]
        for copy in load:
            copy.start()
        loads.append(load)
    for shift, kv in enumerate(kv_pieces):
        columns = pl.ds(pl.multiple_of(lax.rem(place + shift, ROW) * DH, DH), DH)
        for part, source in enumerate((keys, values)):
            copy = pltpu.make_async_copy(
                source.at[:, columns], kv.at[:, pl.ds(part * DH, DH)], sems.at[shift, 6 + part]
            )
            copy.start()
            copies.append(copy)
    for slot, (shift, piece) in enumerate(zip(shifts, pieces)):
        group = lax.rem(place + shift, ROW)
        span = pl.ds(pl.multiple_of(group * WIDE, WIDE), WIDE)
        copy = pltpu.make_async_copy(
            queries.at[:, span], piece.at[pl.ds(0, BLOCK), :], sems.at[slot, 2]
        )
        copy.start()
        copies.append(copy)
    norm_copy.wait()
    turned = held_norms[...].astype(F32)
    ones = jnp.ones((16, DH), BF16)
    row_id = lax.broadcasted_iota(jnp.int32, (16, BLOCK), 0)
    head_id = lax.broadcasted_iota(jnp.int32, (H, BLOCK), 0)
    for slot, (shift, piece) in enumerate(zip(shifts, pieces)):
        group = lax.rem(place + shift, ROW)
        for copy in loads[slot]:
            copy.wait()
        copy = pltpu.make_async_copy(
            held_grads.at[slot], piece.at[pl.ds(BLOCK, BLOCK), :], sems.at[slot, 3]
        )
        copy.start()
        copies.append(copy)
        for head in range(GQ):
            cut = slice(head * DH, (head + 1) * DH)
            product = held_grads[slot, :, cut].astype(F32) * held_outputs[slot, :, cut].astype(F32)
            high = product.astype(BF16)
            low = (product - high.astype(F32)).astype(BF16)
            dots = nt(ones, high) + nt(ones, low)
            first = dots.astype(BF16).astype(F32)
            second = (dots - first).astype(BF16).astype(F32)
            third = dots - first - second
            norm = jnp.sum(
                jnp.where(head_id == group * GQ + head, turned, 0.0), axis=0, keepdims=True
            )
            both = jnp.where(
                row_id == 0,
                norm,
                jnp.where(row_id == 1, first, jnp.where(row_id == 2, second, third)),
            )
            stats[slot, :, cut] = both.astype(BF16)
        copy = pltpu.make_async_copy(
            stats.at[slot], piece.at[pl.ds(STAT, PIECE - STAT), :], sems.at[slot, 4]
        )
        copy.start()
        copies.append(copy)
    for copy in copies:
        copy.wait()


def in_order(piece0, piece1, piece2, piece3, all_out, late_out):
    place = lax.rem(lax.axis_index("head"), ROW)
    for block in range(ROW):
        shift = lax.rem(place + ROW - block, ROW)
        value = piece0[...]
        for number, piece in enumerate((piece1, piece2, piece3)):
            value = jnp.where(shift == number + 1, piece[...], value)
        all_out[block] = value
        if block > 0:
            late_out[block - 1] = value


def stacked(piece, start):
    return jnp.concatenate(
        [piece[start : start + BLOCK, head * DH : (head + 1) * DH] for head in range(GQ)], axis=0
    )


def sweep(back, doc_start, pieces, kv, dq, dkv):
    head = lax.axis_index("head")
    place = lax.rem(head, ROW)
    own_row = head // ROW
    first_key = lax.axis_index("seq") * (ROW * ROW) + (own_row - back) * ROW
    for slot, piece in pieces.items():
        query_place = lax.rem(place + ROW - slot, ROW)
        start = doc_start[own_row * ROW + query_place]

        def turn(key_slot, carry, slot=slot, piece=piece, start=start, query_place=query_place):
            key_place = key_slot + (1 if back == 2 else 0)
            seen = first_key + key_place >= start
            if back == 0:
                seen = seen & (key_place <= query_place)

            @pl.when(seen)
            def _():
                key = kv[key_slot, :, :DH]
                value = kv[key_slot, :, DH:]
                query = stacked(piece, 0)
                grad = stacked(piece, BLOCK)
                stats = piece[STAT:, :].astype(F32)
                norm = stats[0:1]
                dots = stats[1:2] + stats[2:3] + stats[3:4]
                weights = jnp.exp(nt(key, query) * SCALE - norm)
                if back == 0:
                    key_pos = lax.broadcasted_iota(jnp.int32, (BLOCK, WIDE), 0)
                    query_pos = lax.broadcasted_iota(jnp.int32, (BLOCK, WIDE), 1) % BLOCK
                    ahead = (query_place - key_place) * BLOCK
                    weights = jnp.where(key_pos <= query_pos + ahead, weights, 0.0)
                grad_scores = (weights * (nt(value, grad) - dots)).astype(BF16)
                dkv[key_slot, :, DH:] += nn(weights.astype(BF16), grad)
                dkv[key_slot, :, :DH] += nn(grad_scores, query)
                dq[slot] += nn(key.T, grad_scores)

            return carry

        lax.fori_loop(0, ROW - 1 if back == 2 else ROW, turn, 0)


def begin_own(doc_start, piece0, piece1, piece3, kv, dkv, dq):
    dkv[...] = jnp.zeros_like(dkv)
    for slot in (0, 1, 3):
        dq[slot] = jnp.zeros((DH, WIDE), F32)
    sweep(0, doc_start, {0: piece0, 1: piece1, 3: piece3}, kv, dq, dkv)


def begin_one(doc_start, piece0, piece1, piece3, kv, dq_in, dkv, dq):
    dkv[...] = jnp.zeros_like(dkv)
    for slot in (0, 1, 3):
        dq[slot] = dq_in[slot]
    sweep(1, doc_start, {0: piece0, 1: piece1, 3: piece3}, kv, dq, dkv)


def round_kv(dkv, out):
    out[:, :, :DH] = (dkv[:, :, :DH] * SCALE).astype(BF16)
    out[:, :, DH:] = dkv[:, :, DH:].astype(BF16)


def finish_earlier(
    doc_start, piece0, piece1, piece2, piece3, kv_two, kv_one, dkv_in, dq_in,
    two_out, one_out, dq, dkv_two, dkv,
):
    for slot in (0, 1, 3):
        dq[slot] = dq_in[slot]
    dq[2] = jnp.zeros((DH, WIDE), F32)
    dkv_two[...] = jnp.zeros_like(dkv_two)
    sweep(2, doc_start, {0: piece0, 1: piece1, 2: piece2, 3: piece3}, kv_two, dq, dkv_two)
    round_kv(dkv_two, two_out)
    dkv[...] = dkv_in[...]
    sweep(1, doc_start, {2: piece2}, kv_one, dq, dkv)
    round_kv(dkv, one_out)


def finish_own(doc_start, piece2, kv, dkv_in, dq_in, dkv, out0, out1, out2, out3, late):
    dkv[...] = dkv_in[...]
    late[0] = dq_in[2]
    sweep(0, doc_start, {2: piece2}, kv, Shifted(late), dkv)
    dkv[:, :, :DH] = dkv[:, :, :DH] * SCALE
    for slot, out in enumerate((out0, out1, out2, out3)):
        for head in range(GQ):
            cut = slice(head * DH, (head + 1) * DH)
            total = late[0, :, cut] if slot == 2 else dq_in[slot, :, cut]
            out[:, cut] = (total.T * SCALE).astype(BF16)


class Shifted:
    def __init__(self, ref):
        self.ref = ref

    def __getitem__(self, slot):
        return self.ref[slot - 2]

    def __setitem__(self, slot, value):
        self.ref[slot - 2] = value


def add_up(own, one, two, *pieces):
    place = lax.rem(lax.axis_index("head"), ROW)
    for slot in range(ROW):
        block = lax.rem(place + ROW - slot, ROW)
        earlier = jnp.where(block > 0, two[jnp.maximum(block - 1, 0)].astype(F32), 0.0)
        pieces[slot][...] = (own[block] + one[block].astype(F32) + earlier).astype(BF16)


def join_queries(piece0, piece1, piece2, piece3, out, sems):
    place = lax.rem(lax.axis_index("head"), ROW)
    copies = []
    for shift, piece in enumerate((piece0, piece1, piece2, piece3)):
        span = pl.ds(pl.multiple_of(lax.rem(place + shift, ROW) * WIDE, WIDE), WIDE)
        copies.append(pltpu.make_async_copy(piece, out.at[:, span], sems.at[shift]))
    for copy in copies:
        copy.start()
    for copy in copies:
        copy.wait()


def join_kv(piece0, piece1, piece2, piece3, key_out, value_out, sems):
    place = lax.rem(lax.axis_index("head"), ROW)
    copies = []
    for shift, piece in enumerate((piece0, piece1, piece2, piece3)):
        columns = pl.ds(pl.multiple_of(lax.rem(place + shift, ROW) * DH, DH), DH)
        for part, out in enumerate((key_out, value_out)):
            copies.append(
                pltpu.make_async_copy(
                    piece.at[:, pl.ds(part * DH, DH)], out.at[:, columns], sems.at[shift, part]
                )
            )
    for copy in copies:
        copy.start()
    for copy in copies:
        copy.wait()


def kernel(body, name, in_specs, shapes, scratch=(), out_spec=VMEM, grant=24, cost=0):
    return pl.pallas_call(
        body,
        in_specs=in_specs,
        out_specs=[out_spec] * len(shapes),
        out_shape=[jax.ShapeDtypeStruct(*shape) for shape in shapes],
        scratch_shapes=scratch,
        compiler_params=pltpu.CompilerParams(vmem_limit_bytes=grant << 20),
        cost_estimate=pl.CostEstimate(flops=cost, bytes_accessed=cost, transcendentals=0),
        name=name,
    )


def per_device(queries, outputs, out_grads, log_norms, keys, values, doc_start):
    seqs = lax.axis_size("seq")
    heads = lax.axis_size("head")
    total = seqs * heads
    sems = pltpu.SemaphoreType.DMA

    def along_row(value, shift):
        if shift % ROW == 0:
            return value
        pairs = [(b, b - b % ROW + (b + shift) % ROW) for b in range(total)]
        return lax.ppermute(value, AXES, pairs)

    def along_rows(value, rows):
        by = rows * ROW
        return lax.ppermute(value, AXES, [(b, (b + by) % total) for b in range(total)])

    kv_shape = (ROW, BLOCK, 2 * DH)
    late_shape = (ROW - 1, BLOCK, 2 * DH)
    dq_shape = ((ROW, DH, WIDE), F32)
    piece_shape = ((PIECE, WIDE), BF16)
    turned = log_norms.T

    def pack_scratch(count):
        return [
            pltpu.VMEM((count, BLOCK, WIDE), BF16),
            pltpu.VMEM((count, BLOCK, WIDE), BF16),
            pltpu.VMEM((count, PIECE - STAT, WIDE), BF16),
            pltpu.VMEM((H, BLOCK), BF16),
            sems((ROW, 8)),
        ]

    packed = kernel(
        functools.partial(pack, (1, 3)),
        "pack_near",
        [HBM] * 6,
        [((BLOCK, 2 * DH), BF16)] * ROW + [piece_shape] * 2,
        pack_scratch(2),
        HBM,
        grant=56,
    )(queries, outputs, out_grads, turned, keys, values)
    kv_pieces = [along_row(packed[shift], shift) for shift in range(ROW)]
    kv_pieces, near = lax.optimization_barrier((kv_pieces, packed[ROW:]))
    piece1 = along_row(near[0], 1)
    piece3 = along_row(near[1], 3)
    kv_own, kv_late = kernel(
        in_order, "in_order", [VMEM] * ROW, [(kv_shape, BF16), (late_shape, BF16)]
    )(*kv_pieces)
    kv_one = along_rows(kv_own, 1)
    kv_late, turned = lax.optimization_barrier((kv_late, turned))
    piece0, far = kernel(
        functools.partial(pack, (0, 2)),
        "pack_rest",
        [HBM] * 4,
        [piece_shape] * 2,
        pack_scratch(2),
        HBM,
        grant=56,
    )(queries, outputs, out_grads, turned)
    far, kv_late = lax.optimization_barrier((far, kv_late))
    piece2 = along_row(far, 2)
    kv_two = along_rows(kv_late, 2)

    dkv_own, dq = kernel(
        begin_own, "begin_own", [SMEM] + [VMEM] * 4, [(kv_shape, F32), dq_shape], cost=HEAVY
    )(doc_start, piece0, piece1, piece3, kv_own)
    dkv_one, dq = kernel(
        begin_one, "begin_one", [SMEM] + [VMEM] * 5, [(kv_shape, F32), dq_shape], cost=HEAVY
    )(doc_start, piece0, piece1, piece3, kv_one, dq)
    dkv_two, dkv_one, dq = kernel(
        finish_earlier,
        "finish_earlier",
        [SMEM] + [VMEM] * 8,
        [(late_shape, BF16), (kv_shape, BF16), dq_shape],
        [pltpu.VMEM(late_shape, F32), pltpu.VMEM(kv_shape, F32)],
        cost=HEAVY,
    )(doc_start, piece0, piece1, piece2, piece3, kv_two, kv_one, dkv_one, dq)
    back_two = along_rows(dkv_two, -2)
    back_one = along_rows(dkv_one, -1)
    dkv_own, *dq_sent = kernel(
        finish_own,
        "finish_own",
        [SMEM] + [VMEM] * 4,
        [(kv_shape, F32)] + [((BLOCK, WIDE), BF16)] * ROW,
        [pltpu.VMEM((1, DH, WIDE), F32)],
        cost=HEAVY,
    )(doc_start, piece2, kv_own, dkv_own, dq)
    dq_pieces = [along_row(dq_sent[slot], -slot) for slot in range(ROW)]
    (query_out,) = kernel(
        join_queries,
        "join_queries",
        [VMEM] * ROW,
        [((BLOCK, H * DH), BF16)],
        [sems((ROW,))],
        HBM,
    )(*dq_pieces)
    dkv_sent = kernel(
        add_up, "add_up", [VMEM] * 3, [((BLOCK, 2 * DH), BF16)] * ROW, cost=HEAVY
    )(
        dkv_own, back_one, back_two
    )
    dkv_pieces = [along_row(dkv_sent[slot], -slot) for slot in range(ROW)]
    key_out, value_out = kernel(
        join_kv,
        "join_kv",
        [VMEM] * ROW,
        [((BLOCK, KVH * DH), BF16)] * 2,
        [sems((ROW, 2))],
        HBM,
    )(*dkv_pieces)
    return (query_out, key_out, value_out)


def solution(mesh):
    placed = P(("seq", "head"), None)
    return jax.shard_map(
        per_device,
        mesh=mesh,
        in_specs=(placed,) * 6 + (P("seq"),),
        out_specs=(placed,) * 3,
        check_vma=False,
    )
```

```python
import functools

import jax
import jax.numpy as jnp
from jax import lax
from jax.experimental import pallas as pl
from jax.experimental.pallas import tpu as pltpu
from jax.sharding import PartitionSpec as P

H = 32
KVH = 4
DH = 128
BLOCK = 128
GQ = 8
ROW = 4
WIDE = GQ * DH
SCALE = DH ** (-0.5)
AXES = ("seq", "head")
STAT = 2 * BLOCK
PIECE = STAT + 16
HEAVY = 20_000_000_000
F32 = jnp.float32
BF16 = jnp.bfloat16

VMEM = pl.BlockSpec(memory_space=pltpu.VMEM)
HBM = pl.BlockSpec(memory_space=pltpu.HBM)
SMEM = pl.BlockSpec(memory_space=pltpu.SMEM)


def nt(left, right):
    return lax.dot_general(left, right, (((1,), (1,)), ((), ())), preferred_element_type=F32)


def nn(left, right):
    return jnp.dot(left, right, preferred_element_type=F32)


def pack(shifts, queries, outputs, grads, norms, *rest):
    place = lax.rem(lax.axis_index("head"), ROW)
    count = len(shifts)
    held_outputs, held_norms, sems = rest[-3:]
    pieces = rest[-3 - count : -3]
    loads = []
    for slot, (shift, piece) in enumerate(zip(shifts, pieces)):
        group = lax.rem(place + shift, ROW)
        span = pl.ds(pl.multiple_of(group * WIDE, WIDE), WIDE)
        loads.append(
            [
                pltpu.make_async_copy(source.at[:, span], target, sems.at[slot, part])
                for part, (source, target) in enumerate(
                    (
                        (grads, piece.at[pl.ds(BLOCK, BLOCK), :]),
                        (outputs, held_outputs.at[slot]),
                        (queries, piece.at[pl.ds(0, BLOCK), :]),
                    )
                )
            ]
        )
    late = [load[2] for load in loads]
    if len(rest) > 3 + count:
        keys, values = rest[:2]
        for shift, kv in enumerate(rest[2 : 2 + ROW]):
            columns = pl.ds(pl.multiple_of(lax.rem(place + shift, ROW) * DH, DH), DH)
            for part, source in enumerate((keys, values)):
                late.append(
                    pltpu.make_async_copy(
                        source.at[:, columns],
                        kv.at[:, pl.ds(part * DH, DH)],
                        sems.at[shift, 4 + part],
                    )
                )
    norm_copy = pltpu.make_async_copy(norms, held_norms, sems.at[0, 3])
    norm_copy.start()
    for load in loads:
        load[0].start()
        load[1].start()
    for copy in late:
        copy.start()
    norm_copy.wait()
    turned = held_norms[...].astype(F32)
    ones = jnp.ones((16, DH), BF16)
    row_id = lax.broadcasted_iota(jnp.int32, (16, BLOCK), 0)
    head_id = lax.broadcasted_iota(jnp.int32, (H, BLOCK), 0)
    for slot, (shift, piece) in enumerate(zip(shifts, pieces)):
        group = lax.rem(place + shift, ROW)
        loads[slot][0].wait()
        loads[slot][1].wait()
        for head in range(GQ):
            cut = slice(head * DH, (head + 1) * DH)
            product = piece[BLOCK:STAT, cut].astype(F32) * held_outputs[slot, :, cut].astype(F32)
            high = product.astype(BF16)
            low = (product - high.astype(F32)).astype(BF16)
            dots = nt(ones, high) + nt(ones, low)
            first = dots.astype(BF16).astype(F32)
            second = (dots - first).astype(BF16).astype(F32)
            third = dots - first - second
            norm = jnp.sum(
                jnp.where(head_id == group * GQ + head, turned, 0.0), axis=0, keepdims=True
            )
            stats = jnp.where(
                row_id == 0,
                norm,
                jnp.where(row_id == 1, first, jnp.where(row_id == 2, second, third)),
            )
            piece[STAT:, cut] = stats.astype(BF16)
    for copy in late:
        copy.wait()


def in_order(piece0, piece1, piece2, piece3, all_out, late_out):
    place = lax.rem(lax.axis_index("head"), ROW)
    for block in range(ROW):
        shift = lax.rem(place + ROW - block, ROW)
        value = piece0[...]
        for number, piece in enumerate((piece1, piece2, piece3)):
            value = jnp.where(shift == number + 1, piece[...], value)
        all_out[block] = value
        if block > 0:
            late_out[block - 1] = value


def stacked(piece, start):
    return jnp.concatenate(
        [piece[start : start + BLOCK, head * DH : (head + 1) * DH] for head in range(GQ)], axis=0
    )


def sweep(back, doc_start, pieces, kv, dq, dkv):
    head = lax.axis_index("head")
    place = lax.rem(head, ROW)
    own_row = head // ROW
    first_key = lax.axis_index("seq") * (ROW * ROW) + (own_row - back) * ROW
    for slot, piece in pieces.items():
        query_place = lax.rem(place + ROW - slot, ROW)
        start = doc_start[own_row * ROW + query_place]

        def turn(key_slot, carry, slot=slot, piece=piece, start=start, query_place=query_place):
            key_place = key_slot + (1 if back == 2 else 0)
            seen = first_key + key_place >= start
            if back == 0:
                seen = seen & (key_place <= query_place)

            @pl.when(seen)
            def _():
                key = kv[key_slot, :, :DH]
                value = kv[key_slot, :, DH:]
                query = stacked(piece, 0)
                grad = stacked(piece, BLOCK)
                stats = piece[STAT:, :].astype(F32)
                norm = stats[0:1]
                dots = stats[1:2] + stats[2:3] + stats[3:4]
                weights = jnp.exp(nt(key, query) * SCALE - norm)
                if back == 0:
                    key_pos = lax.broadcasted_iota(jnp.int32, (BLOCK, WIDE), 0)
                    query_pos = lax.broadcasted_iota(jnp.int32, (BLOCK, WIDE), 1) % BLOCK
                    ahead = (query_place - key_place) * BLOCK
                    weights = jnp.where(key_pos <= query_pos + ahead, weights, 0.0)
                grad_scores = (weights * (nt(value, grad) - dots)).astype(BF16)
                dkv[key_slot, :, DH:] += nn(weights.astype(BF16), grad)
                dkv[key_slot, :, :DH] += nn(grad_scores, query)
                dq[slot] += nn(key.T, grad_scores)

            return carry

        lax.fori_loop(0, ROW - 1 if back == 2 else ROW, turn, 0)


def begin_own(doc_start, piece0, piece1, piece3, kv, dkv, dq):
    dkv[...] = jnp.zeros_like(dkv)
    for slot in (0, 1, 3):
        dq[slot] = jnp.zeros((DH, WIDE), F32)
    sweep(0, doc_start, {0: piece0, 1: piece1, 3: piece3}, kv, dq, dkv)


def begin_one(doc_start, piece0, piece1, piece3, kv, dq_in, dkv, dq):
    dkv[...] = jnp.zeros_like(dkv)
    for slot in (0, 1, 3):
        dq[slot] = dq_in[slot]
    sweep(1, doc_start, {0: piece0, 1: piece1, 3: piece3}, kv, dq, dkv)


def round_kv(dkv, out):
    out[:, :, :DH] = (dkv[:, :, :DH] * SCALE).astype(BF16)
    out[:, :, DH:] = dkv[:, :, DH:].astype(BF16)


def finish_earlier(
    doc_start, piece0, piece1, piece2, piece3, kv_two, kv_one, dkv_in, dq_in,
    two_out, one_out, dq, dkv_two, dkv,
):
    for slot in (0, 1, 3):
        dq[slot] = dq_in[slot]
    dq[2] = jnp.zeros((DH, WIDE), F32)
    dkv_two[...] = jnp.zeros_like(dkv_two)
    sweep(2, doc_start, {0: piece0, 1: piece1, 2: piece2, 3: piece3}, kv_two, dq, dkv_two)
    round_kv(dkv_two, two_out)
    dkv[...] = dkv_in[...]
    sweep(1, doc_start, {2: piece2}, kv_one, dq, dkv)
    round_kv(dkv, one_out)


def finish_own(doc_start, piece2, kv, dkv_in, dq_in, dkv, out0, out1, out2, out3, late):
    dkv[...] = dkv_in[...]
    late[0] = dq_in[2]
    sweep(0, doc_start, {2: piece2}, kv, Shifted(late), dkv)
    dkv[:, :, :DH] = dkv[:, :, :DH] * SCALE
    for slot, out in enumerate((out0, out1, out2, out3)):
        for head in range(GQ):
            cut = slice(head * DH, (head + 1) * DH)
            total = late[0, :, cut] if slot == 2 else dq_in[slot, :, cut]
            out[:, cut] = (total.T * SCALE).astype(BF16)


class Shifted:
    def __init__(self, ref):
        self.ref = ref

    def __getitem__(self, slot):
        return self.ref[slot - 2]

    def __setitem__(self, slot, value):
        self.ref[slot - 2] = value


def add_up(own, one, two, *pieces):
    place = lax.rem(lax.axis_index("head"), ROW)
    for slot in range(ROW):
        block = lax.rem(place + ROW - slot, ROW)
        earlier = jnp.where(block > 0, two[jnp.maximum(block - 1, 0)].astype(F32), 0.0)
        pieces[slot][...] = (own[block] + one[block].astype(F32) + earlier).astype(BF16)


def join_queries(piece0, piece1, piece2, piece3, out, sems):
    place = lax.rem(lax.axis_index("head"), ROW)
    copies = []
    for shift, piece in enumerate((piece0, piece1, piece2, piece3)):
        span = pl.ds(pl.multiple_of(lax.rem(place + shift, ROW) * WIDE, WIDE), WIDE)
        copies.append(pltpu.make_async_copy(piece, out.at[:, span], sems.at[shift]))
    for copy in copies:
        copy.start()
    for copy in copies:
        copy.wait()


def join_kv(piece0, piece1, piece2, piece3, key_out, value_out, sems):
    place = lax.rem(lax.axis_index("head"), ROW)
    copies = []
    for shift, piece in enumerate((piece0, piece1, piece2, piece3)):
        columns = pl.ds(pl.multiple_of(lax.rem(place + shift, ROW) * DH, DH), DH)
        for part, out in enumerate((key_out, value_out)):
            copies.append(
                pltpu.make_async_copy(
                    piece.at[:, pl.ds(part * DH, DH)], out.at[:, columns], sems.at[shift, part]
                )
            )
    for copy in copies:
        copy.start()
    for copy in copies:
        copy.wait()


def kernel(body, name, in_specs, shapes, scratch=(), out_spec=VMEM, grant=24, cost=0):
    return pl.pallas_call(
        body,
        in_specs=in_specs,
        out_specs=[out_spec] * len(shapes),
        out_shape=[jax.ShapeDtypeStruct(*shape) for shape in shapes],
        scratch_shapes=scratch,
        compiler_params=pltpu.CompilerParams(vmem_limit_bytes=grant << 20),
        cost_estimate=pl.CostEstimate(flops=cost, bytes_accessed=cost, transcendentals=0),
        name=name,
    )


def per_device(queries, outputs, out_grads, log_norms, keys, values, doc_start):
    seqs = lax.axis_size("seq")
    heads = lax.axis_size("head")
    total = seqs * heads
    sems = pltpu.SemaphoreType.DMA

    def along_row(value, shift):
        if shift % ROW == 0:
            return value
        pairs = [(b, b - b % ROW + (b + shift) % ROW) for b in range(total)]
        return lax.ppermute(value, AXES, pairs)

    def along_rows(value, rows):
        by = rows * ROW
        return lax.ppermute(value, AXES, [(b, (b + by) % total) for b in range(total)])

    kv_shape = (ROW, BLOCK, 2 * DH)
    late_shape = (ROW - 1, BLOCK, 2 * DH)
    dq_shape = ((ROW, DH, WIDE), F32)
    piece_shape = ((PIECE, WIDE), BF16)
    turned = log_norms.T

    def pack_scratch(count):
        return [
            pltpu.VMEM((count, BLOCK, WIDE), BF16),
            pltpu.VMEM((H, BLOCK), BF16),
            sems((ROW, 6)),
        ]

    packed = kernel(
        functools.partial(pack, (1, 3)),
        "pack_near",
        [HBM] * 6,
        [((BLOCK, 2 * DH), BF16)] * ROW + [piece_shape] * 2,
        pack_scratch(2),
        grant=56,
    )(queries, outputs, out_grads, turned, keys, values)
    kv_pieces = [along_row(packed[shift], shift) for shift in range(ROW)]
    kv_pieces, near = lax.optimization_barrier((kv_pieces, packed[ROW:]))
    piece1 = along_row(near[0], 1)
    piece3 = along_row(near[1], 3)
    kv_own, kv_late = kernel(
        in_order, "in_order", [VMEM] * ROW, [(kv_shape, BF16), (late_shape, BF16)]
    )(*kv_pieces)
    kv_one = along_rows(kv_own, 1)
    kv_late, turned = lax.optimization_barrier((kv_late, turned))
    piece0, far = kernel(
        functools.partial(pack, (0, 2)),
        "pack_rest",
        [HBM] * 4,
        [piece_shape] * 2,
        pack_scratch(2),
        grant=52,
    )(queries, outputs, out_grads, turned)
    far, kv_late = lax.optimization_barrier((far, kv_late))
    piece2 = along_row(far, 2)
    kv_two = along_rows(kv_late, 2)

    dkv_own, dq = kernel(
        begin_own, "begin_own", [SMEM] + [VMEM] * 4, [(kv_shape, F32), dq_shape], cost=HEAVY
    )(doc_start, piece0, piece1, piece3, kv_own)
    dkv_one, dq = kernel(
        begin_one, "begin_one", [SMEM] + [VMEM] * 5, [(kv_shape, F32), dq_shape], cost=HEAVY
    )(doc_start, piece0, piece1, piece3, kv_one, dq)
    dkv_two, dkv_one, dq = kernel(
        finish_earlier,
        "finish_earlier",
        [SMEM] + [VMEM] * 8,
        [(late_shape, BF16), (kv_shape, BF16), dq_shape],
        [pltpu.VMEM(late_shape, F32), pltpu.VMEM(kv_shape, F32)],
        cost=HEAVY,
    )(doc_start, piece0, piece1, piece2, piece3, kv_two, kv_one, dkv_one, dq)
    back_two = along_rows(dkv_two, -2)
    back_one = along_rows(dkv_one, -1)
    dkv_own, *dq_sent = kernel(
        finish_own,
        "finish_own",
        [SMEM] + [VMEM] * 4,
        [(kv_shape, F32)] + [((BLOCK, WIDE), BF16)] * ROW,
        [pltpu.VMEM((1, DH, WIDE), F32)],
        cost=HEAVY,
    )(doc_start, piece2, kv_own, dkv_own, dq)
    dq_pieces = [along_row(dq_sent[slot], -slot) for slot in range(ROW)]
    (query_out,) = kernel(
        join_queries,
        "join_queries",
        [VMEM] * ROW,
        [((BLOCK, H * DH), BF16)],
        [sems((ROW,))],
        HBM,
    )(*dq_pieces)
    dkv_sent = kernel(
        add_up, "add_up", [VMEM] * 3, [((BLOCK, 2 * DH), BF16)] * ROW, cost=HEAVY
    )(
        dkv_own, back_one, back_two
    )
    dkv_pieces = [along_row(dkv_sent[slot], -slot) for slot in range(ROW)]
    key_out, value_out = kernel(
        join_kv,
        "join_kv",
        [VMEM] * ROW,
        [((BLOCK, KVH * DH), BF16)] * 2,
        [sems((ROW, 2))],
        HBM,
    )(*dkv_pieces)
    return (query_out, key_out, value_out)


def solution(mesh):
    placed = P(("seq", "head"), None)
    return jax.shard_map(
        per_device,
        mesh=mesh,
        in_specs=(placed,) * 6 + (P("seq"),),
        out_specs=(placed,) * 3,
        check_vma=False,
    )
```

```python
import functools

import jax
import jax.numpy as jnp
from jax import lax
from jax.experimental import pallas as pl
from jax.experimental.pallas import tpu as pltpu
from jax.sharding import PartitionSpec as P

H = 32
KVH = 4
DH = 128
BLOCK = 128
GQ = 8
ROW = 4
WIDE = GQ * DH
SCALE = DH ** (-0.5)
AXES = ("seq", "head")
STAT = 2 * BLOCK
PIECE = STAT + 16
HEAVY = 20_000_000_000
F32 = jnp.float32
BF16 = jnp.bfloat16

VMEM = pl.BlockSpec(memory_space=pltpu.VMEM)
HBM = pl.BlockSpec(memory_space=pltpu.HBM)
SMEM = pl.BlockSpec(memory_space=pltpu.SMEM)


def nt(left, right):
    return lax.dot_general(left, right, (((1,), (1,)), ((), ())), preferred_element_type=F32)


def nn(left, right):
    return jnp.dot(left, right, preferred_element_type=F32)


def pack(shifts, queries, outputs, grads, norms, *rest):
    place = lax.rem(lax.axis_index("head"), ROW)
    count = len(shifts)
    held_outputs, held_norms, sems = rest[-3:]
    pieces = rest[-3 - count : -3]
    loads = []
    for slot, (shift, piece) in enumerate(zip(shifts, pieces)):
        group = lax.rem(place + shift, ROW)
        span = pl.ds(pl.multiple_of(group * WIDE, WIDE), WIDE)
        loads.append(
            [
                pltpu.make_async_copy(source.at[:, span], target, sems.at[slot, part])
                for part, (source, target) in enumerate(
                    (
                        (grads, piece.at[pl.ds(BLOCK, BLOCK), :]),
                        (outputs, held_outputs.at[slot]),
                        (queries, piece.at[pl.ds(0, BLOCK), :]),
                    )
                )
            ]
        )
    late = [load[2] for load in loads]
    if len(rest) > 3 + count:
        keys, values = rest[:2]
        for shift, kv in enumerate(rest[2 : 2 + ROW]):
            columns = pl.ds(pl.multiple_of(lax.rem(place + shift, ROW) * DH, DH), DH)
            for part, source in enumerate((keys, values)):
                late.append(
                    pltpu.make_async_copy(
                        source.at[:, columns],
                        kv.at[:, pl.ds(part * DH, DH)],
                        sems.at[shift, 4 + part],
                    )
                )
    norm_copy = pltpu.make_async_copy(norms, held_norms, sems.at[0, 3])
    norm_copy.start()
    for load in loads:
        load[0].start()
        load[1].start()
    for copy in late:
        copy.start()
    norm_copy.wait()
    turned = held_norms[...].astype(F32)
    ones = jnp.ones((16, DH), BF16)
    row_id = lax.broadcasted_iota(jnp.int32, (16, BLOCK), 0)
    head_id = lax.broadcasted_iota(jnp.int32, (H, BLOCK), 0)
    for slot, (shift, piece) in enumerate(zip(shifts, pieces)):
        group = lax.rem(place + shift, ROW)
        loads[slot][0].wait()
        loads[slot][1].wait()
        for head in range(GQ):
            cut = slice(head * DH, (head + 1) * DH)
            product = piece[BLOCK:STAT, cut].astype(F32) * held_outputs[slot, :, cut].astype(F32)
            high = product.astype(BF16)
            low = (product - high.astype(F32)).astype(BF16)
            dots = nt(ones, high) + nt(ones, low)
            first = dots.astype(BF16).astype(F32)
            second = (dots - first).astype(BF16).astype(F32)
            third = dots - first - second
            norm = jnp.sum(
                jnp.where(head_id == group * GQ + head, turned, 0.0), axis=0, keepdims=True
            )
            stats = jnp.where(
                row_id == 0,
                norm,
                jnp.where(row_id == 1, first, jnp.where(row_id == 2, second, third)),
            )
            piece[STAT:, cut] = stats.astype(BF16)
    for copy in late:
        copy.wait()


def in_order(piece0, piece1, piece2, piece3, all_out, late_out):
    place = lax.rem(lax.axis_index("head"), ROW)
    for block in range(ROW):
        shift = lax.rem(place + ROW - block, ROW)
        value = piece0[...]
        for number, piece in enumerate((piece1, piece2, piece3)):
            value = jnp.where(shift == number + 1, piece[...], value)
        all_out[block] = value
        if block > 0:
            late_out[block - 1] = value


def stacked(piece, start):
    return jnp.concatenate(
        [piece[start : start + BLOCK, head * DH : (head + 1) * DH] for head in range(GQ)], axis=0
    )


def sweep(back, doc_start, pieces, kv, dq, dkv):
    head = lax.axis_index("head")
    place = lax.rem(head, ROW)
    own_row = head // ROW
    first_key = lax.axis_index("seq") * (ROW * ROW) + (own_row - back) * ROW
    for slot, piece in pieces.items():
        query_place = lax.rem(place + ROW - slot, ROW)
        start = doc_start[own_row * ROW + query_place]

        def turn(key_slot, carry, slot=slot, piece=piece, start=start, query_place=query_place):
            key_place = key_slot + (1 if back == 2 else 0)
            seen = first_key + key_place >= start
            if back == 0:
                seen = seen & (key_place <= query_place)

            @pl.when(seen)
            def _():
                key = kv[key_slot, :, :DH]
                value = kv[key_slot, :, DH:]
                query = stacked(piece, 0)
                grad = stacked(piece, BLOCK)
                stats = piece[STAT:, :].astype(F32)
                norm = stats[0:1]
                dots = stats[1:2] + stats[2:3] + stats[3:4]
                weights = jnp.exp(nt(key, query) * SCALE - norm)
                if back == 0:
                    key_pos = lax.broadcasted_iota(jnp.int32, (BLOCK, WIDE), 0)
                    query_pos = lax.broadcasted_iota(jnp.int32, (BLOCK, WIDE), 1) % BLOCK
                    ahead = (query_place - key_place) * BLOCK
                    weights = jnp.where(key_pos <= query_pos + ahead, weights, 0.0)
                grad_scores = (weights * (nt(value, grad) - dots)).astype(BF16)
                dkv[key_slot, :, DH:] += nn(weights.astype(BF16), grad)
                dkv[key_slot, :, :DH] += nn(grad_scores, query)
                dq[slot] += nn(key.T, grad_scores)

            return carry

        lax.fori_loop(0, ROW - 1 if back == 2 else ROW, turn, 0)


def begin_own(doc_start, piece0, piece1, piece3, kv, dkv, dq):
    dkv[...] = jnp.zeros_like(dkv)
    for slot in (0, 1, 3):
        dq[slot] = jnp.zeros((DH, WIDE), F32)
    sweep(0, doc_start, {0: piece0, 1: piece1, 3: piece3}, kv, dq, dkv)


def begin_one(doc_start, piece0, piece1, piece3, kv, dq_in, dkv, dq):
    dkv[...] = jnp.zeros_like(dkv)
    for slot in (0, 1, 3):
        dq[slot] = dq_in[slot]
    sweep(1, doc_start, {0: piece0, 1: piece1, 3: piece3}, kv, dq, dkv)


def begin_two(doc_start, piece0, piece1, piece3, kv, dq_in, dkv, dq):
    dkv[...] = jnp.zeros_like(dkv)
    for slot in (0, 1, 3):
        dq[slot] = dq_in[slot]
    sweep(2, doc_start, {0: piece0, 1: piece1, 3: piece3}, kv, dq, dkv)


def round_kv(dkv, out):
    out[:, :, :DH] = (dkv[:, :, :DH] * SCALE).astype(BF16)
    out[:, :, DH:] = dkv[:, :, DH:].astype(BF16)


def finish_earlier(
    doc_start, piece2, kv_two, kv_one, two_in, one_in, two_out, one_out, late, two, one
):
    late[...] = jnp.zeros_like(late)
    two[...] = two_in[...]
    one[...] = one_in[...]
    sweep(2, doc_start, {2: piece2}, kv_two, Shifted(late), two)
    round_kv(two, two_out)
    sweep(1, doc_start, {2: piece2}, kv_one, Shifted(late), one)
    round_kv(one, one_out)


def finish_own(
    doc_start, piece2, kv, dkv_in, dq_in, late_in, dkv, out0, out1, out2, out3, late
):
    dkv[...] = dkv_in[...]
    late[...] = late_in[...]
    sweep(0, doc_start, {2: piece2}, kv, Shifted(late), dkv)
    dkv[:, :, :DH] = dkv[:, :, :DH] * SCALE
    for slot, out in enumerate((out0, out1, out2, out3)):
        for head in range(GQ):
            cut = slice(head * DH, (head + 1) * DH)
            total = late[0, :, cut] if slot == 2 else dq_in[slot, :, cut]
            out[:, cut] = (total.T * SCALE).astype(BF16)


class Shifted:
    def __init__(self, ref):
        self.ref = ref

    def __getitem__(self, slot):
        return self.ref[slot - 2]

    def __setitem__(self, slot, value):
        self.ref[slot - 2] = value


def add_up(own, one, two, *pieces):
    place = lax.rem(lax.axis_index("head"), ROW)
    for slot in range(ROW):
        block = lax.rem(place + ROW - slot, ROW)
        earlier = jnp.where(block > 0, two[jnp.maximum(block - 1, 0)].astype(F32), 0.0)
        pieces[slot][...] = (own[block] + one[block].astype(F32) + earlier).astype(BF16)


def join_queries(piece0, piece1, piece2, piece3, out, sems):
    place = lax.rem(lax.axis_index("head"), ROW)
    copies = []
    for shift, piece in enumerate((piece0, piece1, piece2, piece3)):
        span = pl.ds(pl.multiple_of(lax.rem(place + shift, ROW) * WIDE, WIDE), WIDE)
        copies.append(pltpu.make_async_copy(piece, out.at[:, span], sems.at[shift]))
    for copy in copies:
        copy.start()
    for copy in copies:
        copy.wait()


def join_kv(piece0, piece1, piece2, piece3, key_out, value_out, sems):
    place = lax.rem(lax.axis_index("head"), ROW)
    copies = []
    for shift, piece in enumerate((piece0, piece1, piece2, piece3)):
        columns = pl.ds(pl.multiple_of(lax.rem(place + shift, ROW) * DH, DH), DH)
        for part, out in enumerate((key_out, value_out)):
            copies.append(
                pltpu.make_async_copy(
                    piece.at[:, pl.ds(part * DH, DH)], out.at[:, columns], sems.at[shift, part]
                )
            )
    for copy in copies:
        copy.start()
    for copy in copies:
        copy.wait()


def kernel(body, name, in_specs, shapes, scratch=(), out_spec=VMEM, grant=24, cost=0):
    return pl.pallas_call(
        body,
        in_specs=in_specs,
        out_specs=[out_spec] * len(shapes),
        out_shape=[jax.ShapeDtypeStruct(*shape) for shape in shapes],
        scratch_shapes=scratch,
        compiler_params=pltpu.CompilerParams(vmem_limit_bytes=grant << 20),
        cost_estimate=pl.CostEstimate(flops=cost, bytes_accessed=cost, transcendentals=0),
        name=name,
    )


def per_device(queries, outputs, out_grads, log_norms, keys, values, doc_start):
    seqs = lax.axis_size("seq")
    heads = lax.axis_size("head")
    total = seqs * heads
    sems = pltpu.SemaphoreType.DMA

    def along_row(value, shift):
        if shift % ROW == 0:
            return value
        pairs = [(b, b - b % ROW + (b + shift) % ROW) for b in range(total)]
        return lax.ppermute(value, AXES, pairs)

    def along_rows(value, rows):
        by = rows * ROW
        return lax.ppermute(value, AXES, [(b, (b + by) % total) for b in range(total)])

    kv_shape = (ROW, BLOCK, 2 * DH)
    late_shape = (ROW - 1, BLOCK, 2 * DH)
    dq_shape = ((ROW, DH, WIDE), F32)
    piece_shape = ((PIECE, WIDE), BF16)
    turned = log_norms.T

    def pack_scratch(count):
        return [
            pltpu.VMEM((count, BLOCK, WIDE), BF16),
            pltpu.VMEM((H, BLOCK), BF16),
            sems((ROW, 6)),
        ]

    packed = kernel(
        functools.partial(pack, (1, 3)),
        "pack_near",
        [HBM] * 6,
        [((BLOCK, 2 * DH), BF16)] * ROW + [piece_shape] * 2,
        pack_scratch(2),
        grant=56,
    )(queries, outputs, out_grads, turned, keys, values)
    kv_pieces = [along_row(packed[shift], shift) for shift in range(ROW)]
    kv_pieces, near = lax.optimization_barrier((kv_pieces, packed[ROW:]))
    piece1 = along_row(near[0], 1)
    piece3 = along_row(near[1], 3)
    kv_own, kv_late = kernel(
        in_order, "in_order", [VMEM] * ROW, [(kv_shape, BF16), (late_shape, BF16)]
    )(*kv_pieces)
    kv_one = along_rows(kv_own, 1)
    kv_late, turned = lax.optimization_barrier((kv_late, turned))
    piece0, far = kernel(
        functools.partial(pack, (0, 2)),
        "pack_rest",
        [HBM] * 4,
        [piece_shape] * 2,
        pack_scratch(2),
        grant=52,
    )(queries, outputs, out_grads, turned)
    far, kv_late = lax.optimization_barrier((far, kv_late))
    kv_two = along_rows(kv_late, 2)
    piece1, piece3, far = lax.optimization_barrier((piece1, piece3, far))
    piece2 = along_row(far, 2)

    dkv_own, dq = kernel(
        begin_own, "begin_own", [SMEM] + [VMEM] * 4, [(kv_shape, F32), dq_shape], cost=HEAVY
    )(doc_start, piece0, piece1, piece3, kv_own)
    dkv_one, dq = kernel(
        begin_one, "begin_one", [SMEM] + [VMEM] * 5, [(kv_shape, F32), dq_shape], cost=HEAVY
    )(doc_start, piece0, piece1, piece3, kv_one, dq)
    dkv_two, dq = kernel(
        begin_two,
        "begin_two",
        [SMEM] + [VMEM] * 5,
        [(late_shape, F32), dq_shape],
        cost=HEAVY,
    )(doc_start, piece0, piece1, piece3, kv_two, dq)
    far_shape = ((1, DH, WIDE), F32)
    dkv_two, dkv_one, dq_far = kernel(
        finish_earlier,
        "finish_earlier",
        [SMEM] + [VMEM] * 5,
        [(late_shape, BF16), (kv_shape, BF16), far_shape],
        [pltpu.VMEM(late_shape, F32), pltpu.VMEM(kv_shape, F32)],
        cost=HEAVY,
    )(doc_start, piece2, kv_two, kv_one, dkv_two, dkv_one)
    back_two = along_rows(dkv_two, -2)
    back_one = along_rows(dkv_one, -1)
    dkv_own, *dq_sent = kernel(
        finish_own,
        "finish_own",
        [SMEM] + [VMEM] * 5,
        [(kv_shape, F32)] + [((BLOCK, WIDE), BF16)] * ROW,
        [pltpu.VMEM(*far_shape)],
        cost=HEAVY,
    )(doc_start, piece2, kv_own, dkv_own, dq, dq_far)
    dq_pieces = [along_row(dq_sent[slot], -slot) for slot in range(ROW)]
    (query_out,) = kernel(
        join_queries,
        "join_queries",
        [VMEM] * ROW,
        [((BLOCK, H * DH), BF16)],
        [sems((ROW,))],
        HBM,
    )(*dq_pieces)
    dkv_sent = kernel(
        add_up, "add_up", [VMEM] * 3, [((BLOCK, 2 * DH), BF16)] * ROW, cost=HEAVY
    )(
        dkv_own, back_one, back_two
    )
    dkv_pieces = [along_row(dkv_sent[slot], -slot) for slot in range(ROW)]
    key_out, value_out = kernel(
        join_kv,
        "join_kv",
        [VMEM] * ROW,
        [((BLOCK, KVH * DH), BF16)] * 2,
        [sems((ROW, 2))],
        HBM,
    )(*dkv_pieces)
    return (query_out, key_out, value_out)


def solution(mesh):
    placed = P(("seq", "head"), None)
    return jax.shard_map(
        per_device,
        mesh=mesh,
        in_specs=(placed,) * 6 + (P("seq"),),
        out_specs=(placed,) * 3,
        check_vma=False,
    )
```

```python
import functools

import jax
import jax.numpy as jnp
from jax import lax
from jax.experimental import pallas as pl
from jax.experimental.pallas import tpu as pltpu
from jax.sharding import PartitionSpec as P

H = 32
KVH = 4
DH = 128
BLOCK = 128
GQ = 8
ROW = 4
WIDE = GQ * DH
SCALE = DH ** (-0.5)
AXES = ("seq", "head")
STAT = 2 * BLOCK
PIECE = STAT + 16
HEAVY = 20_000_000_000
F32 = jnp.float32
BF16 = jnp.bfloat16

VMEM = pl.BlockSpec(memory_space=pltpu.VMEM)
HBM = pl.BlockSpec(memory_space=pltpu.HBM)
SMEM = pl.BlockSpec(memory_space=pltpu.SMEM)


def nt(left, right):
    return lax.dot_general(left, right, (((1,), (1,)), ((), ())), preferred_element_type=F32)


def nn(left, right):
    return jnp.dot(left, right, preferred_element_type=F32)


def pack_kv(keys, values, piece0, piece1, piece2, piece3, sems):
    place = lax.rem(lax.axis_index("head"), ROW)
    copies = []
    for shift, piece in enumerate((piece0, piece1, piece2, piece3)):
        columns = pl.ds(pl.multiple_of(lax.rem(place + shift, ROW) * DH, DH), DH)
        for part, source in enumerate((keys, values)):
            copies.append(
                pltpu.make_async_copy(
                    source.at[:, columns],
                    piece.at[:, pl.ds(part * DH, DH)],
                    sems.at[shift, part],
                )
            )
    for copy in copies:
        copy.start()
    for copy in copies:
        copy.wait()


def pack(shifts, queries, outputs, grads, norms, *rest):
    place = lax.rem(lax.axis_index("head"), ROW)
    count = len(shifts)
    held_outputs, held_norms, sems = rest[-3:]
    pieces = rest[-3 - count : -3]
    loads = []
    for slot, (shift, piece) in enumerate(zip(shifts, pieces)):
        group = lax.rem(place + shift, ROW)
        span = pl.ds(pl.multiple_of(group * WIDE, WIDE), WIDE)
        loads.append(
            [
                pltpu.make_async_copy(source.at[:, span], target, sems.at[slot, part])
                for part, (source, target) in enumerate(
                    (
                        (grads, piece.at[pl.ds(BLOCK, BLOCK), :]),
                        (outputs, held_outputs.at[slot]),
                        (queries, piece.at[pl.ds(0, BLOCK), :]),
                    )
                )
            ]
        )
    late = [load[2] for load in loads]
    norm_copy = pltpu.make_async_copy(norms, held_norms, sems.at[0, 3])
    norm_copy.start()
    for load in loads:
        load[0].start()
        load[1].start()
    for copy in late:
        copy.start()
    norm_copy.wait()
    turned = held_norms[...].astype(F32)
    ones = jnp.ones((16, DH), BF16)
    row_id = lax.broadcasted_iota(jnp.int32, (16, BLOCK), 0)
    head_id = lax.broadcasted_iota(jnp.int32, (H, BLOCK), 0)
    for slot, (shift, piece) in enumerate(zip(shifts, pieces)):
        group = lax.rem(place + shift, ROW)
        loads[slot][0].wait()
        loads[slot][1].wait()
        for head in range(GQ):
            cut = slice(head * DH, (head + 1) * DH)
            product = piece[BLOCK:STAT, cut].astype(F32) * held_outputs[slot, :, cut].astype(F32)
            high = product.astype(BF16)
            low = (product - high.astype(F32)).astype(BF16)
            dots = nt(ones, high) + nt(ones, low)
            first = dots.astype(BF16).astype(F32)
            second = (dots - first).astype(BF16).astype(F32)
            third = dots - first - second
            norm = jnp.sum(
                jnp.where(head_id == group * GQ + head, turned, 0.0), axis=0, keepdims=True
            )
            stats = jnp.where(
                row_id == 0,
                norm,
                jnp.where(row_id == 1, first, jnp.where(row_id == 2, second, third)),
            )
            piece[STAT:, cut] = stats.astype(BF16)
    for copy in late:
        copy.wait()


def in_order(piece0, piece1, piece2, piece3, all_out, late_out):
    place = lax.rem(lax.axis_index("head"), ROW)
    for block in range(ROW):
        shift = lax.rem(place + ROW - block, ROW)
        value = piece0[...]
        for number, piece in enumerate((piece1, piece2, piece3)):
            value = jnp.where(shift == number + 1, piece[...], value)
        all_out[block] = value
        if block > 0:
            late_out[block - 1] = value


def stacked(piece, start):
    return jnp.concatenate(
        [piece[start : start + BLOCK, head * DH : (head + 1) * DH] for head in range(GQ)], axis=0
    )


def sweep(back, doc_start, pieces, kv, dq, dkv):
    head = lax.axis_index("head")
    place = lax.rem(head, ROW)
    own_row = head // ROW
    first_key = lax.axis_index("seq") * (ROW * ROW) + (own_row - back) * ROW
    for slot, piece in pieces.items():
        query_place = lax.rem(place + ROW - slot, ROW)
        start = doc_start[own_row * ROW + query_place]

        def turn(key_slot, carry, slot=slot, piece=piece, start=start, query_place=query_place):
            key_place = key_slot + (1 if back == 2 else 0)
            seen = first_key + key_place >= start
            if back == 0:
                seen = seen & (key_place <= query_place)

            @pl.when(seen)
            def _():
                key = kv[key_slot, :, :DH]
                value = kv[key_slot, :, DH:]
                query = stacked(piece, 0)
                grad = stacked(piece, BLOCK)
                stats = piece[STAT:, :].astype(F32)
                norm = stats[0:1]
                dots = stats[1:2] + stats[2:3] + stats[3:4]
                weights = jnp.exp(nt(key, query) * SCALE - norm)
                if back == 0:
                    key_pos = lax.broadcasted_iota(jnp.int32, (BLOCK, WIDE), 0)
                    query_pos = lax.broadcasted_iota(jnp.int32, (BLOCK, WIDE), 1) % BLOCK
                    ahead = (query_place - key_place) * BLOCK
                    weights = jnp.where(key_pos <= query_pos + ahead, weights, 0.0)
                grad_scores = (weights * (nt(value, grad) - dots)).astype(BF16)
                dkv[key_slot, :, DH:] += nn(weights.astype(BF16), grad)
                dkv[key_slot, :, :DH] += nn(grad_scores, query)
                dq[slot] += nn(key.T, grad_scores)

            return carry

        lax.fori_loop(0, ROW - 1 if back == 2 else ROW, turn, 0)


def begin_own(doc_start, piece0, piece1, piece3, kv, dkv, dq):
    dkv[...] = jnp.zeros_like(dkv)
    for slot in (0, 1, 3):
        dq[slot] = jnp.zeros((DH, WIDE), F32)
    sweep(0, doc_start, {0: piece0, 1: piece1, 3: piece3}, kv, dq, dkv)


def begin_one(doc_start, piece0, piece1, piece3, kv, dq_in, dkv, dq):
    dkv[...] = jnp.zeros_like(dkv)
    for slot in (0, 1, 3):
        dq[slot] = dq_in[slot]
    sweep(1, doc_start, {0: piece0, 1: piece1, 3: piece3}, kv, dq, dkv)


def begin_two(doc_start, piece0, piece1, piece3, kv, dq_in, dkv, dq):
    dkv[...] = jnp.zeros_like(dkv)
    for slot in (0, 1, 3):
        dq[slot] = dq_in[slot]
    sweep(2, doc_start, {0: piece0, 1: piece1, 3: piece3}, kv, dq, dkv)


def round_kv(dkv, out):
    out[:, :, :DH] = (dkv[:, :, :DH] * SCALE).astype(BF16)
    out[:, :, DH:] = dkv[:, :, DH:].astype(BF16)


def finish_earlier(
    doc_start, piece2, kv_two, kv_one, two_in, one_in, two_out, one_out, late, two, one
):
    late[...] = jnp.zeros_like(late)
    two[...] = two_in[...]
    one[...] = one_in[...]
    sweep(2, doc_start, {2: piece2}, kv_two, Shifted(late), two)
    round_kv(two, two_out)
    sweep(1, doc_start, {2: piece2}, kv_one, Shifted(late), one)
    round_kv(one, one_out)


def finish_own(
    doc_start, piece2, kv, dkv_in, dq_in, late_in, dkv, out0, out1, out2, out3, late
):
    dkv[...] = dkv_in[...]
    late[...] = late_in[...]
    sweep(0, doc_start, {2: piece2}, kv, Shifted(late), dkv)
    dkv[:, :, :DH] = dkv[:, :, :DH] * SCALE
    for slot, out in enumerate((out0, out1, out2, out3)):
        for head in range(GQ):
            cut = slice(head * DH, (head + 1) * DH)
            total = late[0, :, cut] if slot == 2 else dq_in[slot, :, cut]
            out[:, cut] = (total.T * SCALE).astype(BF16)


class Shifted:
    def __init__(self, ref):
        self.ref = ref

    def __getitem__(self, slot):
        return self.ref[slot - 2]

    def __setitem__(self, slot, value):
        self.ref[slot - 2] = value


def add_up(own, one, two, *pieces):
    place = lax.rem(lax.axis_index("head"), ROW)
    for slot in range(ROW):
        block = lax.rem(place + ROW - slot, ROW)
        earlier = jnp.where(block > 0, two[jnp.maximum(block - 1, 0)].astype(F32), 0.0)
        pieces[slot][...] = (own[block] + one[block].astype(F32) + earlier).astype(BF16)


def join_queries(piece0, piece1, piece2, piece3, out, sems):
    place = lax.rem(lax.axis_index("head"), ROW)
    copies = []
    for shift, piece in enumerate((piece0, piece1, piece2, piece3)):
        span = pl.ds(pl.multiple_of(lax.rem(place + shift, ROW) * WIDE, WIDE), WIDE)
        copies.append(pltpu.make_async_copy(piece, out.at[:, span], sems.at[shift]))
    for copy in copies:
        copy.start()
    for copy in copies:
        copy.wait()


def join_kv(piece0, piece1, piece2, piece3, key_out, value_out, sems):
    place = lax.rem(lax.axis_index("head"), ROW)
    copies = []
    for shift, piece in enumerate((piece0, piece1, piece2, piece3)):
        columns = pl.ds(pl.multiple_of(lax.rem(place + shift, ROW) * DH, DH), DH)
        for part, out in enumerate((key_out, value_out)):
            copies.append(
                pltpu.make_async_copy(
                    piece.at[:, pl.ds(part * DH, DH)], out.at[:, columns], sems.at[shift, part]
                )
            )
    for copy in copies:
        copy.start()
    for copy in copies:
        copy.wait()


def kernel(body, name, in_specs, shapes, scratch=(), out_spec=VMEM, grant=24, cost=0):
    return pl.pallas_call(
        body,
        in_specs=in_specs,
        out_specs=[out_spec] * len(shapes),
        out_shape=[jax.ShapeDtypeStruct(*shape) for shape in shapes],
        scratch_shapes=scratch,
        compiler_params=pltpu.CompilerParams(vmem_limit_bytes=grant << 20),
        cost_estimate=pl.CostEstimate(flops=cost, bytes_accessed=cost, transcendentals=0),
        name=name,
    )


def per_device(queries, outputs, out_grads, log_norms, keys, values, doc_start):
    seqs = lax.axis_size("seq")
    heads = lax.axis_size("head")
    total = seqs * heads
    sems = pltpu.SemaphoreType.DMA

    def along_row(value, shift):
        if shift % ROW == 0:
            return value
        pairs = [(b, b - b % ROW + (b + shift) % ROW) for b in range(total)]
        return lax.ppermute(value, AXES, pairs)

    def along_rows(value, rows):
        by = rows * ROW
        return lax.ppermute(value, AXES, [(b, (b + by) % total) for b in range(total)])

    kv_shape = (ROW, BLOCK, 2 * DH)
    late_shape = (ROW - 1, BLOCK, 2 * DH)
    dq_shape = ((ROW, DH, WIDE), F32)
    piece_shape = ((PIECE, WIDE), BF16)
    turned = log_norms.T

    def pack_scratch(count):
        return [
            pltpu.VMEM((count, BLOCK, WIDE), BF16),
            pltpu.VMEM((H, BLOCK), BF16),
            sems((ROW, 6)),
        ]

    kv_piece = ((BLOCK, 2 * DH), BF16)
    kv_sent = kernel(
        pack_kv, "pack_kv", [HBM] * 2, [kv_piece] * ROW, [sems((ROW, 2))], grant=56
    )(keys, values)
    kv_pieces = [along_row(kv_sent[shift], shift) for shift in range(ROW)]
    kv_sent, turned = lax.optimization_barrier((kv_sent, turned))
    near = kernel(
        functools.partial(pack, (1, 3)),
        "pack_near",
        [HBM] * 4,
        [piece_shape] * 2,
        pack_scratch(2),
        grant=56,
    )(queries, outputs, out_grads, turned)
    kv_pieces, near = lax.optimization_barrier((kv_pieces, near))
    piece1 = along_row(near[0], 1)
    piece3 = along_row(near[1], 3)
    kv_own, kv_late = kernel(
        in_order, "in_order", [VMEM] * ROW, [(kv_shape, BF16), (late_shape, BF16)]
    )(*kv_pieces)
    kv_one = along_rows(kv_own, 1)
    kv_two = along_rows(kv_late, 2)
    kv_own, turned = lax.optimization_barrier((kv_own, turned))
    piece0, far = kernel(
        functools.partial(pack, (0, 2)),
        "pack_rest",
        [HBM] * 4,
        [piece_shape] * 2,
        pack_scratch(2),
        grant=52,
    )(queries, outputs, out_grads, turned)
    piece1, far = lax.optimization_barrier((piece1, far))
    piece2 = along_row(far, 2)

    dkv_own, dq = kernel(
        begin_own, "begin_own", [SMEM] + [VMEM] * 4, [(kv_shape, F32), dq_shape], cost=HEAVY
    )(doc_start, piece0, piece1, piece3, kv_own)
    dkv_one, dq = kernel(
        begin_one, "begin_one", [SMEM] + [VMEM] * 5, [(kv_shape, F32), dq_shape], cost=HEAVY
    )(doc_start, piece0, piece1, piece3, kv_one, dq)
    dkv_two, dq = kernel(
        begin_two,
        "begin_two",
        [SMEM] + [VMEM] * 5,
        [(late_shape, F32), dq_shape],
        cost=HEAVY,
    )(doc_start, piece0, piece1, piece3, kv_two, dq)
    far_shape = ((1, DH, WIDE), F32)
    dkv_two, dkv_one, dq_far = kernel(
        finish_earlier,
        "finish_earlier",
        [SMEM] + [VMEM] * 5,
        [(late_shape, BF16), (kv_shape, BF16), far_shape],
        [pltpu.VMEM(late_shape, F32), pltpu.VMEM(kv_shape, F32)],
        cost=HEAVY,
    )(doc_start, piece2, kv_two, kv_one, dkv_two, dkv_one)
    back_two = along_rows(dkv_two, -2)
    back_one = along_rows(dkv_one, -1)
    dkv_own, *dq_sent = kernel(
        finish_own,
        "finish_own",
        [SMEM] + [VMEM] * 5,
        [(kv_shape, F32)] + [((BLOCK, WIDE), BF16)] * ROW,
        [pltpu.VMEM(*far_shape)],
        cost=HEAVY,
    )(doc_start, piece2, kv_own, dkv_own, dq, dq_far)
    dq_pieces = [along_row(dq_sent[slot], -slot) for slot in range(ROW)]
    (query_out,) = kernel(
        join_queries,
        "join_queries",
        [VMEM] * ROW,
        [((BLOCK, H * DH), BF16)],
        [sems((ROW,))],
        HBM,
    )(*dq_pieces)
    dkv_sent = kernel(
        add_up, "add_up", [VMEM] * 3, [((BLOCK, 2 * DH), BF16)] * ROW, cost=HEAVY
    )(
        dkv_own, back_one, back_two
    )
    dkv_pieces = [along_row(dkv_sent[slot], -slot) for slot in range(ROW)]
    key_out, value_out = kernel(
        join_kv,
        "join_kv",
        [VMEM] * ROW,
        [((BLOCK, KVH * DH), BF16)] * 2,
        [sems((ROW, 2))],
        HBM,
    )(*dkv_pieces)
    return (query_out, key_out, value_out)


def solution(mesh):
    placed = P(("seq", "head"), None)
    return jax.shard_map(
        per_device,
        mesh=mesh,
        in_specs=(placed,) * 6 + (P("seq"),),
        out_specs=(placed,) * 3,
        check_vma=False,
    )
```

```python
import functools

import jax
import jax.numpy as jnp
from jax import lax
from jax.experimental import pallas as pl
from jax.experimental.pallas import tpu as pltpu
from jax.sharding import PartitionSpec as P

H = 32
KVH = 4
DH = 128
BLOCK = 128
GQ = 8
ROW = 4
WIDE = GQ * DH
SCALE = DH ** (-0.5)
AXES = ("seq", "head")
STAT = 2 * BLOCK
PIECE = STAT + 16
HEAVY = 20_000_000_000
F32 = jnp.float32
BF16 = jnp.bfloat16

VMEM = pl.BlockSpec(memory_space=pltpu.VMEM)
HBM = pl.BlockSpec(memory_space=pltpu.HBM)
SMEM = pl.BlockSpec(memory_space=pltpu.SMEM)


def nt(left, right):
    return lax.dot_general(left, right, (((1,), (1,)), ((), ())), preferred_element_type=F32)


def nn(left, right):
    return jnp.dot(left, right, preferred_element_type=F32)


def pack_kv(keys, values, piece0, piece1, piece2, piece3, sems):
    place = lax.rem(lax.axis_index("head"), ROW)
    copies = []
    for shift, piece in enumerate((piece0, piece1, piece2, piece3)):
        columns = pl.ds(pl.multiple_of(lax.rem(place + shift, ROW) * DH, DH), DH)
        for part, source in enumerate((keys, values)):
            copies.append(
                pltpu.make_async_copy(
                    source.at[:, columns],
                    piece.at[:, pl.ds(part * DH, DH)],
                    sems.at[shift, part],
                )
            )
    for copy in copies:
        copy.start()
    for copy in copies:
        copy.wait()


def pack(shifts, queries, outputs, grads, norms, *rest):
    place = lax.rem(lax.axis_index("head"), ROW)
    count = len(shifts)
    held_outputs, held_norms, sems = rest[-3:]
    pieces = rest[-3 - count : -3]
    loads = []
    for slot, (shift, piece) in enumerate(zip(shifts, pieces)):
        group = lax.rem(place + shift, ROW)
        span = pl.ds(pl.multiple_of(group * WIDE, WIDE), WIDE)
        loads.append(
            [
                pltpu.make_async_copy(source.at[:, span], target, sems.at[slot, part])
                for part, (source, target) in enumerate(
                    (
                        (grads, piece.at[pl.ds(BLOCK, BLOCK), :]),
                        (outputs, held_outputs.at[slot]),
                        (queries, piece.at[pl.ds(0, BLOCK), :]),
                    )
                )
            ]
        )
    late = [load[2] for load in loads]
    norm_copy = pltpu.make_async_copy(norms, held_norms, sems.at[0, 3])
    norm_copy.start()
    for load in loads:
        load[0].start()
        load[1].start()
    for copy in late:
        copy.start()
    norm_copy.wait()
    turned = held_norms[...].astype(F32)
    ones = jnp.ones((16, DH), BF16)
    row_id = lax.broadcasted_iota(jnp.int32, (16, BLOCK), 0)
    head_id = lax.broadcasted_iota(jnp.int32, (H, BLOCK), 0)
    for slot, (shift, piece) in enumerate(zip(shifts, pieces)):
        group = lax.rem(place + shift, ROW)
        loads[slot][0].wait()
        loads[slot][1].wait()
        for head in range(GQ):
            cut = slice(head * DH, (head + 1) * DH)
            product = piece[BLOCK:STAT, cut].astype(F32) * held_outputs[slot, :, cut].astype(F32)
            high = product.astype(BF16)
            low = (product - high.astype(F32)).astype(BF16)
            dots = nt(ones, high) + nt(ones, low)
            first = dots.astype(BF16).astype(F32)
            second = (dots - first).astype(BF16).astype(F32)
            third = dots - first - second
            norm = jnp.sum(
                jnp.where(head_id == group * GQ + head, turned, 0.0), axis=0, keepdims=True
            )
            stats = jnp.where(
                row_id == 0,
                norm,
                jnp.where(row_id == 1, first, jnp.where(row_id == 2, second, third)),
            )
            piece[STAT:, cut] = stats.astype(BF16)
    for copy in late:
        copy.wait()


def in_order(piece0, piece1, piece2, piece3, all_out, late_out):
    place = lax.rem(lax.axis_index("head"), ROW)
    for block in range(ROW):
        shift = lax.rem(place + ROW - block, ROW)
        value = piece0[...]
        for number, piece in enumerate((piece1, piece2, piece3)):
            value = jnp.where(shift == number + 1, piece[...], value)
        all_out[block] = value
        if block > 0:
            late_out[block - 1] = value


def stacked(piece, start):
    return jnp.concatenate(
        [piece[start : start + BLOCK, head * DH : (head + 1) * DH] for head in range(GQ)], axis=0
    )


def sweep(back, doc_start, pieces, kv, dq, dkv):
    head = lax.axis_index("head")
    place = lax.rem(head, ROW)
    own_row = head // ROW
    first_key = lax.axis_index("seq") * (ROW * ROW) + (own_row - back) * ROW
    for slot, piece in pieces.items():
        query_place = lax.rem(place + ROW - slot, ROW)
        start = doc_start[own_row * ROW + query_place]

        def turn(key_slot, carry, slot=slot, piece=piece, start=start, query_place=query_place):
            key_place = key_slot + (1 if back == 2 else 0)
            seen = first_key + key_place >= start
            if back == 0:
                seen = seen & (key_place <= query_place)

            @pl.when(seen)
            def _():
                key = kv[key_slot, :, :DH]
                value = kv[key_slot, :, DH:]
                query = stacked(piece, 0)
                grad = stacked(piece, BLOCK)
                stats = piece[STAT:, :].astype(F32)
                norm = stats[0:1]
                dots = stats[1:2] + stats[2:3] + stats[3:4]
                weights = jnp.exp(nt(key, query) * SCALE - norm)
                if back == 0:
                    key_pos = lax.broadcasted_iota(jnp.int32, (BLOCK, WIDE), 0)
                    query_pos = lax.broadcasted_iota(jnp.int32, (BLOCK, WIDE), 1) % BLOCK
                    ahead = (query_place - key_place) * BLOCK
                    weights = jnp.where(key_pos <= query_pos + ahead, weights, 0.0)
                grad_scores = (weights * (nt(value, grad) - dots)).astype(BF16)
                dkv[key_slot, :, DH:] += nn(weights.astype(BF16), grad)
                dkv[key_slot, :, :DH] += nn(grad_scores, query)
                dq[slot] += nn(key.T, grad_scores)

            return carry

        lax.fori_loop(0, ROW - 1 if back == 2 else ROW, turn, 0)


def begin_own(doc_start, piece0, piece1, piece3, kv, dkv, dq):
    dkv[...] = jnp.zeros_like(dkv)
    for slot in (0, 1, 3):
        dq[slot] = jnp.zeros((DH, WIDE), F32)
    sweep(0, doc_start, {0: piece0, 1: piece1, 3: piece3}, kv, dq, dkv)


def begin_one(doc_start, piece0, piece1, piece3, kv, dq_in, dkv, dq):
    dkv[...] = jnp.zeros_like(dkv)
    for slot in (0, 1, 3):
        dq[slot] = dq_in[slot]
    sweep(1, doc_start, {0: piece0, 1: piece1, 3: piece3}, kv, dq, dkv)


def begin_two(doc_start, piece0, piece1, piece3, kv, dq_in, dkv, dq):
    dkv[...] = jnp.zeros_like(dkv)
    for slot in (0, 1, 3):
        dq[slot] = dq_in[slot]
    sweep(2, doc_start, {0: piece0, 1: piece1, 3: piece3}, kv, dq, dkv)


def round_kv(dkv, out):
    out[:, :, :DH] = (dkv[:, :, :DH] * SCALE).astype(BF16)
    out[:, :, DH:] = dkv[:, :, DH:].astype(BF16)


def finish_earlier(
    doc_start, piece2, kv_two, kv_one, two_in, one_in, two_out, one_out, late, two, one
):
    late[...] = jnp.zeros_like(late)
    two[...] = two_in[...]
    one[...] = one_in[...]
    sweep(2, doc_start, {2: piece2}, kv_two, Shifted(late), two)
    round_kv(two, two_out)
    sweep(1, doc_start, {2: piece2}, kv_one, Shifted(late), one)
    round_kv(one, one_out)


def finish_own(
    doc_start, piece2, kv, dkv_in, dq_in, late_in, dkv, out0, out1, out2, out3, late
):
    dkv[...] = dkv_in[...]
    late[...] = late_in[...]
    sweep(0, doc_start, {2: piece2}, kv, Shifted(late), dkv)
    dkv[:, :, :DH] = dkv[:, :, :DH] * SCALE
    for slot, out in enumerate((out0, out1, out2, out3)):
        for head in range(GQ):
            cut = slice(head * DH, (head + 1) * DH)
            total = late[0, :, cut] if slot == 2 else dq_in[slot, :, cut]
            out[:, cut] = (total.T * SCALE).astype(BF16)


class Shifted:
    def __init__(self, ref):
        self.ref = ref

    def __getitem__(self, slot):
        return self.ref[slot - 2]

    def __setitem__(self, slot, value):
        self.ref[slot - 2] = value


def add_up(own, one, two, *pieces):
    place = lax.rem(lax.axis_index("head"), ROW)
    for slot in range(ROW):
        block = lax.rem(place + ROW - slot, ROW)
        earlier = jnp.where(block > 0, two[jnp.maximum(block - 1, 0)].astype(F32), 0.0)
        pieces[slot][...] = (own[block] + one[block].astype(F32) + earlier).astype(BF16)


def join_queries(piece0, piece1, piece2, piece3, out, sems):
    place = lax.rem(lax.axis_index("head"), ROW)
    copies = []
    for shift, piece in enumerate((piece0, piece1, piece2, piece3)):
        span = pl.ds(pl.multiple_of(lax.rem(place + shift, ROW) * WIDE, WIDE), WIDE)
        copies.append(pltpu.make_async_copy(piece, out.at[:, span], sems.at[shift]))
    for copy in copies:
        copy.start()
    for copy in copies:
        copy.wait()


def join_kv(piece0, piece1, piece2, piece3, key_out, value_out, sems):
    place = lax.rem(lax.axis_index("head"), ROW)
    copies = []
    for shift, piece in enumerate((piece0, piece1, piece2, piece3)):
        columns = pl.ds(pl.multiple_of(lax.rem(place + shift, ROW) * DH, DH), DH)
        for part, out in enumerate((key_out, value_out)):
            copies.append(
                pltpu.make_async_copy(
                    piece.at[:, pl.ds(part * DH, DH)], out.at[:, columns], sems.at[shift, part]
                )
            )
    for copy in copies:
        copy.start()
    for copy in copies:
        copy.wait()


def kernel(body, name, in_specs, shapes, scratch=(), out_spec=VMEM, grant=24, cost=0):
    return pl.pallas_call(
        body,
        in_specs=in_specs,
        out_specs=[out_spec] * len(shapes),
        out_shape=[jax.ShapeDtypeStruct(*shape) for shape in shapes],
        scratch_shapes=scratch,
        compiler_params=pltpu.CompilerParams(vmem_limit_bytes=grant << 20),
        cost_estimate=pl.CostEstimate(flops=cost, bytes_accessed=cost, transcendentals=0),
        name=name,
    )


def per_device(queries, outputs, out_grads, log_norms, keys, values, doc_start):
    seqs = lax.axis_size("seq")
    heads = lax.axis_size("head")
    total = seqs * heads
    sems = pltpu.SemaphoreType.DMA

    def along_row(value, shift):
        if shift % ROW == 0:
            return value
        pairs = [(b, b - b % ROW + (b + shift) % ROW) for b in range(total)]
        return lax.ppermute(value, AXES, pairs)

    def along_rows(value, rows):
        by = rows * ROW
        return lax.ppermute(value, AXES, [(b, (b + by) % total) for b in range(total)])

    kv_shape = (ROW, BLOCK, 2 * DH)
    late_shape = (ROW - 1, BLOCK, 2 * DH)
    dq_shape = ((ROW, DH, WIDE), F32)
    piece_shape = ((PIECE, WIDE), BF16)
    turned = log_norms.T

    def pack_scratch(count):
        return [
            pltpu.VMEM((count, BLOCK, WIDE), BF16),
            pltpu.VMEM((H, BLOCK), BF16),
            sems((ROW, 6)),
        ]

    kv_piece = ((BLOCK, 2 * DH), BF16)
    kv_sent = kernel(
        pack_kv, "pack_kv", [HBM] * 2, [kv_piece] * ROW, [sems((ROW, 2))], grant=56
    )(keys, values)
    kv_pieces = [along_row(kv_sent[shift], shift) for shift in range(ROW)]
    kv_sent, turned = lax.optimization_barrier((kv_sent, turned))
    near = kernel(
        functools.partial(pack, (1, 3)),
        "pack_near",
        [HBM] * 4,
        [piece_shape] * 2,
        pack_scratch(2),
        grant=56,
    )(queries, outputs, out_grads, turned)
    kv_pieces, near = lax.optimization_barrier((kv_pieces, near))
    piece1 = along_row(near[0], 1)
    piece3 = along_row(near[1], 3)
    kv_own, kv_late = kernel(
        in_order, "in_order", [VMEM] * ROW, [(kv_shape, BF16), (late_shape, BF16)]
    )(*kv_pieces)
    kv_one = along_rows(kv_own, 1)
    kv_two = along_rows(kv_late, 2)
    kv_own, turned = lax.optimization_barrier((kv_own, turned))
    piece0, far = kernel(
        functools.partial(pack, (0, 2)),
        "pack_rest",
        [HBM] * 4,
        [piece_shape] * 2,
        pack_scratch(2),
        grant=52,
    )(queries, outputs, out_grads, turned)
    piece1, piece3, far = lax.optimization_barrier((piece1, piece3, far))
    piece2 = along_row(far, 2)

    dkv_own, dq = kernel(
        begin_own, "begin_own", [SMEM] + [VMEM] * 4, [(kv_shape, F32), dq_shape], cost=HEAVY
    )(doc_start, piece0, piece1, piece3, kv_own)
    dkv_one, dq = kernel(
        begin_one, "begin_one", [SMEM] + [VMEM] * 5, [(kv_shape, F32), dq_shape], cost=HEAVY
    )(doc_start, piece0, piece1, piece3, kv_one, dq)
    dkv_two, dq = kernel(
        begin_two,
        "begin_two",
        [SMEM] + [VMEM] * 5,
        [(late_shape, F32), dq_shape],
        cost=HEAVY,
    )(doc_start, piece0, piece1, piece3, kv_two, dq)
    far_shape = ((1, DH, WIDE), F32)
    dkv_two, dkv_one, dq_far = kernel(
        finish_earlier,
        "finish_earlier",
        [SMEM] + [VMEM] * 5,
        [(late_shape, BF16), (kv_shape, BF16), far_shape],
        [pltpu.VMEM(late_shape, F32), pltpu.VMEM(kv_shape, F32)],
        cost=HEAVY,
    )(doc_start, piece2, kv_two, kv_one, dkv_two, dkv_one)
    back_two = along_rows(dkv_two, -2)
    back_one = along_rows(dkv_one, -1)
    dkv_own, *dq_sent = kernel(
        finish_own,
        "finish_own",
        [SMEM] + [VMEM] * 5,
        [(kv_shape, F32)] + [((BLOCK, WIDE), BF16)] * ROW,
        [pltpu.VMEM(*far_shape)],
        cost=HEAVY,
    )(doc_start, piece2, kv_own, dkv_own, dq, dq_far)
    dq_pieces = [along_row(dq_sent[slot], -slot) for slot in range(ROW)]
    (query_out,) = kernel(
        join_queries,
        "join_queries",
        [VMEM] * ROW,
        [((BLOCK, H * DH), BF16)],
        [sems((ROW,))],
        HBM,
    )(*dq_pieces)
    dkv_sent = kernel(
        add_up, "add_up", [VMEM] * 3, [((BLOCK, 2 * DH), BF16)] * ROW, cost=HEAVY
    )(
        dkv_own, back_one, back_two
    )
    dkv_pieces = [along_row(dkv_sent[slot], -slot) for slot in range(ROW)]
    key_out, value_out = kernel(
        join_kv,
        "join_kv",
        [VMEM] * ROW,
        [((BLOCK, KVH * DH), BF16)] * 2,
        [sems((ROW, 2))],
        HBM,
    )(*dkv_pieces)
    return (query_out, key_out, value_out)


def solution(mesh):
    placed = P(("seq", "head"), None)
    return jax.shard_map(
        per_device,
        mesh=mesh,
        in_specs=(placed,) * 6 + (P("seq"),),
        out_specs=(placed,) * 3,
        check_vma=False,
    )
```

```python
import functools

import jax
import jax.numpy as jnp
from jax import lax
from jax.experimental import pallas as pl
from jax.experimental.pallas import tpu as pltpu
from jax.sharding import PartitionSpec as P

H = 32
KVH = 4
DH = 128
BLOCK = 128
GQ = 8
ROW = 4
WIDE = GQ * DH
SCALE = DH ** (-0.5)
AXES = ("seq", "head")
PAIR = 2 * DH
HALF = GQ // 2 * BLOCK
STAT = 2 * HALF
PIECE = STAT + 16
HEAVY = 20_000_000_000
F32 = jnp.float32
BF16 = jnp.bfloat16

VMEM = pl.BlockSpec(memory_space=pltpu.VMEM)
HBM = pl.BlockSpec(memory_space=pltpu.HBM)
SMEM = pl.BlockSpec(memory_space=pltpu.SMEM)


def nt(left, right):
    return lax.dot_general(left, right, (((1,), (1,)), ((), ())), preferred_element_type=F32)


def nn(left, right):
    return jnp.dot(left, right, preferred_element_type=F32)


def pack_kv(keys, values, piece0, piece1, piece2, piece3, sems):
    place = lax.rem(lax.axis_index("head"), ROW)
    copies = []
    for shift, piece in enumerate((piece0, piece1, piece2, piece3)):
        columns = pl.ds(pl.multiple_of(lax.rem(place + shift, ROW) * DH, DH), DH)
        for part, source in enumerate((keys, values)):
            copies.append(
                pltpu.make_async_copy(
                    source.at[:, columns],
                    piece.at[:, pl.ds(part * DH, DH)],
                    sems.at[shift, part],
                )
            )
    for copy in copies:
        copy.start()
    for copy in copies:
        copy.wait()


def pack(shifts, queries, outputs, grads, norms, *rest):
    place = lax.rem(lax.axis_index("head"), ROW)
    count = len(shifts)
    pieces = rest[:count]
    held, held_norms, sems = rest[count:]
    loads = []
    for slot, shift in enumerate(shifts):
        group = lax.rem(place + shift, ROW)
        span = pl.ds(pl.multiple_of(group * WIDE, WIDE), WIDE)
        loads.append(
            [
                pltpu.make_async_copy(
                    source.at[:, span], held.at[slot, part], sems.at[slot, part]
                )
                for part, source in enumerate((grads, outputs, queries))
            ]
        )
    norm_copy = pltpu.make_async_copy(norms, held_norms, sems.at[0, 3])
    norm_copy.start()
    for load in loads:
        for copy in load:
            copy.start()
    norm_copy.wait()
    turned = held_norms[...].astype(F32)
    ones = jnp.ones((16, DH), BF16)
    row_id = lax.broadcasted_iota(jnp.int32, (16, BLOCK), 0)
    kind = row_id // 4
    head_id = lax.broadcasted_iota(jnp.int32, (H, BLOCK), 0)
    for slot, (shift, piece) in enumerate(zip(shifts, pieces)):
        group = lax.rem(place + shift, ROW)
        loads[slot][0].wait()
        loads[slot][1].wait()
        stats = [jnp.zeros((16, BLOCK), F32)] * 2
        for head in range(GQ):
            cut = slice(head * DH, (head + 1) * DH)
            grad = held[slot, 0, :, cut]
            product = grad.astype(F32) * held[slot, 1, :, cut].astype(F32)
            high = product.astype(BF16)
            low = (product - high.astype(F32)).astype(BF16)
            dots = nt(ones, high) + nt(ones, low)
            first = dots.astype(BF16).astype(F32)
            second = (dots - first).astype(BF16).astype(F32)
            third = dots - first - second
            norm = jnp.sum(
                jnp.where(head_id == group * GQ + head, turned, 0.0), axis=0, keepdims=True
            )
            both = jnp.where(
                kind == 0,
                norm,
                jnp.where(kind == 1, first, jnp.where(kind == 2, second, third)),
            )
            stats[head % 2] = jnp.where(row_id % 4 == head // 2, both, stats[head % 2])
            rows = slice(HALF + head // 2 * BLOCK, HALF + (head // 2 + 1) * BLOCK)
            piece[rows, head % 2 * DH : (head % 2 + 1) * DH] = grad
        piece[STAT:, :DH] = stats[0].astype(BF16)
        piece[STAT:, DH:] = stats[1].astype(BF16)
    for slot, piece in enumerate(pieces):
        loads[slot][2].wait()
        for pair in range(GQ // 2):
            piece[pair * BLOCK : (pair + 1) * BLOCK, :] = held[
                slot, 2, :, pair * PAIR : (pair + 1) * PAIR
            ]


def in_order(piece0, piece1, piece2, piece3, all_out, late_out):
    place = lax.rem(lax.axis_index("head"), ROW)
    for block in range(ROW):
        shift = lax.rem(place + ROW - block, ROW)
        value = piece0[...]
        for number, piece in enumerate((piece1, piece2, piece3)):
            value = jnp.where(shift == number + 1, piece[...], value)
        all_out[block] = value
        if block > 0:
            late_out[block - 1] = value


def stacked(piece, start):
    return jnp.concatenate(
        [
            piece[
                start + head // 2 * BLOCK : start + (head // 2 + 1) * BLOCK,
                head % 2 * DH : (head % 2 + 1) * DH,
            ]
            for head in range(GQ)
        ],
        axis=0,
    )


def side_by_side(rows):
    return jnp.concatenate([rows[pair : pair + 1] for pair in range(GQ // 2)], axis=1)


def sweep(back, doc_start, pieces, kv, dq, dkv):
    head = lax.axis_index("head")
    place = lax.rem(head, ROW)
    own_row = head // ROW
    first_key = lax.axis_index("seq") * (ROW * ROW) + (own_row - back) * ROW
    for slot, piece in pieces.items():
        query_place = lax.rem(place + ROW - slot, ROW)
        start = doc_start[own_row * ROW + query_place]

        def turn(key_slot, carry, slot=slot, piece=piece, start=start, query_place=query_place):
            key_place = key_slot + (1 if back == 2 else 0)
            seen = first_key + key_place >= start
            if back == 0:
                seen = seen & (key_place <= query_place)

            @pl.when(seen)
            def _():
                key = kv[key_slot, :, :DH]
                value = kv[key_slot, :, DH:]
                query = stacked(piece, 0)
                grad = stacked(piece, HALF)
                stats = piece[STAT:, :].astype(F32)
                norm = side_by_side(stats[0:4])
                dots = side_by_side(stats[4:8] + stats[8:12] + stats[12:16])
                weights = jnp.exp(nt(key, query) * SCALE - norm)
                if back == 0:
                    key_pos = lax.broadcasted_iota(jnp.int32, (BLOCK, WIDE), 0)
                    query_pos = lax.broadcasted_iota(jnp.int32, (BLOCK, WIDE), 1) % BLOCK
                    ahead = (query_place - key_place) * BLOCK
                    weights = jnp.where(key_pos <= query_pos + ahead, weights, 0.0)
                grad_scores = (weights * (nt(value, grad) - dots)).astype(BF16)
                dkv[key_slot, :, DH:] += nn(weights.astype(BF16), grad)
                dkv[key_slot, :, :DH] += nn(grad_scores, query)
                dq[slot] += nn(key.T, grad_scores)

            return carry

        lax.fori_loop(0, ROW - 1 if back == 2 else ROW, turn, 0)


def begin_own(doc_start, piece0, piece1, piece3, kv, dkv, dq):
    dkv[...] = jnp.zeros_like(dkv)
    for slot in (0, 1, 3):
        dq[slot] = jnp.zeros((DH, WIDE), F32)
    sweep(0, doc_start, {0: piece0, 1: piece1, 3: piece3}, kv, dq, dkv)


def begin_one(doc_start, piece0, piece1, piece3, kv, dq_in, dkv, dq):
    dkv[...] = jnp.zeros_like(dkv)
    for slot in (0, 1, 3):
        dq[slot] = dq_in[slot]
    sweep(1, doc_start, {0: piece0, 1: piece1, 3: piece3}, kv, dq, dkv)


def begin_two(doc_start, piece0, piece1, piece3, kv, dq_in, dkv, dq):
    dkv[...] = jnp.zeros_like(dkv)
    for slot in (0, 1, 3):
        dq[slot] = dq_in[slot]
    sweep(2, doc_start, {0: piece0, 1: piece1, 3: piece3}, kv, dq, dkv)


def round_kv(dkv, out):
    out[:, :, :DH] = (dkv[:, :, :DH] * SCALE).astype(BF16)
    out[:, :, DH:] = dkv[:, :, DH:].astype(BF16)


def finish_earlier(
    doc_start, piece2, kv_two, kv_one, two_in, one_in, two_out, one_out, late, two, one
):
    late[...] = jnp.zeros_like(late)
    two[...] = two_in[...]
    one[...] = one_in[...]
    sweep(2, doc_start, {2: piece2}, kv_two, Shifted(late), two)
    round_kv(two, two_out)
    sweep(1, doc_start, {2: piece2}, kv_one, Shifted(late), one)
    round_kv(one, one_out)


def finish_own(
    doc_start, piece2, kv, dkv_in, dq_in, late_in, dkv, out0, out1, out2, out3, late
):
    dkv[...] = dkv_in[...]
    late[...] = late_in[...]
    sweep(0, doc_start, {2: piece2}, kv, Shifted(late), dkv)
    dkv[:, :, :DH] = dkv[:, :, :DH] * SCALE
    for slot, out in enumerate((out0, out1, out2, out3)):
        for head in range(GQ):
            cut = slice(head * DH, (head + 1) * DH)
            total = late[0, :, cut] if slot == 2 else dq_in[slot, :, cut]
            out[:, cut] = (total.T * SCALE).astype(BF16)


class Shifted:
    def __init__(self, ref):
        self.ref = ref

    def __getitem__(self, slot):
        return self.ref[slot - 2]

    def __setitem__(self, slot, value):
        self.ref[slot - 2] = value


def add_up(own, one, two, *pieces):
    place = lax.rem(lax.axis_index("head"), ROW)
    for slot in range(ROW):
        block = lax.rem(place + ROW - slot, ROW)
        earlier = jnp.where(block > 0, two[jnp.maximum(block - 1, 0)].astype(F32), 0.0)
        pieces[slot][...] = (own[block] + one[block].astype(F32) + earlier).astype(BF16)


def join_queries(piece0, piece1, piece2, piece3, out, sems):
    place = lax.rem(lax.axis_index("head"), ROW)
    copies = []
    for shift, piece in enumerate((piece0, piece1, piece2, piece3)):
        span = pl.ds(pl.multiple_of(lax.rem(place + shift, ROW) * WIDE, WIDE), WIDE)
        copies.append(pltpu.make_async_copy(piece, out.at[:, span], sems.at[shift]))
    for copy in copies:
        copy.start()
    for copy in copies:
        copy.wait()


def join_kv(piece0, piece1, piece2, piece3, key_out, value_out, sems):
    place = lax.rem(lax.axis_index("head"), ROW)
    copies = []
    for shift, piece in enumerate((piece0, piece1, piece2, piece3)):
        columns = pl.ds(pl.multiple_of(lax.rem(place + shift, ROW) * DH, DH), DH)
        for part, out in enumerate((key_out, value_out)):
            copies.append(
                pltpu.make_async_copy(
                    piece.at[:, pl.ds(part * DH, DH)], out.at[:, columns], sems.at[shift, part]
                )
            )
    for copy in copies:
        copy.start()
    for copy in copies:
        copy.wait()


def kernel(body, name, in_specs, shapes, scratch=(), out_spec=VMEM, grant=24, cost=0):
    return pl.pallas_call(
        body,
        in_specs=in_specs,
        out_specs=[out_spec] * len(shapes),
        out_shape=[jax.ShapeDtypeStruct(*shape) for shape in shapes],
        scratch_shapes=scratch,
        compiler_params=pltpu.CompilerParams(vmem_limit_bytes=grant << 20),
        cost_estimate=pl.CostEstimate(flops=cost, bytes_accessed=cost, transcendentals=0),
        name=name,
    )


def per_device(queries, outputs, out_grads, log_norms, keys, values, doc_start):
    seqs = lax.axis_size("seq")
    heads = lax.axis_size("head")
    total = seqs * heads
    sems = pltpu.SemaphoreType.DMA

    def along_row(value, shift):
        if shift % ROW == 0:
            return value
        pairs = [(b, b - b % ROW + (b + shift) % ROW) for b in range(total)]
        return lax.ppermute(value, AXES, pairs)

    def along_rows(value, rows):
        by = rows * ROW
        return lax.ppermute(value, AXES, [(b, (b + by) % total) for b in range(total)])

    kv_shape = (ROW, BLOCK, 2 * DH)
    late_shape = (ROW - 1, BLOCK, 2 * DH)
    dq_shape = ((ROW, DH, WIDE), F32)
    piece_shape = ((PIECE, PAIR), BF16)
    turned = log_norms.T

    def pack_scratch(count):
        return [
            pltpu.VMEM((count, 3, BLOCK, WIDE), BF16),
            pltpu.VMEM((H, BLOCK), BF16),
            sems((count, 4)),
        ]

    kv_piece = ((BLOCK, 2 * DH), BF16)
    kv_sent = kernel(
        pack_kv, "pack_kv", [HBM] * 2, [kv_piece] * ROW, [sems((ROW, 2))], grant=56
    )(keys, values)
    kv_pieces = [along_row(kv_sent[shift], shift) for shift in range(ROW)]
    kv_sent, grads = lax.optimization_barrier((kv_sent, out_grads))
    near = kernel(
        functools.partial(pack, (1, 3)),
        "pack_near",
        [HBM] * 4,
        [piece_shape] * 2,
        pack_scratch(2),
        grant=52,
    )(queries, outputs, grads, turned)
    kv_pieces, near = lax.optimization_barrier((kv_pieces, near))
    piece1 = along_row(near[0], 1)
    piece3 = along_row(near[1], 3)
    kv_own, kv_late = kernel(
        in_order, "in_order", [VMEM] * ROW, [(kv_shape, BF16), (late_shape, BF16)]
    )(*kv_pieces)
    kv_one = along_rows(kv_own, 1)
    kv_two = along_rows(kv_late, 2)
    kv_own, grads_later = lax.optimization_barrier((kv_own, out_grads))
    piece0, far = kernel(
        functools.partial(pack, (0, 2)),
        "pack_rest",
        [HBM] * 4,
        [piece_shape] * 2,
        pack_scratch(2),
        grant=52,
    )(queries, outputs, grads_later, turned)
    piece1, piece3, far = lax.optimization_barrier((piece1, piece3, far))
    piece2 = along_row(far, 2)

    dkv_own, dq = kernel(
        begin_own, "begin_own", [SMEM] + [VMEM] * 4, [(kv_shape, F32), dq_shape], cost=HEAVY
    )(doc_start, piece0, piece1, piece3, kv_own)
    dkv_one, dq = kernel(
        begin_one, "begin_one", [SMEM] + [VMEM] * 5, [(kv_shape, F32), dq_shape], cost=HEAVY
    )(doc_start, piece0, piece1, piece3, kv_one, dq)
    dkv_two, dq = kernel(
        begin_two,
        "begin_two",
        [SMEM] + [VMEM] * 5,
        [(late_shape, F32), dq_shape],
        cost=HEAVY,
    )(doc_start, piece0, piece1, piece3, kv_two, dq)
    far_shape = ((1, DH, WIDE), F32)
    dkv_two, dkv_one, dq_far = kernel(
        finish_earlier,
        "finish_earlier",
        [SMEM] + [VMEM] * 5,
        [(late_shape, BF16), (kv_shape, BF16), far_shape],
        [pltpu.VMEM(late_shape, F32), pltpu.VMEM(kv_shape, F32)],
        cost=HEAVY,
    )(doc_start, piece2, kv_two, kv_one, dkv_two, dkv_one)
    back_two = along_rows(dkv_two, -2)
    back_one = along_rows(dkv_one, -1)
    dkv_own, *dq_sent = kernel(
        finish_own,
        "finish_own",
        [SMEM] + [VMEM] * 5,
        [(kv_shape, F32)] + [((BLOCK, WIDE), BF16)] * ROW,
        [pltpu.VMEM(*far_shape)],
        cost=HEAVY,
    )(doc_start, piece2, kv_own, dkv_own, dq, dq_far)
    dq_pieces = [along_row(dq_sent[slot], -slot) for slot in range(ROW)]
    (query_out,) = kernel(
        join_queries,
        "join_queries",
        [VMEM] * ROW,
        [((BLOCK, H * DH), BF16)],
        [sems((ROW,))],
        HBM,
    )(*dq_pieces)
    dkv_sent = kernel(
        add_up, "add_up", [VMEM] * 3, [((BLOCK, 2 * DH), BF16)] * ROW, cost=HEAVY
    )(
        dkv_own, back_one, back_two
    )
    dkv_pieces = [along_row(dkv_sent[slot], -slot) for slot in range(ROW)]
    key_out, value_out = kernel(
        join_kv,
        "join_kv",
        [VMEM] * ROW,
        [((BLOCK, KVH * DH), BF16)] * 2,
        [sems((ROW, 2))],
        HBM,
    )(*dkv_pieces)
    return (query_out, key_out, value_out)


def solution(mesh):
    placed = P(("seq", "head"), None)
    return jax.shard_map(
        per_device,
        mesh=mesh,
        in_specs=(placed,) * 6 + (P("seq"),),
        out_specs=(placed,) * 3,
        check_vma=False,
    )
```

```python
import functools

import jax
import jax.numpy as jnp
from jax import lax
from jax.experimental import pallas as pl
from jax.experimental.pallas import tpu as pltpu
from jax.sharding import PartitionSpec as P

H = 32
KVH = 4
DH = 128
BLOCK = 128
GQ = 8
ROW = 4
WIDE = GQ * DH
SCALE = DH ** (-0.5)
AXES = ("seq", "head")
PAIR = 2 * DH
HALF = GQ // 2 * BLOCK
STAT = 2 * HALF
PIECE = STAT + 16
HEAVY = 20_000_000_000
F32 = jnp.float32
BF16 = jnp.bfloat16

VMEM = pl.BlockSpec(memory_space=pltpu.VMEM)
HBM = pl.BlockSpec(memory_space=pltpu.HBM)
SMEM = pl.BlockSpec(memory_space=pltpu.SMEM)


def nt(left, right):
    return lax.dot_general(left, right, (((1,), (1,)), ((), ())), preferred_element_type=F32)


def nn(left, right):
    return jnp.dot(left, right, preferred_element_type=F32)


def pack_kv(keys, values, piece0, piece1, piece2, piece3, sems):
    place = lax.rem(lax.axis_index("head"), ROW)
    copies = []
    for shift, piece in enumerate((piece0, piece1, piece2, piece3)):
        columns = pl.ds(pl.multiple_of(lax.rem(place + shift, ROW) * DH, DH), DH)
        for part, source in enumerate((keys, values)):
            copies.append(
                pltpu.make_async_copy(
                    source.at[:, columns],
                    piece.at[:, pl.ds(part * DH, DH)],
                    sems.at[shift, part],
                )
            )
    for copy in copies:
        copy.start()
    for copy in copies:
        copy.wait()


def pack(shifts, queries, outputs, grads, norms, *rest):
    place = lax.rem(lax.axis_index("head"), ROW)
    count = len(shifts)
    pieces = rest[:count]
    held, held_norms, sems = rest[count:]
    loads = []
    for slot, shift in enumerate(shifts):
        group = lax.rem(place + shift, ROW)
        span = pl.ds(pl.multiple_of(group * WIDE, WIDE), WIDE)
        loads.append(
            [
                pltpu.make_async_copy(
                    source.at[:, span], held.at[slot, part], sems.at[slot, part]
                )
                for part, source in enumerate((grads, outputs, queries))
            ]
        )
    norm_copy = pltpu.make_async_copy(norms, held_norms, sems.at[0, 3])
    norm_copy.start()
    for load in loads:
        for copy in load:
            copy.start()
    norm_copy.wait()
    turned = held_norms[...].astype(F32)
    ones = jnp.ones((16, DH), BF16)
    row_id = lax.broadcasted_iota(jnp.int32, (16, BLOCK), 0)
    kind = row_id // 4
    head_id = lax.broadcasted_iota(jnp.int32, (H, BLOCK), 0)
    for slot, (shift, piece) in enumerate(zip(shifts, pieces)):
        group = lax.rem(place + shift, ROW)
        loads[slot][0].wait()
        loads[slot][1].wait()
        stats = [jnp.zeros((16, BLOCK), F32)] * 2
        for head in range(GQ):
            cut = slice(head * DH, (head + 1) * DH)
            grad = held[slot, 0, :, cut]
            product = grad.astype(F32) * held[slot, 1, :, cut].astype(F32)
            high = product.astype(BF16)
            low = (product - high.astype(F32)).astype(BF16)
            dots = nt(ones, high) + nt(ones, low)
            first = dots.astype(BF16).astype(F32)
            second = (dots - first).astype(BF16).astype(F32)
            third = dots - first - second
            norm = jnp.sum(
                jnp.where(head_id == group * GQ + head, turned, 0.0), axis=0, keepdims=True
            )
            both = jnp.where(
                kind == 0,
                norm,
                jnp.where(kind == 1, first, jnp.where(kind == 2, second, third)),
            )
            stats[head % 2] = jnp.where(row_id % 4 == head // 2, both, stats[head % 2])
            rows = slice(HALF + head // 2 * BLOCK, HALF + (head // 2 + 1) * BLOCK)
            piece[rows, head % 2 * DH : (head % 2 + 1) * DH] = grad
        piece[STAT:, :DH] = stats[0].astype(BF16)
        piece[STAT:, DH:] = stats[1].astype(BF16)
    for slot, piece in enumerate(pieces):
        loads[slot][2].wait()
        for pair in range(GQ // 2):
            piece[pair * BLOCK : (pair + 1) * BLOCK, :] = held[
                slot, 2, :, pair * PAIR : (pair + 1) * PAIR
            ]


def in_order(piece0, piece1, piece2, piece3, all_out, late_out):
    place = lax.rem(lax.axis_index("head"), ROW)
    for block in range(ROW):
        shift = lax.rem(place + ROW - block, ROW)
        value = piece0[...]
        for number, piece in enumerate((piece1, piece2, piece3)):
            value = jnp.where(shift == number + 1, piece[...], value)
        all_out[block] = value
        if block > 0:
            late_out[block - 1] = value


def stacked(piece, start):
    return jnp.concatenate(
        [
            piece[
                start + head // 2 * BLOCK : start + (head // 2 + 1) * BLOCK,
                head % 2 * DH : (head % 2 + 1) * DH,
            ]
            for head in range(GQ)
        ],
        axis=0,
    )


def side_by_side(rows):
    return jnp.concatenate([rows[pair : pair + 1] for pair in range(GQ // 2)], axis=1)


def sweep(back, doc_start, pieces, kv, dq, dkv):
    head = lax.axis_index("head")
    place = lax.rem(head, ROW)
    own_row = head // ROW
    first_key = lax.axis_index("seq") * (ROW * ROW) + (own_row - back) * ROW
    for slot, piece in pieces.items():
        query_place = lax.rem(place + ROW - slot, ROW)
        start = doc_start[own_row * ROW + query_place]

        def turn(key_slot, carry, slot=slot, piece=piece, start=start, query_place=query_place):
            key_place = key_slot + (1 if back == 2 else 0)
            seen = first_key + key_place >= start
            if back == 0:
                seen = seen & (key_place <= query_place)

            @pl.when(seen)
            def _():
                key = kv[key_slot, :, :DH]
                value = kv[key_slot, :, DH:]
                query = stacked(piece, 0)
                grad = stacked(piece, HALF)
                stats = piece[STAT:, :].astype(F32)
                norm = side_by_side(stats[0:4])
                dots = side_by_side(stats[4:8] + stats[8:12] + stats[12:16])
                weights = jnp.exp(nt(key, query) * SCALE - norm)
                if back == 0:
                    key_pos = lax.broadcasted_iota(jnp.int32, (BLOCK, WIDE), 0)
                    query_pos = lax.broadcasted_iota(jnp.int32, (BLOCK, WIDE), 1) % BLOCK
                    ahead = (query_place - key_place) * BLOCK
                    weights = jnp.where(key_pos <= query_pos + ahead, weights, 0.0)
                grad_scores = (weights * (nt(value, grad) - dots)).astype(BF16)
                dkv[key_slot, :, DH:] += nn(weights.astype(BF16), grad)
                dkv[key_slot, :, :DH] += nn(grad_scores, query)
                dq[slot] += nn(key.T, grad_scores)

            return carry

        lax.fori_loop(0, ROW - 1 if back == 2 else ROW, turn, 0)


def begin_own(doc_start, piece0, piece1, piece3, kv, dkv, dq):
    dkv[...] = jnp.zeros_like(dkv)
    for slot in (0, 1, 3):
        dq[slot] = jnp.zeros((DH, WIDE), F32)
    sweep(0, doc_start, {0: piece0, 1: piece1, 3: piece3}, kv, dq, dkv)


def begin_one(doc_start, piece0, piece1, piece3, kv, dq_in, dkv, dq):
    dkv[...] = jnp.zeros_like(dkv)
    for slot in (0, 1, 3):
        dq[slot] = dq_in[slot]
    sweep(1, doc_start, {0: piece0, 1: piece1, 3: piece3}, kv, dq, dkv)


def round_kv(dkv, out):
    out[:, :, :DH] = (dkv[:, :, :DH] * SCALE).astype(BF16)
    out[:, :, DH:] = dkv[:, :, DH:].astype(BF16)


def finish_one(doc_start, piece2, kv, one_in, out, late, one):
    late[...] = jnp.zeros_like(late)
    one[...] = one_in[...]
    sweep(1, doc_start, {2: piece2}, kv, Shifted(late), one)
    round_kv(one, out)


def all_two(
    doc_start, piece0, piece1, piece2, piece3, kv, dq_in, late_in, out, dq, late, two
):
    two[...] = jnp.zeros_like(two)
    late[...] = late_in[...]
    for slot in (0, 1, 3):
        dq[slot] = dq_in[slot]
    sweep(2, doc_start, {0: piece0, 1: piece1, 3: piece3}, kv, dq, two)
    sweep(2, doc_start, {2: piece2}, kv, Shifted(late), two)
    round_kv(two, out)


def finish_own(
    doc_start, piece2, kv, dkv_in, dq_in, late_in, dkv, out0, out1, out2, out3, late
):
    dkv[...] = dkv_in[...]
    late[...] = late_in[...]
    sweep(0, doc_start, {2: piece2}, kv, Shifted(late), dkv)
    dkv[:, :, :DH] = dkv[:, :, :DH] * SCALE
    for slot, out in enumerate((out0, out1, out2, out3)):
        for head in range(GQ):
            cut = slice(head * DH, (head + 1) * DH)
            total = late[0, :, cut] if slot == 2 else dq_in[slot, :, cut]
            out[:, cut] = (total.T * SCALE).astype(BF16)


class Shifted:
    def __init__(self, ref):
        self.ref = ref

    def __getitem__(self, slot):
        return self.ref[slot - 2]

    def __setitem__(self, slot, value):
        self.ref[slot - 2] = value


def add_up(own, one, two, *pieces):
    place = lax.rem(lax.axis_index("head"), ROW)
    for slot in range(ROW):
        block = lax.rem(place + ROW - slot, ROW)
        earlier = jnp.where(block > 0, two[jnp.maximum(block - 1, 0)].astype(F32), 0.0)
        pieces[slot][...] = (own[block] + one[block].astype(F32) + earlier).astype(BF16)


def join_queries(piece0, piece1, piece2, piece3, out, sems):
    place = lax.rem(lax.axis_index("head"), ROW)
    copies = []
    for shift, piece in enumerate((piece0, piece1, piece2, piece3)):
        span = pl.ds(pl.multiple_of(lax.rem(place + shift, ROW) * WIDE, WIDE), WIDE)
        copies.append(pltpu.make_async_copy(piece, out.at[:, span], sems.at[shift]))
    for copy in copies:
        copy.start()
    for copy in copies:
        copy.wait()


def join_kv(piece0, piece1, piece2, piece3, key_out, value_out, sems):
    place = lax.rem(lax.axis_index("head"), ROW)
    copies = []
    for shift, piece in enumerate((piece0, piece1, piece2, piece3)):
        columns = pl.ds(pl.multiple_of(lax.rem(place + shift, ROW) * DH, DH), DH)
        for part, out in enumerate((key_out, value_out)):
            copies.append(
                pltpu.make_async_copy(
                    piece.at[:, pl.ds(part * DH, DH)], out.at[:, columns], sems.at[shift, part]
                )
            )
    for copy in copies:
        copy.start()
    for copy in copies:
        copy.wait()


def kernel(body, name, in_specs, shapes, scratch=(), out_spec=VMEM, grant=24, cost=0):
    return pl.pallas_call(
        body,
        in_specs=in_specs,
        out_specs=[out_spec] * len(shapes),
        out_shape=[jax.ShapeDtypeStruct(*shape) for shape in shapes],
        scratch_shapes=scratch,
        compiler_params=pltpu.CompilerParams(vmem_limit_bytes=grant << 20),
        cost_estimate=pl.CostEstimate(flops=cost, bytes_accessed=cost, transcendentals=0),
        name=name,
    )


def per_device(queries, outputs, out_grads, log_norms, keys, values, doc_start):
    seqs = lax.axis_size("seq")
    heads = lax.axis_size("head")
    total = seqs * heads
    sems = pltpu.SemaphoreType.DMA

    def along_row(value, shift):
        if shift % ROW == 0:
            return value
        pairs = [(b, b - b % ROW + (b + shift) % ROW) for b in range(total)]
        return lax.ppermute(value, AXES, pairs)

    def along_rows(value, rows):
        by = rows * ROW
        return lax.ppermute(value, AXES, [(b, (b + by) % total) for b in range(total)])

    kv_shape = (ROW, BLOCK, 2 * DH)
    late_shape = (ROW - 1, BLOCK, 2 * DH)
    dq_shape = ((ROW, DH, WIDE), F32)
    piece_shape = ((PIECE, PAIR), BF16)
    turned = log_norms.T

    def pack_scratch(count):
        return [
            pltpu.VMEM((count, 3, BLOCK, WIDE), BF16),
            pltpu.VMEM((H, BLOCK), BF16),
            sems((count, 4)),
        ]

    kv_piece = ((BLOCK, 2 * DH), BF16)
    kv_sent = kernel(
        pack_kv, "pack_kv", [HBM] * 2, [kv_piece] * ROW, [sems((ROW, 2))], grant=56
    )(keys, values)
    kv_pieces = [along_row(kv_sent[shift], shift) for shift in range(ROW)]
    kv_sent, grads = lax.optimization_barrier((kv_sent, out_grads))
    near = kernel(
        functools.partial(pack, (1, 3)),
        "pack_near",
        [HBM] * 4,
        [piece_shape] * 2,
        pack_scratch(2),
        grant=52,
    )(queries, outputs, grads, turned)
    kv_pieces, near = lax.optimization_barrier((kv_pieces, near))
    piece1 = along_row(near[0], 1)
    piece3 = along_row(near[1], 3)
    kv_own, kv_late = kernel(
        in_order, "in_order", [VMEM] * ROW, [(kv_shape, BF16), (late_shape, BF16)]
    )(*kv_pieces)
    kv_one = along_rows(kv_own, 1)
    kv_two = along_rows(kv_late, 2)
    kv_own, grads_later = lax.optimization_barrier((kv_own, out_grads))
    piece0, far = kernel(
        functools.partial(pack, (0, 2)),
        "pack_rest",
        [HBM] * 4,
        [piece_shape] * 2,
        pack_scratch(2),
        grant=52,
    )(queries, outputs, grads_later, turned)
    piece1, piece3, far = lax.optimization_barrier((piece1, piece3, far))
    piece2 = along_row(far, 2)

    dkv_own, dq = kernel(
        begin_own, "begin_own", [SMEM] + [VMEM] * 4, [(kv_shape, F32), dq_shape], cost=HEAVY
    )(doc_start, piece0, piece1, piece3, kv_own)
    dkv_one, dq = kernel(
        begin_one, "begin_one", [SMEM] + [VMEM] * 5, [(kv_shape, F32), dq_shape], cost=HEAVY
    )(doc_start, piece0, piece1, piece3, kv_one, dq)
    far_shape = ((1, DH, WIDE), F32)
    dkv_one, dq_far = kernel(
        finish_one,
        "finish_one",
        [SMEM] + [VMEM] * 3,
        [(kv_shape, BF16), far_shape],
        [pltpu.VMEM(kv_shape, F32)],
        cost=HEAVY,
    )(doc_start, piece2, kv_one, dkv_one)
    dkv_two, dq, dq_far = kernel(
        all_two,
        "all_two",
        [SMEM] + [VMEM] * 7,
        [(late_shape, BF16), dq_shape, far_shape],
        [pltpu.VMEM(late_shape, F32)],
        cost=HEAVY,
    )(doc_start, piece0, piece1, piece2, piece3, kv_two, dq, dq_far)
    back_two = along_rows(dkv_two, -2)
    back_one = along_rows(dkv_one, -1)
    dkv_own, *dq_sent = kernel(
        finish_own,
        "finish_own",
        [SMEM] + [VMEM] * 5,
        [(kv_shape, F32)] + [((BLOCK, WIDE), BF16)] * ROW,
        [pltpu.VMEM(*far_shape)],
        cost=0,
    )(doc_start, piece2, kv_own, dkv_own, dq, dq_far)
    dq_pieces = [along_row(dq_sent[slot], -slot) for slot in range(ROW)]
    (query_out,) = kernel(
        join_queries,
        "join_queries",
        [VMEM] * ROW,
        [((BLOCK, H * DH), BF16)],
        [sems((ROW,))],
        HBM,
    )(*dq_pieces)
    dkv_sent = kernel(
        add_up, "add_up", [VMEM] * 3, [((BLOCK, 2 * DH), BF16)] * ROW, cost=HEAVY
    )(
        dkv_own, back_one, back_two
    )
    dkv_pieces = [along_row(dkv_sent[slot], -slot) for slot in range(ROW)]
    key_out, value_out = kernel(
        join_kv,
        "join_kv",
        [VMEM] * ROW,
        [((BLOCK, KVH * DH), BF16)] * 2,
        [sems((ROW, 2))],
        HBM,
    )(*dkv_pieces)
    return (query_out, key_out, value_out)


def solution(mesh):
    placed = P(("seq", "head"), None)
    return jax.shard_map(
        per_device,
        mesh=mesh,
        in_specs=(placed,) * 6 + (P("seq"),),
        out_specs=(placed,) * 3,
        check_vma=False,
    )
```

```python
import functools

import jax
import jax.numpy as jnp
from jax import lax
from jax.experimental import pallas as pl
from jax.experimental.pallas import tpu as pltpu
from jax.sharding import PartitionSpec as P

H = 32
KVH = 4
DH = 128
BLOCK = 128
GQ = 8
ROW = 4
WIDE = GQ * DH
SCALE = DH ** (-0.5)
AXES = ("seq", "head")
PAIR = 2 * DH
HALF = GQ // 2 * BLOCK
STAT = 2 * HALF
PIECE = STAT + 16
HEAVY = 20_000_000_000
F32 = jnp.float32
BF16 = jnp.bfloat16

VMEM = pl.BlockSpec(memory_space=pltpu.VMEM)
HBM = pl.BlockSpec(memory_space=pltpu.HBM)
SMEM = pl.BlockSpec(memory_space=pltpu.SMEM)


def nt(left, right):
    return lax.dot_general(left, right, (((1,), (1,)), ((), ())), preferred_element_type=F32)


def nn(left, right):
    return jnp.dot(left, right, preferred_element_type=F32)


def pack_kv(keys, values, piece0, piece1, piece2, piece3, sems):
    place = lax.rem(lax.axis_index("head"), ROW)
    copies = []
    for shift, piece in enumerate((piece0, piece1, piece2, piece3)):
        columns = pl.ds(pl.multiple_of(lax.rem(place + shift, ROW) * DH, DH), DH)
        for part, source in enumerate((keys, values)):
            copies.append(
                pltpu.make_async_copy(
                    source.at[:, columns],
                    piece.at[:, pl.ds(part * DH, DH)],
                    sems.at[shift, part],
                )
            )
    for copy in copies:
        copy.start()
    for copy in copies:
        copy.wait()


def pack(shifts, queries, outputs, grads, norms, *rest):
    place = lax.rem(lax.axis_index("head"), ROW)
    count = len(shifts)
    pieces = rest[:count]
    held, held_norms, sems = rest[count:]
    loads = []
    for slot, shift in enumerate(shifts):
        group = lax.rem(place + shift, ROW)
        span = pl.ds(pl.multiple_of(group * WIDE, WIDE), WIDE)
        loads.append(
            [
                pltpu.make_async_copy(
                    source.at[:, span], held.at[slot, part], sems.at[slot, part]
                )
                for part, source in enumerate((grads, outputs, queries))
            ]
        )
    norm_copy = pltpu.make_async_copy(norms, held_norms, sems.at[0, 3])
    norm_copy.start()
    for load in loads:
        for copy in load:
            copy.start()
    norm_copy.wait()
    turned = held_norms[...].astype(F32)
    ones = jnp.ones((16, DH), BF16)
    row_id = lax.broadcasted_iota(jnp.int32, (16, BLOCK), 0)
    kind = row_id // 4
    head_id = lax.broadcasted_iota(jnp.int32, (H, BLOCK), 0)
    for slot, (shift, piece) in enumerate(zip(shifts, pieces)):
        group = lax.rem(place + shift, ROW)
        loads[slot][0].wait()
        loads[slot][1].wait()
        stats = [jnp.zeros((16, BLOCK), F32)] * 2
        for head in range(GQ):
            cut = slice(head * DH, (head + 1) * DH)
            grad = held[slot, 0, :, cut]
            product = grad.astype(F32) * held[slot, 1, :, cut].astype(F32)
            high = product.astype(BF16)
            low = (product - high.astype(F32)).astype(BF16)
            dots = nt(ones, high) + nt(ones, low)
            first = dots.astype(BF16).astype(F32)
            second = (dots - first).astype(BF16).astype(F32)
            third = dots - first - second
            norm = jnp.sum(
                jnp.where(head_id == group * GQ + head, turned, 0.0), axis=0, keepdims=True
            )
            both = jnp.where(
                kind == 0,
                norm,
                jnp.where(kind == 1, first, jnp.where(kind == 2, second, third)),
            )
            stats[head % 2] = jnp.where(row_id % 4 == head // 2, both, stats[head % 2])
            rows = slice(HALF + head // 2 * BLOCK, HALF + (head // 2 + 1) * BLOCK)
            piece[rows, head % 2 * DH : (head % 2 + 1) * DH] = grad
        piece[STAT:, :DH] = stats[0].astype(BF16)
        piece[STAT:, DH:] = stats[1].astype(BF16)
    for slot, piece in enumerate(pieces):
        loads[slot][2].wait()
        for pair in range(GQ // 2):
            piece[pair * BLOCK : (pair + 1) * BLOCK, :] = held[
                slot, 2, :, pair * PAIR : (pair + 1) * PAIR
            ]


def in_order(piece0, piece1, piece2, piece3, all_out, late_out):
    place = lax.rem(lax.axis_index("head"), ROW)
    for block in range(ROW):
        shift = lax.rem(place + ROW - block, ROW)
        value = piece0[...]
        for number, piece in enumerate((piece1, piece2, piece3)):
            value = jnp.where(shift == number + 1, piece[...], value)
        all_out[block] = value
        if block > 0:
            late_out[block - 1] = value


def stacked(piece, start):
    return jnp.concatenate(
        [
            piece[
                start + head // 2 * BLOCK : start + (head // 2 + 1) * BLOCK,
                head % 2 * DH : (head % 2 + 1) * DH,
            ]
            for head in range(GQ)
        ],
        axis=0,
    )


def side_by_side(rows):
    return jnp.concatenate([rows[pair : pair + 1] for pair in range(GQ // 2)], axis=1)


def sweep(back, doc_start, pieces, kv, dq, dkv):
    head = lax.axis_index("head")
    place = lax.rem(head, ROW)
    own_row = head // ROW
    first_key = lax.axis_index("seq") * (ROW * ROW) + (own_row - back) * ROW
    for slot, piece in pieces.items():
        query_place = lax.rem(place + ROW - slot, ROW)
        start = doc_start[own_row * ROW + query_place]

        def work(key_slot, count, slot=slot, piece=piece, query_place=query_place):
            keys = count * BLOCK
            span = pl.ds(key_slot, count)
            key = kv[span, :, :DH].reshape(keys, DH)
            value = kv[span, :, DH:].reshape(keys, DH)
            query = stacked(piece, 0)
            grad = stacked(piece, HALF)
            stats = piece[STAT:, :].astype(F32)
            norm = side_by_side(stats[0:4])
            dots = side_by_side(stats[4:8] + stats[8:12] + stats[12:16])
            weights = jnp.exp(nt(key, query) * SCALE - norm)
            if back == 0:
                key_pos = lax.broadcasted_iota(jnp.int32, (BLOCK, WIDE), 0)
                query_pos = lax.broadcasted_iota(jnp.int32, (BLOCK, WIDE), 1) % BLOCK
                ahead = (query_place - key_slot) * BLOCK
                weights = jnp.where(key_pos <= query_pos + ahead, weights, 0.0)
            grad_scores = (weights * (nt(value, grad) - dots)).astype(BF16)
            dkv[span, :, DH:] += nn(weights.astype(BF16), grad).reshape(count, BLOCK, DH)
            dkv[span, :, :DH] += nn(grad_scores, query).reshape(count, BLOCK, DH)
            dq[slot] += nn(key.T, grad_scores)

        def turn(key_slot, carry, start=start, query_place=query_place, work=work):
            key_place = key_slot + (1 if back == 2 else 0)
            seen = first_key + key_place >= start
            if back == 0:
                seen = seen & (key_place <= query_place)

            @pl.when(seen)
            def _():
                work(key_slot, 1)

            return carry

        if back == 1:
            whole = first_key >= start

            @pl.when(whole)
            def _(work=work):
                work(0, ROW)

            @pl.when(jnp.logical_not(whole))
            def _(turn=turn):
                lax.fori_loop(1, ROW, turn, 0)
        else:
            lax.fori_loop(0, ROW - 1 if back == 2 else ROW, turn, 0)


def begin_own(doc_start, piece0, piece1, piece3, kv, dkv, dq):
    dkv[...] = jnp.zeros_like(dkv)
    for slot in (0, 1, 3):
        dq[slot] = jnp.zeros((DH, WIDE), F32)
    sweep(0, doc_start, {0: piece0, 1: piece1, 3: piece3}, kv, dq, dkv)


def begin_one(doc_start, piece0, piece1, piece3, kv, dq_in, dkv, dq):
    dkv[...] = jnp.zeros_like(dkv)
    for slot in (0, 1, 3):
        dq[slot] = dq_in[slot]
    sweep(1, doc_start, {0: piece0, 1: piece1, 3: piece3}, kv, dq, dkv)


def round_kv(dkv, out):
    out[:, :, :DH] = (dkv[:, :, :DH] * SCALE).astype(BF16)
    out[:, :, DH:] = dkv[:, :, DH:].astype(BF16)


def finish_one(doc_start, piece2, kv, one_in, out, late, one):
    late[...] = jnp.zeros_like(late)
    one[...] = one_in[...]
    sweep(1, doc_start, {2: piece2}, kv, Shifted(late), one)
    round_kv(one, out)


def all_two(
    doc_start, piece0, piece1, piece2, piece3, kv, dq_in, late_in, out, dq, late, two
):
    two[...] = jnp.zeros_like(two)
    late[...] = late_in[...]
    for slot in (0, 1, 3):
        dq[slot] = dq_in[slot]
    sweep(2, doc_start, {0: piece0, 1: piece1, 3: piece3}, kv, dq, two)
    sweep(2, doc_start, {2: piece2}, kv, Shifted(late), two)
    round_kv(two, out)


def finish_own(
    doc_start, piece2, kv, dkv_in, dq_in, late_in, dkv, out0, out1, out2, out3, late
):
    dkv[...] = dkv_in[...]
    late[...] = late_in[...]
    sweep(0, doc_start, {2: piece2}, kv, Shifted(late), dkv)
    dkv[:, :, :DH] = dkv[:, :, :DH] * SCALE
    for slot, out in enumerate((out0, out1, out2, out3)):
        for head in range(GQ):
            cut = slice(head * DH, (head + 1) * DH)
            total = late[0, :, cut] if slot == 2 else dq_in[slot, :, cut]
            out[:, cut] = (total.T * SCALE).astype(BF16)


class Shifted:
    def __init__(self, ref):
        self.ref = ref

    def __getitem__(self, slot):
        return self.ref[slot - 2]

    def __setitem__(self, slot, value):
        self.ref[slot - 2] = value


def add_up(own, one, two, *pieces):
    place = lax.rem(lax.axis_index("head"), ROW)
    for slot in range(ROW):
        block = lax.rem(place + ROW - slot, ROW)
        earlier = jnp.where(block > 0, two[jnp.maximum(block - 1, 0)].astype(F32), 0.0)
        pieces[slot][...] = (own[block] + one[block].astype(F32) + earlier).astype(BF16)


def join_queries(piece0, piece1, piece2, piece3, out, sems):
    place = lax.rem(lax.axis_index("head"), ROW)
    copies = []
    for shift, piece in enumerate((piece0, piece1, piece2, piece3)):
        span = pl.ds(pl.multiple_of(lax.rem(place + shift, ROW) * WIDE, WIDE), WIDE)
        copies.append(pltpu.make_async_copy(piece, out.at[:, span], sems.at[shift]))
    for copy in copies:
        copy.start()
    for copy in copies:
        copy.wait()


def join_kv(piece0, piece1, piece2, piece3, key_out, value_out, sems):
    place = lax.rem(lax.axis_index("head"), ROW)
    copies = []
    for shift, piece in enumerate((piece0, piece1, piece2, piece3)):
        columns = pl.ds(pl.multiple_of(lax.rem(place + shift, ROW) * DH, DH), DH)
        for part, out in enumerate((key_out, value_out)):
            copies.append(
                pltpu.make_async_copy(
                    piece.at[:, pl.ds(part * DH, DH)], out.at[:, columns], sems.at[shift, part]
                )
            )
    for copy in copies:
        copy.start()
    for copy in copies:
        copy.wait()


def kernel(body, name, in_specs, shapes, scratch=(), out_spec=VMEM, grant=24, cost=0):
    return pl.pallas_call(
        body,
        in_specs=in_specs,
        out_specs=[out_spec] * len(shapes),
        out_shape=[jax.ShapeDtypeStruct(*shape) for shape in shapes],
        scratch_shapes=scratch,
        compiler_params=pltpu.CompilerParams(vmem_limit_bytes=grant << 20),
        cost_estimate=pl.CostEstimate(flops=cost, bytes_accessed=cost, transcendentals=0),
        name=name,
    )


def per_device(queries, outputs, out_grads, log_norms, keys, values, doc_start):
    seqs = lax.axis_size("seq")
    heads = lax.axis_size("head")
    total = seqs * heads
    sems = pltpu.SemaphoreType.DMA

    def along_row(value, shift):
        if shift % ROW == 0:
            return value
        pairs = [(b, b - b % ROW + (b + shift) % ROW) for b in range(total)]
        return lax.ppermute(value, AXES, pairs)

    def along_rows(value, rows):
        by = rows * ROW
        return lax.ppermute(value, AXES, [(b, (b + by) % total) for b in range(total)])

    kv_shape = (ROW, BLOCK, 2 * DH)
    late_shape = (ROW - 1, BLOCK, 2 * DH)
    dq_shape = ((ROW, DH, WIDE), F32)
    piece_shape = ((PIECE, PAIR), BF16)
    turned = log_norms.T

    def pack_scratch(count):
        return [
            pltpu.VMEM((count, 3, BLOCK, WIDE), BF16),
            pltpu.VMEM((H, BLOCK), BF16),
            sems((count, 4)),
        ]

    kv_piece = ((BLOCK, 2 * DH), BF16)
    kv_sent = kernel(
        pack_kv, "pack_kv", [HBM] * 2, [kv_piece] * ROW, [sems((ROW, 2))], grant=56
    )(keys, values)
    kv_pieces = [along_row(kv_sent[shift], shift) for shift in range(ROW)]
    kv_sent, grads = lax.optimization_barrier((kv_sent, out_grads))
    near = kernel(
        functools.partial(pack, (1, 3)),
        "pack_near",
        [HBM] * 4,
        [piece_shape] * 2,
        pack_scratch(2),
        grant=52,
    )(queries, outputs, grads, turned)
    kv_pieces, near = lax.optimization_barrier((kv_pieces, near))
    piece1 = along_row(near[0], 1)
    piece3 = along_row(near[1], 3)
    kv_own, kv_late = kernel(
        in_order, "in_order", [VMEM] * ROW, [(kv_shape, BF16), (late_shape, BF16)]
    )(*kv_pieces)
    kv_one = along_rows(kv_own, 1)
    kv_two = along_rows(kv_late, 2)
    kv_own, grads_later = lax.optimization_barrier((kv_own, out_grads))
    piece0, far = kernel(
        functools.partial(pack, (0, 2)),
        "pack_rest",
        [HBM] * 4,
        [piece_shape] * 2,
        pack_scratch(2),
        grant=52,
    )(queries, outputs, grads_later, turned)
    piece1, piece3, far = lax.optimization_barrier((piece1, piece3, far))
    piece2 = along_row(far, 2)

    dkv_own, dq = kernel(
        begin_own, "begin_own", [SMEM] + [VMEM] * 4, [(kv_shape, F32), dq_shape], cost=HEAVY
    )(doc_start, piece0, piece1, piece3, kv_own)
    dkv_one, dq = kernel(
        begin_one, "begin_one", [SMEM] + [VMEM] * 5, [(kv_shape, F32), dq_shape], cost=HEAVY
    )(doc_start, piece0, piece1, piece3, kv_one, dq)
    far_shape = ((1, DH, WIDE), F32)
    dkv_one, dq_far = kernel(
        finish_one,
        "finish_one",
        [SMEM] + [VMEM] * 3,
        [(kv_shape, BF16), far_shape],
        [pltpu.VMEM(kv_shape, F32)],
        cost=HEAVY,
    )(doc_start, piece2, kv_one, dkv_one)
    dkv_two, dq, dq_far = kernel(
        all_two,
        "all_two",
        [SMEM] + [VMEM] * 7,
        [(late_shape, BF16), dq_shape, far_shape],
        [pltpu.VMEM(late_shape, F32)],
        cost=HEAVY,
    )(doc_start, piece0, piece1, piece2, piece3, kv_two, dq, dq_far)
    back_two = along_rows(dkv_two, -2)
    back_one = along_rows(dkv_one, -1)
    dkv_own, *dq_sent = kernel(
        finish_own,
        "finish_own",
        [SMEM] + [VMEM] * 5,
        [(kv_shape, F32)] + [((BLOCK, WIDE), BF16)] * ROW,
        [pltpu.VMEM(*far_shape)],
        cost=0,
    )(doc_start, piece2, kv_own, dkv_own, dq, dq_far)
    dq_pieces = [along_row(dq_sent[slot], -slot) for slot in range(ROW)]
    (query_out,) = kernel(
        join_queries,
        "join_queries",
        [VMEM] * ROW,
        [((BLOCK, H * DH), BF16)],
        [sems((ROW,))],
        HBM,
    )(*dq_pieces)
    dkv_sent = kernel(
        add_up, "add_up", [VMEM] * 3, [((BLOCK, 2 * DH), BF16)] * ROW, cost=HEAVY
    )(
        dkv_own, back_one, back_two
    )
    dkv_pieces = [along_row(dkv_sent[slot], -slot) for slot in range(ROW)]
    key_out, value_out = kernel(
        join_kv,
        "join_kv",
        [VMEM] * ROW,
        [((BLOCK, KVH * DH), BF16)] * 2,
        [sems((ROW, 2))],
        HBM,
    )(*dkv_pieces)
    return (query_out, key_out, value_out)


def solution(mesh):
    placed = P(("seq", "head"), None)
    return jax.shard_map(
        per_device,
        mesh=mesh,
        in_specs=(placed,) * 6 + (P("seq"),),
        out_specs=(placed,) * 3,
        check_vma=False,
    )
```

```python
import functools

import jax
import jax.numpy as jnp
from jax import lax
from jax.experimental import pallas as pl
from jax.experimental.pallas import tpu as pltpu
from jax.sharding import PartitionSpec as P

H = 32
KVH = 4
DH = 128
BLOCK = 128
GQ = 8
ROW = 4
WIDE = GQ * DH
SCALE = DH ** (-0.5)
AXES = ("seq", "head")
PAIR = 2 * DH
HALF = GQ // 2 * BLOCK
STAT = 2 * HALF
PIECE = STAT + 16
HEAVY = 20_000_000_000
F32 = jnp.float32
BF16 = jnp.bfloat16

VMEM = pl.BlockSpec(memory_space=pltpu.VMEM)
HBM = pl.BlockSpec(memory_space=pltpu.HBM)
SMEM = pl.BlockSpec(memory_space=pltpu.SMEM)


def nt(left, right):
    return lax.dot_general(left, right, (((1,), (1,)), ((), ())), preferred_element_type=F32)


def nn(left, right):
    return jnp.dot(left, right, preferred_element_type=F32)


def pack_kv(keys, values, piece0, piece1, piece2, piece3, sems):
    place = lax.rem(lax.axis_index("head"), ROW)
    copies = []
    for shift, piece in enumerate((piece0, piece1, piece2, piece3)):
        columns = pl.ds(pl.multiple_of(lax.rem(place + shift, ROW) * DH, DH), DH)
        for part, source in enumerate((keys, values)):
            copies.append(
                pltpu.make_async_copy(
                    source.at[:, columns],
                    piece.at[:, pl.ds(part * DH, DH)],
                    sems.at[shift, part],
                )
            )
    for copy in copies:
        copy.start()
    for copy in copies:
        copy.wait()


def pack(shifts, queries, outputs, grads, norms, *rest):
    place = lax.rem(lax.axis_index("head"), ROW)
    count = len(shifts)
    pieces = rest[:count]
    held, held_norms, sems = rest[count:]
    loads = []
    for slot, shift in enumerate(shifts):
        group = lax.rem(place + shift, ROW)
        span = pl.ds(pl.multiple_of(group * WIDE, WIDE), WIDE)
        loads.append(
            [
                pltpu.make_async_copy(
                    source.at[:, span], held.at[slot, part], sems.at[slot, part]
                )
                for part, source in enumerate((grads, outputs, queries))
            ]
        )
    norm_copy = pltpu.make_async_copy(norms, held_norms, sems.at[0, 3])
    norm_copy.start()
    for load in loads:
        for copy in load:
            copy.start()
    norm_copy.wait()
    turned = held_norms[...].astype(F32)
    ones = jnp.ones((16, DH), BF16)
    row_id = lax.broadcasted_iota(jnp.int32, (16, BLOCK), 0)
    kind = row_id // 4
    head_id = lax.broadcasted_iota(jnp.int32, (H, BLOCK), 0)
    for slot, (shift, piece) in enumerate(zip(shifts, pieces)):
        group = lax.rem(place + shift, ROW)
        loads[slot][0].wait()
        loads[slot][1].wait()
        stats = [jnp.zeros((16, BLOCK), F32)] * 2
        for head in range(GQ):
            cut = slice(head * DH, (head + 1) * DH)
            grad = held[slot, 0, :, cut]
            product = grad.astype(F32) * held[slot, 1, :, cut].astype(F32)
            high = product.astype(BF16)
            low = (product - high.astype(F32)).astype(BF16)
            dots = nt(ones, high) + nt(ones, low)
            first = dots.astype(BF16).astype(F32)
            second = (dots - first).astype(BF16).astype(F32)
            third = dots - first - second
            norm = jnp.sum(
                jnp.where(head_id == group * GQ + head, turned, 0.0), axis=0, keepdims=True
            )
            both = jnp.where(
                kind == 0,
                norm,
                jnp.where(kind == 1, first, jnp.where(kind == 2, second, third)),
            )
            stats[head % 2] = jnp.where(row_id % 4 == head // 2, both, stats[head % 2])
            rows = slice(HALF + head // 2 * BLOCK, HALF + (head // 2 + 1) * BLOCK)
            piece[rows, head % 2 * DH : (head % 2 + 1) * DH] = grad
        piece[STAT:, :DH] = stats[0].astype(BF16)
        piece[STAT:, DH:] = stats[1].astype(BF16)
    for slot, piece in enumerate(pieces):
        loads[slot][2].wait()
        for pair in range(GQ // 2):
            piece[pair * BLOCK : (pair + 1) * BLOCK, :] = held[
                slot, 2, :, pair * PAIR : (pair + 1) * PAIR
            ]


def in_order(piece0, piece1, piece2, piece3, all_out, late_out):
    place = lax.rem(lax.axis_index("head"), ROW)
    for block in range(ROW):
        shift = lax.rem(place + ROW - block, ROW)
        value = piece0[...]
        for number, piece in enumerate((piece1, piece2, piece3)):
            value = jnp.where(shift == number + 1, piece[...], value)
        all_out[block] = value
        if block > 0:
            late_out[block - 1] = value


def stacked(piece, start):
    return jnp.concatenate(
        [
            piece[
                start + head // 2 * BLOCK : start + (head // 2 + 1) * BLOCK,
                head % 2 * DH : (head % 2 + 1) * DH,
            ]
            for head in range(GQ)
        ],
        axis=0,
    )


def side_by_side(rows):
    return jnp.concatenate([rows[pair : pair + 1] for pair in range(GQ // 2)], axis=1)


def sweep(back, doc_start, pieces, kv, dq, dkv):
    head = lax.axis_index("head")
    place = lax.rem(head, ROW)
    own_row = head // ROW
    first_key = lax.axis_index("seq") * (ROW * ROW) + (own_row - back) * ROW
    for slot, piece in pieces.items():
        query_place = lax.rem(place + ROW - slot, ROW)
        start = doc_start[own_row * ROW + query_place]

        def work(key_slot, count, slot=slot, piece=piece, query_place=query_place):
            keys = count * BLOCK
            span = pl.ds(key_slot, count)
            key = kv[span, :, :DH].reshape(keys, DH)
            value = kv[span, :, DH:].reshape(keys, DH)
            query = stacked(piece, 0)
            grad = stacked(piece, HALF)
            stats = piece[STAT:, :].astype(F32)
            norm = side_by_side(stats[0:4])
            dots = side_by_side(stats[4:8] + stats[8:12] + stats[12:16])
            weights = jnp.exp(nt(key, query) * SCALE - norm)
            if back == 0:
                key_pos = lax.broadcasted_iota(jnp.int32, (BLOCK, WIDE), 0)
                query_pos = lax.broadcasted_iota(jnp.int32, (BLOCK, WIDE), 1) % BLOCK
                ahead = (query_place - key_slot) * BLOCK
                weights = jnp.where(key_pos <= query_pos + ahead, weights, 0.0)
            grad_scores = (weights * (nt(value, grad) - dots)).astype(BF16)
            dkv[span, :, DH:] += nn(weights.astype(BF16), grad).reshape(count, BLOCK, DH)
            dkv[span, :, :DH] += nn(grad_scores, query).reshape(count, BLOCK, DH)
            dq[slot] += nn(key.T, grad_scores)

        def turn(key_slot, carry, start=start, query_place=query_place, work=work):
            key_place = key_slot + (1 if back == 2 else 0)
            seen = first_key + key_place >= start
            if back == 0:
                seen = seen & (key_place <= query_place)

            @pl.when(seen)
            def _():
                work(key_slot, 1)

            return carry

        if back > 0:
            count = ROW - 1 if back == 2 else ROW
            whole = first_key + ROW - count >= start

            @pl.when(whole)
            def _(work=work, count=count):
                work(0, count)

            @pl.when(jnp.logical_not(whole))
            def _(turn=turn, count=count):
                lax.fori_loop(1, count, turn, 0)
        else:
            lax.fori_loop(0, ROW, turn, 0)


def begin_own(doc_start, piece0, piece1, piece3, kv, dkv, dq):
    dkv[...] = jnp.zeros_like(dkv)
    for slot in (0, 1, 3):
        dq[slot] = jnp.zeros((DH, WIDE), F32)
    sweep(0, doc_start, {0: piece0, 1: piece1, 3: piece3}, kv, dq, dkv)


def begin_one(doc_start, piece0, piece1, piece3, kv, dq_in, dkv, dq):
    dkv[...] = jnp.zeros_like(dkv)
    for slot in (0, 1, 3):
        dq[slot] = dq_in[slot]
    sweep(1, doc_start, {0: piece0, 1: piece1, 3: piece3}, kv, dq, dkv)


def round_kv(dkv, out):
    out[:, :, :DH] = (dkv[:, :, :DH] * SCALE).astype(BF16)
    out[:, :, DH:] = dkv[:, :, DH:].astype(BF16)


def finish_one(doc_start, piece2, kv, one_in, out, late, one):
    late[...] = jnp.zeros_like(late)
    one[...] = one_in[...]
    sweep(1, doc_start, {2: piece2}, kv, Shifted(late), one)
    round_kv(one, out)


def all_two(
    doc_start, piece0, piece1, piece2, piece3, kv, dq_in, late_in, out, dq, late, two
):
    two[...] = jnp.zeros_like(two)
    late[...] = late_in[...]
    for slot in (0, 1, 3):
        dq[slot] = dq_in[slot]
    sweep(2, doc_start, {0: piece0, 1: piece1, 3: piece3}, kv, dq, two)
    sweep(2, doc_start, {2: piece2}, kv, Shifted(late), two)
    round_kv(two, out)


def finish_own(
    doc_start, piece2, kv, dkv_in, dq_in, late_in, dkv, out0, out1, out2, out3, late
):
    dkv[...] = dkv_in[...]
    late[...] = late_in[...]
    sweep(0, doc_start, {2: piece2}, kv, Shifted(late), dkv)
    dkv[:, :, :DH] = dkv[:, :, :DH] * SCALE
    for slot, out in enumerate((out0, out1, out2, out3)):
        for head in range(GQ):
            cut = slice(head * DH, (head + 1) * DH)
            total = late[0, :, cut] if slot == 2 else dq_in[slot, :, cut]
            out[:, cut] = (total.T * SCALE).astype(BF16)


class Shifted:
    def __init__(self, ref):
        self.ref = ref

    def __getitem__(self, slot):
        return self.ref[slot - 2]

    def __setitem__(self, slot, value):
        self.ref[slot - 2] = value


def add_up(own, one, two, *pieces):
    place = lax.rem(lax.axis_index("head"), ROW)
    for slot in range(ROW):
        block = lax.rem(place + ROW - slot, ROW)
        earlier = jnp.where(block > 0, two[jnp.maximum(block - 1, 0)].astype(F32), 0.0)
        pieces[slot][...] = (own[block] + one[block].astype(F32) + earlier).astype(BF16)


def join_queries(piece0, piece1, piece2, piece3, out, sems):
    place = lax.rem(lax.axis_index("head"), ROW)
    copies = []
    for shift, piece in enumerate((piece0, piece1, piece2, piece3)):
        span = pl.ds(pl.multiple_of(lax.rem(place + shift, ROW) * WIDE, WIDE), WIDE)
        copies.append(pltpu.make_async_copy(piece, out.at[:, span], sems.at[shift]))
    for copy in copies:
        copy.start()
    for copy in copies:
        copy.wait()


def join_kv(piece0, piece1, piece2, piece3, key_out, value_out, sems):
    place = lax.rem(lax.axis_index("head"), ROW)
    copies = []
    for shift, piece in enumerate((piece0, piece1, piece2, piece3)):
        columns = pl.ds(pl.multiple_of(lax.rem(place + shift, ROW) * DH, DH), DH)
        for part, out in enumerate((key_out, value_out)):
            copies.append(
                pltpu.make_async_copy(
                    piece.at[:, pl.ds(part * DH, DH)], out.at[:, columns], sems.at[shift, part]
                )
            )
    for copy in copies:
        copy.start()
    for copy in copies:
        copy.wait()


def kernel(body, name, in_specs, shapes, scratch=(), out_spec=VMEM, grant=24, cost=0):
    return pl.pallas_call(
        body,
        in_specs=in_specs,
        out_specs=[out_spec] * len(shapes),
        out_shape=[jax.ShapeDtypeStruct(*shape) for shape in shapes],
        scratch_shapes=scratch,
        compiler_params=pltpu.CompilerParams(vmem_limit_bytes=grant << 20),
        cost_estimate=pl.CostEstimate(flops=cost, bytes_accessed=cost, transcendentals=0),
        name=name,
    )


def per_device(queries, outputs, out_grads, log_norms, keys, values, doc_start):
    seqs = lax.axis_size("seq")
    heads = lax.axis_size("head")
    total = seqs * heads
    sems = pltpu.SemaphoreType.DMA

    def along_row(value, shift):
        if shift % ROW == 0:
            return value
        pairs = [(b, b - b % ROW + (b + shift) % ROW) for b in range(total)]
        return lax.ppermute(value, AXES, pairs)

    def along_rows(value, rows):
        by = rows * ROW
        return lax.ppermute(value, AXES, [(b, (b + by) % total) for b in range(total)])

    kv_shape = (ROW, BLOCK, 2 * DH)
    late_shape = (ROW - 1, BLOCK, 2 * DH)
    dq_shape = ((ROW, DH, WIDE), F32)
    piece_shape = ((PIECE, PAIR), BF16)
    turned = log_norms.T

    def pack_scratch(count):
        return [
            pltpu.VMEM((count, 3, BLOCK, WIDE), BF16),
            pltpu.VMEM((H, BLOCK), BF16),
            sems((count, 4)),
        ]

    kv_piece = ((BLOCK, 2 * DH), BF16)
    kv_sent = kernel(
        pack_kv, "pack_kv", [HBM] * 2, [kv_piece] * ROW, [sems((ROW, 2))], grant=56
    )(keys, values)
    kv_pieces = [along_row(kv_sent[shift], shift) for shift in range(ROW)]
    kv_sent, grads = lax.optimization_barrier((kv_sent, out_grads))
    near = kernel(
        functools.partial(pack, (1, 3)),
        "pack_near",
        [HBM] * 4,
        [piece_shape] * 2,
        pack_scratch(2),
        grant=52,
    )(queries, outputs, grads, turned)
    kv_pieces, near = lax.optimization_barrier((kv_pieces, near))
    piece1 = along_row(near[0], 1)
    piece3 = along_row(near[1], 3)
    kv_own, kv_late = kernel(
        in_order, "in_order", [VMEM] * ROW, [(kv_shape, BF16), (late_shape, BF16)]
    )(*kv_pieces)
    kv_one = along_rows(kv_own, 1)
    kv_two = along_rows(kv_late, 2)
    kv_own, grads_later = lax.optimization_barrier((kv_own, out_grads))
    piece0, far = kernel(
        functools.partial(pack, (0, 2)),
        "pack_rest",
        [HBM] * 4,
        [piece_shape] * 2,
        pack_scratch(2),
        grant=52,
    )(queries, outputs, grads_later, turned)
    piece1, piece3, far = lax.optimization_barrier((piece1, piece3, far))
    piece2 = along_row(far, 2)

    dkv_own, dq = kernel(
        begin_own, "begin_own", [SMEM] + [VMEM] * 4, [(kv_shape, F32), dq_shape], cost=HEAVY
    )(doc_start, piece0, piece1, piece3, kv_own)
    dkv_one, dq = kernel(
        begin_one, "begin_one", [SMEM] + [VMEM] * 5, [(kv_shape, F32), dq_shape], cost=HEAVY
    )(doc_start, piece0, piece1, piece3, kv_one, dq)
    far_shape = ((1, DH, WIDE), F32)
    dkv_one, dq_far = kernel(
        finish_one,
        "finish_one",
        [SMEM] + [VMEM] * 3,
        [(kv_shape, BF16), far_shape],
        [pltpu.VMEM(kv_shape, F32)],
        cost=HEAVY,
    )(doc_start, piece2, kv_one, dkv_one)
    dkv_two, dq, dq_far = kernel(
        all_two,
        "all_two",
        [SMEM] + [VMEM] * 7,
        [(late_shape, BF16), dq_shape, far_shape],
        [pltpu.VMEM(late_shape, F32)],
        cost=HEAVY,
    )(doc_start, piece0, piece1, piece2, piece3, kv_two, dq, dq_far)
    back_two = along_rows(dkv_two, -2)
    back_one = along_rows(dkv_one, -1)
    dkv_own, *dq_sent = kernel(
        finish_own,
        "finish_own",
        [SMEM] + [VMEM] * 5,
        [(kv_shape, F32)] + [((BLOCK, WIDE), BF16)] * ROW,
        [pltpu.VMEM(*far_shape)],
        cost=0,
    )(doc_start, piece2, kv_own, dkv_own, dq, dq_far)
    dq_pieces = [along_row(dq_sent[slot], -slot) for slot in range(ROW)]
    (query_out,) = kernel(
        join_queries,
        "join_queries",
        [VMEM] * ROW,
        [((BLOCK, H * DH), BF16)],
        [sems((ROW,))],
        HBM,
    )(*dq_pieces)
    dkv_sent = kernel(
        add_up, "add_up", [VMEM] * 3, [((BLOCK, 2 * DH), BF16)] * ROW, cost=HEAVY
    )(
        dkv_own, back_one, back_two
    )
    dkv_pieces = [along_row(dkv_sent[slot], -slot) for slot in range(ROW)]
    key_out, value_out = kernel(
        join_kv,
        "join_kv",
        [VMEM] * ROW,
        [((BLOCK, KVH * DH), BF16)] * 2,
        [sems((ROW, 2))],
        HBM,
    )(*dkv_pieces)
    return (query_out, key_out, value_out)


def solution(mesh):
    placed = P(("seq", "head"), None)
    return jax.shard_map(
        per_device,
        mesh=mesh,
        in_specs=(placed,) * 6 + (P("seq"),),
        out_specs=(placed,) * 3,
        check_vma=False,
    )
```
